512 devices in a mesh: dp: 64 (over z, x), tensor: 8 (over y, core).
Axes of the slice: x: 4, y: 4, z: 16, core: 2. Of those that a mesh axis runs over, the one named last changes fastest.
Arguments:
- grad_buckets: bfloat16 [8192, 57344], P(('tensor', 'dp')), may hold values from -33 to 33
- sketch: bfloat16 [8192, 512], P('tensor'), may hold values from -0.0625 to 0.0625
Outputs:
- basis_out: bfloat16 [512, 57344], P(None, ('dp', 'tensor'))
- projected: bfloat16 [512, 8192], P('dp', 'tensor')
The draws below stay inside these ranges and needn't reach their ends.
All inputs are finite; a program needn't handle non-finite values.
Results may differ from the reference program's by a relative error of at most 0.0013.
Values may be sent and summed in bfloat16 or wider, within the bound.
A program may use at most 192 MiB of HBM per device.

```python
import math
import jax
import jax.numpy as jnp
from jax import lax

D = 8192
RANK = 512
ROWS = 57344
N_DP = 64
N_TENSOR = 8


def draw_grad_buckets(key, part):
    key = jax.random.fold_in(key, 11)
    first_key = jax.random.fold_in(key, 0)
    second_key = jax.random.fold_in(key, 1)
    fourth_key = jax.random.fold_in(key, 3)
    position = jnp.arange(ROWS, dtype=jnp.float32) / (ROWS - 1)
    rising = jnp.exp(position * math.log(3.0))
    block_rows = ROWS // (N_DP * N_TENSOR)
    heavy_block = jax.random.randint(fourth_key, (), 0, N_DP * N_TENSOR)
    row_block = jnp.arange(ROWS, dtype=jnp.int32) // block_rows
    boost = jnp.where(row_block == heavy_block, 3.0, 1.0).astype(jnp.float32)
    spreads = jnp.exp(jax.random.uniform(second_key, (ROWS,), jnp.float32, 0.0, math.log(6.0)))
    entries = jax.random.truncated_normal(first_key, -6.0, 6.0, (D, ROWS), jnp.float32)
    return (0.1 * entries * (rising * spreads * boost)[None, :]).astype(jnp.bfloat16)


def shard_levels(stream_key, shape, cuts, low, largest):
    loudness, own = 1.0, jax.random.fold_in(stream_key, 6)
    for dim, blocks in cuts:
        heights = jnp.exp(jax.random.uniform(jax.random.fold_in(own, dim), (blocks,), jnp.float32, low / len(cuts), largest / len(cuts)))
        loudness = loudness * jnp.repeat(heights, shape[dim] // blocks).reshape([-1 if axis == dim else 1 for axis in range(len(shape))])
    return loudness


def bell_draw(own_key, extent, width, reach, cuts=(), kind=jnp.bfloat16):
    factor_of = shard_levels(own_key, extent, cuts, -0.22, 0.18) if cuts else 1.0
    values = jax.random.normal(own_key, extent, jnp.float32) * width * factor_of
    return jnp.minimum(jnp.maximum(values, -reach), reach).astype(kind)


def setup_inputs(seed: int = 0) -> dict:
    key_list = jax.random.split(jax.random.key(seed), 3)
    grad_buckets = draw_grad_buckets(jax.random.fold_in(key_list[2], 71), 0)
    sketch = bell_draw(key_list[1], (D, RANK), D ** -0.5, 0.0625, ((0, 8),))
    return {"grad_buckets": grad_buckets, "sketch": sketch}


def reference(grad_buckets, sketch):
    sketched = jnp.dot(sketch.T.astype(jnp.float32), grad_buckets.astype(jnp.float32), preferred_element_type=jnp.float32)
    gram_matrix = jnp.dot(sketched.astype(jnp.float32), sketched.T.astype(jnp.float32), precision=lax.Precision.HIGHEST, preferred_element_type=jnp.float32)
    lower_factor = jnp.linalg.cholesky(gram_matrix)
    basis_rows = jax.scipy.linalg.solve_triangular(lower_factor, sketched, lower=True)
    basis_out = (basis_rows * math.sqrt(ROWS)).astype(jnp.bfloat16)
    column_blocks = grad_buckets.reshape(8, D // 8, ROWS)

    def project_block(column_block):
        return jnp.dot(basis_rows, column_block.astype(jnp.float32).T, precision=lax.Precision.HIGHEST)
    stacked = lax.map(project_block, column_blocks)
    projected = jnp.transpose(stacked, (1, 0, 2)).reshape(RANK, D)
    return (basis_out, projected.astype(jnp.bfloat16))
```

```python
import math

import jax
import jax.numpy as jnp
from jax import lax
from jax.experimental import pallas as pl
from jax.experimental.pallas import tpu as pltpu
from jax.sharding import PartitionSpec as P

MESH = pl.DeviceIdType.MESH
F32 = jnp.float32
BF16 = jnp.bfloat16
NZ, NX, NT = 16, 4, 8
NM = NX * NT
ROWS = 57344
RANK = 512
WIDE = 16
BLK = ROWS // (NZ * NM)
COLS = BLK * NZ
PW = WIDE * NM
HALF = RANK // 2
CHUNK = 256
TDOT = (((0,), (0,)), ((), ()))


def mod(a, n):
    return lax.rem(a + n, n)


def comm_kernel(
    packed, s_piece, gall_out, rhs_out,
    recv_b, recv_s, ypart, yall, rup, rdn, wpart, wrecv, gpart, grecv, gz,
    local_sem, a2a_send, a2a_recv, s_send, s_recv, rs_send, rs_recv, ag_send, ag_recv,
    g_send, g_recv, w_send, w_recv, gz_send, gz_recv, gp_send, gp_recv,
):
    dp = lax.axis_index("dp")
    t = lax.axis_index("tensor")
    z = dp // NX
    x = dp % NX
    m = x * NT + t
    chip = m // 2
    core = m % 2

    def member(i):
        return (z * NX + i // NT, i % NT)

    def at_z(i):
        return (i * NX + x, t)

    zup, zdn = at_z(mod(z + 1, NZ)), at_z(mod(z - 1, NZ))

    barrier = pltpu.get_barrier_semaphore()

    @pl.loop(1, NM)
    def _(k):
        pl.semaphore_signal(barrier, inc=1, device_id=member((m + k) % NM), device_id_type=MESH)

    @pl.loop(1, NZ)
    def _(k):
        pl.semaphore_signal(barrier, inc=1, device_id=at_z((z + k) % NZ), device_id_type=MESH)

    pl.semaphore_wait(barrier, NM - 1 + NZ - 1)

    def b_copy(k):
        peer = (m + k) % NM
        return pltpu.make_async_remote_copy(
            src_ref=packed.at[peer], dst_ref=recv_b.at[pl.ds(pl.multiple_of(m * WIDE, WIDE), WIDE)],
            send_sem=a2a_send.at[k], recv_sem=a2a_recv.at[k], device_id=member(peer), device_id_type=MESH,
        )

    def s_copy(k):
        peer = (t + k) % NT
        return pltpu.make_async_remote_copy(
            src_ref=s_piece, dst_ref=recv_s.at[:, t],
            send_sem=s_send.at[k], recv_sem=s_recv.at[k], device_id=(dp, peer), device_id_type=MESH,
        )

    @pl.loop(1, NT)
    def _(k):
        s_copy(k).start()

    @pl.loop(1, NM)
    def _(k):
        b_copy(k).start()

    own_b = pltpu.make_async_copy(
        packed.at[m], recv_b.at[pl.ds(pl.multiple_of(m * WIDE, WIDE), WIDE)], local_sem.at[0])
    own_s = pltpu.make_async_copy(s_piece, recv_s.at[:, t], local_sem.at[1])
    own_b.start()
    own_s.start()
    own_b.wait()
    own_s.wait()

    @pl.loop(1, NT)
    def _(k):
        s_copy(k).wait()

    @pl.loop(1, NM)
    def _(k):
        b_copy(k).wait()

    @pl.loop(0, COLS // CHUNK)
    def _(i):
        rows = pl.ds(pl.multiple_of(i * CHUNK, CHUNK), CHUNK)
        ypart[rows, :] = lax.dot_general(
            recv_b[:, rows], recv_s[...].reshape(PW, RANK), TDOT, preferred_element_type=F32)

    def block(b):
        return pl.ds(pl.multiple_of(mod(b, NZ) * BLK, 8), BLK)

    halves = (pl.ds(0, HALF), pl.ds(HALF, HALF))
    chains = ((0, 1, 0, 0), (1, -1, 1, 0), (2, 1, 1, 1), (3, -1, 0, 1))

    def rs_copy(chain, s, src):
        name, way, h, _ = chain
        buf = rup if way == 1 else rdn
        return pltpu.make_async_remote_copy(
            src_ref=src, dst_ref=buf.at[s, :, halves[h]],
            send_sem=rs_send.at[name, s], recv_sem=rs_recv.at[name, s],
            device_id=zup if way == 1 else zdn, device_id_type=MESH,
        )

    def rs_first(chain):
        _, way, h, s = chain
        rs_copy(chain, s, ypart.at[block(z + way * (8 - s)), halves[h]]).start()

    def rs_next(chain, s):
        _, way, h, _ = chain
        buf = rup if way == 1 else rdn
        slot = buf.at[s - 1, :, halves[h]]
        rs_copy(chain, s - 1, slot).wait_recv()
        buf[s - 1, :, halves[h]] += ypart[block(z + way * (8 - s)), halves[h]]
        rs_copy(chain, s, slot).start()

    for chain in chains:
        rs_first(chain)
    for chain in chains[:2]:
        rs_next(chain, 1)

    @pl.loop(2, 8)
    def _(s):
        for chain in chains:
            rs_next(chain, s)

    own = block(z)
    for chain in chains:
        _, way, h, _ = chain
        rs_copy(chain, 7, (rup if way == 1 else rdn).at[7, :, halves[h]]).wait_recv()
    yall[own, :] = ypart[own, :] + rup[7] + rdn[7]

    def ag_copy(chain, s):
        name, way, h, _ = chain
        piece = yall.at[block(z - way * s), halves[h]]
        return pltpu.make_async_remote_copy(
            src_ref=piece, dst_ref=piece, send_sem=ag_send.at[name, s], recv_sem=ag_recv.at[name, s],
            device_id=zup if way == 1 else zdn, device_id_type=MESH,
        )

    def ag_arrived(chain, s):
        name, way, h, _ = chain
        piece = yall.at[block(z - way * (s + 1)), halves[h]]
        pltpu.make_async_remote_copy(
            src_ref=piece, dst_ref=piece, send_sem=ag_send.at[name, s], recv_sem=ag_recv.at[name, s],
            device_id=zup if way == 1 else zdn, device_id_type=MESH,
        ).wait_recv()

    for chain in chains:
        ag_copy(chain, 0).start()
    rhs_out[pl.ds(0, BLK), :] = yall[own, :]

    @pl.loop(1, 7)
    def _(s):
        for chain in chains:
            ag_arrived(chain, s - 1)
            ag_copy(chain, s).start()

    for chain in chains[:2]:
        ag_arrived(chain, 6)
        ag_copy(chain, 7).start()
    for chain in chains[2:]:
        ag_arrived(chain, 6)
    for chain in chains[:2]:
        ag_arrived(chain, 7)

    gcols = pl.ds(pl.multiple_of((z // 4) * 128, 128), 128)
    gpart[...] = jnp.zeros_like(gpart)

    @pl.loop(0, COLS // CHUNK)
    def _(i):
        rows = pl.ds(pl.multiple_of(i * CHUNK, CHUNK), CHUNK)
        y = yall[rows, :]
        hi = y.astype(BF16)
        lo = (y - hi.astype(F32)).astype(BF16)
        ys = yall[rows, gcols]
        shi = ys.astype(BF16)
        slo = (ys - shi.astype(F32)).astype(BF16)
        gpart[...] += (
            lax.dot_general(shi, hi, TDOT, preferred_element_type=F32)
            + (lax.dot_general(shi, lo, TDOT, preferred_element_type=F32)
               + lax.dot_general(slo, hi, TDOT, preferred_element_type=F32))
        )

    def tile(j):
        return gpart.at[
            pl.ds(pl.multiple_of((z % 4) * 32 + (j // 4) * 8, 8), 8), pl.ds(pl.multiple_of((j % 4) * 128, 128), 128)]

    def g_copy(k):
        peer = (m + k) % NM
        return pltpu.make_async_remote_copy(
            src_ref=tile(peer // 2), dst_ref=grecv.at[m],
            send_sem=g_send.at[k], recv_sem=g_recv.at[k], device_id=member(peer), device_id_type=MESH,
        )

    @pl.loop(1, NM)
    def _(k):
        g_copy(k).start()

    own_g = pltpu.make_async_copy(tile(chip), grecv.at[m], local_sem.at[2])
    own_g.start()

    wpart[...] = jnp.zeros_like(wpart)

    @pl.loop(0, COLS // CHUNK)
    def _(i):
        rows = pl.ds(pl.multiple_of(i * CHUNK, CHUNK), CHUNK)
        y = yall[rows, :]
        hi = y.astype(BF16)
        lo = (y - hi.astype(F32)).astype(BF16)
        b = recv_b[:, rows]
        wpart[...] += jnp.dot(b, hi, preferred_element_type=F32) + jnp.dot(b, lo, preferred_element_type=F32)

    own_g.wait()

    @pl.loop(1, NM)
    def _(k):
        g_copy(k).wait()

    gz[z] = jnp.sum(grecv[...], axis=0)

    def gz_copy(k):
        return pltpu.make_async_remote_copy(
            src_ref=gz.at[z], dst_ref=gz.at[z], send_sem=gz_send.at[k], recv_sem=gz_recv.at[k],
            device_id=at_z((z + k) % NZ), device_id_type=MESH,
        )

    def gz_arrived(k):
        piece = gz.at[mod(z - k, NZ)]
        pltpu.make_async_remote_copy(
            src_ref=piece, dst_ref=piece, send_sem=gz_send.at[k], recv_sem=gz_recv.at[k],
            device_id=at_z((z + k) % NZ), device_id_type=MESH,
        ).wait_recv()

    @pl.loop(1, NZ)
    def _(k):
        gz_copy(k).start()

    def w_copy(k):
        peer = (m + k) % NM
        return pltpu.make_async_remote_copy(
            src_ref=wpart.at[pl.ds(pl.multiple_of(peer * WIDE, WIDE), WIDE)], dst_ref=wrecv.at[m],
            send_sem=w_send.at[k], recv_sem=w_recv.at[k], device_id=member(peer), device_id_type=MESH,
        )

    own_w = pltpu.make_async_copy(
        wpart.at[pl.ds(pl.multiple_of(m * WIDE, WIDE), WIDE)], wrecv.at[m], local_sem.at[3])

    @pl.loop(1, NZ)
    def _(k):
        gz_arrived(k)

    def gp_copy(k):
        peer = (chip + k) % (NM // 2)
        return pltpu.make_async_remote_copy(
            src_ref=gz, dst_ref=gall_out.at[chip], send_sem=gp_send.at[k], recv_sem=gp_recv.at[k],
            device_id=member(peer * 2 + core), device_id_type=MESH,
        )

    @pl.loop(1, NM // 2)
    def _(k):
        gp_copy(k).start()

    own_w.start()

    @pl.loop(1, NM)
    def _(k):
        w_copy(k).start()

    gall_out[chip] = gz[...]
    own_w.wait()

    @pl.loop(1, NM)
    def _(k):
        w_copy(k).wait()

    rhs_out[pl.ds(BLK, WIDE), :] = jnp.sum(wrecv[...], axis=0)

    @pl.loop(1, NM // 2)
    def _(k):
        gp_copy(k).wait()

    @pl.loop(1, NZ)
    def _(k):
        gz_copy(k).wait_send()

    for chain in chains:
        first = chain[3]
        _, way, h, _ = chain
        buf = rup if way == 1 else rdn

        @pl.loop(first, 8)
        def _(s):
            rs_copy(chain, s, buf.at[s, :, halves[h]]).wait_send()

        @pl.loop(0, 8 - first)
        def _(s):
            ag_copy(chain, s).wait_send()


def exchange(packed, s_piece):
    vmem = pl.BlockSpec(memory_space=pltpu.VMEM)
    dma = pltpu.SemaphoreType.DMA
    return pl.pallas_call(
        comm_kernel,
        out_shape=(
            jax.ShapeDtypeStruct((NM // 2, NZ, 8, 128), F32),
            jax.ShapeDtypeStruct((BLK + WIDE, RANK), F32),
        ),
        in_specs=[vmem, vmem],
        out_specs=(vmem, vmem),
        scratch_shapes=[
            pltpu.VMEM((PW, COLS), BF16),
            pltpu.VMEM((NX, NT, WIDE, RANK), BF16),
            pltpu.VMEM((COLS, RANK), F32),
            pltpu.VMEM((COLS, RANK), F32),
            pltpu.VMEM((8, BLK, RANK), F32),
            pltpu.VMEM((8, BLK, RANK), F32),
            pltpu.VMEM((PW, RANK), F32),
            pltpu.VMEM((NM, WIDE, RANK), F32),
            pltpu.VMEM((128, RANK), F32),
            pltpu.VMEM((NM, 8, 128), F32),
            pltpu.VMEM((NZ, 8, 128), F32),
            dma((4,)),
            dma((NM,)), dma((NM,)),
            dma((NT,)), dma((NT,)),
            dma((4, 8)), dma((4, 8)),
            dma((4, 8)), dma((4, 8)),
            dma((NM,)), dma((NM,)),
            dma((NM,)), dma((NM,)),
            dma((NZ,)), dma((NZ,)),
            dma((NM // 2,)), dma((NM // 2,)),
        ],
        compiler_params=pltpu.CompilerParams(
            collective_id=0, has_side_effects=True, vmem_limit_bytes=48 * 1024 * 1024),
    )(packed, s_piece)


def shards(grad_buckets, sketch):
    z = lax.axis_index("dp") // NX
    packed = grad_buckets.reshape(WIDE, NZ, NM, BLK).transpose(2, 0, 1, 3).reshape(NM, WIDE, COLS)
    s_piece = lax.dynamic_slice_in_dim(sketch, z * (NX * WIDE), NX * WIDE, 0).reshape(NX, WIDE, RANK)
    gall, rhs = exchange(packed, s_piece)
    gram = gall.reshape(4, 4, NZ, 8, 128).transpose(2, 0, 3, 1, 4).reshape(RANK, RANK)
    lower = jnp.linalg.cholesky(gram)
    solved = jax.scipy.linalg.solve_triangular(lower, rhs.T, lower=True)
    basis_out = (solved[:, :BLK] * math.sqrt(ROWS)).astype(BF16)
    mine = solved[:, BLK:].astype(BF16).reshape(NZ * NX, RANK // (NZ * NX), WIDE)
    got = lax.all_to_all(mine, "dp", split_axis=0, concat_axis=0, tiled=True)
    projected = got.transpose(1, 0, 2).reshape(RANK // (NZ * NX), NZ * NX * WIDE)
    return basis_out, projected


def solution(mesh):
    in_specs = (P(("tensor", "dp"), None), P("tensor", None))
    out_specs = (P(None, ("dp", "tensor")), P("dp", "tensor"))
    return jax.shard_map(shards, mesh=mesh, in_specs=in_specs, out_specs=out_specs, check_vma=False)
```

```python
import math

import jax
import jax.numpy as jnp
from jax import lax
from jax.experimental import pallas as pl
from jax.experimental.pallas import tpu as pltpu
from jax.sharding import PartitionSpec as P

MESH = pl.DeviceIdType.MESH
F32 = jnp.float32
BF16 = jnp.bfloat16
NZ, NX, NT = 16, 4, 8
NM = NX * NT
ROWS = 57344
RANK = 512
WIDE = 16
BLK = ROWS // (NZ * NM)
COLS = BLK * NZ
PW = WIDE * NM
HALF = RANK // 2
CHUNK = 256
N_DP = NZ * NX
PER_DP = RANK // N_DP
NB = 128
GROUP = 8
HIGHEST = lax.Precision.HIGHEST
TDOT = (((0,), (0,)), ((), ()))


def mod(a, n):
    return lax.rem(a + n, n)


def comm_kernel(
    packed, s_piece, gall_out, rhs_out,
    recv_b, recv_s, ypart, yall, rup, rdn, wpart, wrecv, gpart, grecv, gz,
    local_sem, a2a_send, a2a_recv, s_send, s_recv, rs_send, rs_recv, ag_send, ag_recv,
    g_send, g_recv, w_send, w_recv, gz_send, gz_recv, gp_send, gp_recv,
):
    dp = lax.axis_index("dp")
    t = lax.axis_index("tensor")
    z = dp // NX
    x = dp % NX
    m = x * NT + t
    chip = m // 2
    core = m % 2

    def member(i):
        return (z * NX + i // NT, i % NT)

    def at_z(i):
        return (i * NX + x, t)

    zup, zdn = at_z(mod(z + 1, NZ)), at_z(mod(z - 1, NZ))

    barrier = pltpu.get_barrier_semaphore()

    @pl.loop(1, NM)
    def _(k):
        pl.semaphore_signal(barrier, inc=1, device_id=member((m + k) % NM), device_id_type=MESH)

    @pl.loop(1, NZ)
    def _(k):
        pl.semaphore_signal(barrier, inc=1, device_id=at_z((z + k) % NZ), device_id_type=MESH)

    pl.semaphore_wait(barrier, NM - 1 + NZ - 1)

    def b_copy(k):
        peer = (m + k) % NM
        return pltpu.make_async_remote_copy(
            src_ref=packed.at[peer], dst_ref=recv_b.at[pl.ds(pl.multiple_of(m * WIDE, WIDE), WIDE)],
            send_sem=a2a_send.at[k], recv_sem=a2a_recv.at[k], device_id=member(peer), device_id_type=MESH,
        )

    def s_copy(k):
        peer = (t + k) % NT
        return pltpu.make_async_remote_copy(
            src_ref=s_piece, dst_ref=recv_s.at[:, t],
            send_sem=s_send.at[k], recv_sem=s_recv.at[k], device_id=(dp, peer), device_id_type=MESH,
        )

    @pl.loop(1, NT)
    def _(k):
        s_copy(k).start()

    @pl.loop(1, NM)
    def _(k):
        b_copy(k).start()

    own_b = pltpu.make_async_copy(
        packed.at[m], recv_b.at[pl.ds(pl.multiple_of(m * WIDE, WIDE), WIDE)], local_sem.at[0])
    own_s = pltpu.make_async_copy(s_piece, recv_s.at[:, t], local_sem.at[1])
    own_b.start()
    own_s.start()
    own_b.wait()
    own_s.wait()

    @pl.loop(1, NT)
    def _(k):
        s_copy(k).wait()

    @pl.loop(1, NM)
    def _(k):
        b_copy(k).wait()

    @pl.loop(0, COLS // CHUNK)
    def _(i):
        rows = pl.ds(pl.multiple_of(i * CHUNK, CHUNK), CHUNK)
        ypart[rows, :] = lax.dot_general(
            recv_b[:, rows], recv_s[...].reshape(PW, RANK), TDOT, preferred_element_type=F32)

    def block(b):
        return pl.ds(pl.multiple_of(mod(b, NZ) * BLK, 8), BLK)

    halves = (pl.ds(0, HALF), pl.ds(HALF, HALF))
    chains = ((0, 1, 0, 0), (1, -1, 1, 0), (2, 1, 1, 1), (3, -1, 0, 1))

    def rs_copy(chain, s, src):
        name, way, h, _ = chain
        buf = rup if way == 1 else rdn
        return pltpu.make_async_remote_copy(
            src_ref=src, dst_ref=buf.at[s, :, halves[h]],
            send_sem=rs_send.at[name, s], recv_sem=rs_recv.at[name, s],
            device_id=zup if way == 1 else zdn, device_id_type=MESH,
        )

    def rs_first(chain):
        _, way, h, s = chain
        rs_copy(chain, s, ypart.at[block(z + way * (8 - s)), halves[h]]).start()

    def rs_next(chain, s):
        _, way, h, _ = chain
        buf = rup if way == 1 else rdn
        slot = buf.at[s - 1, :, halves[h]]
        rs_copy(chain, s - 1, slot).wait_recv()
        buf[s - 1, :, halves[h]] += ypart[block(z + way * (8 - s)), halves[h]]
        rs_copy(chain, s, slot).start()

    for chain in chains:
        rs_first(chain)
    for chain in chains[:2]:
        rs_next(chain, 1)

    @pl.loop(2, 8)
    def _(s):
        for chain in chains:
            rs_next(chain, s)

    own = block(z)
    for chain in chains:
        _, way, h, _ = chain
        rs_copy(chain, 7, (rup if way == 1 else rdn).at[7, :, halves[h]]).wait_recv()
    yall[own, :] = ypart[own, :] + rup[7] + rdn[7]

    def ag_copy(chain, s):
        name, way, h, _ = chain
        piece = yall.at[block(z - way * s), halves[h]]
        return pltpu.make_async_remote_copy(
            src_ref=piece, dst_ref=piece, send_sem=ag_send.at[name, s], recv_sem=ag_recv.at[name, s],
            device_id=zup if way == 1 else zdn, device_id_type=MESH,
        )

    def ag_arrived(chain, s):
        name, way, h, _ = chain
        piece = yall.at[block(z - way * (s + 1)), halves[h]]
        pltpu.make_async_remote_copy(
            src_ref=piece, dst_ref=piece, send_sem=ag_send.at[name, s], recv_sem=ag_recv.at[name, s],
            device_id=zup if way == 1 else zdn, device_id_type=MESH,
        ).wait_recv()

    for chain in chains:
        ag_copy(chain, 0).start()
    rhs_out[pl.ds(0, BLK), :] = yall[own, :]

    @pl.loop(1, 7)
    def _(s):
        for chain in chains:
            ag_arrived(chain, s - 1)
            ag_copy(chain, s).start()

    for chain in chains[:2]:
        ag_arrived(chain, 6)
        ag_copy(chain, 7).start()
    for chain in chains[2:]:
        ag_arrived(chain, 6)
    for chain in chains[:2]:
        ag_arrived(chain, 7)

    gcols = pl.ds(pl.multiple_of((z // 4) * 128, 128), 128)
    gpart[...] = jnp.zeros_like(gpart)

    @pl.loop(0, COLS // CHUNK)
    def _(i):
        rows = pl.ds(pl.multiple_of(i * CHUNK, CHUNK), CHUNK)
        y = yall[rows, :]
        hi = y.astype(BF16)
        lo = (y - hi.astype(F32)).astype(BF16)
        ys = yall[rows, gcols]
        shi = ys.astype(BF16)
        slo = (ys - shi.astype(F32)).astype(BF16)
        gpart[...] += (
            lax.dot_general(shi, hi, TDOT, preferred_element_type=F32)
            + (lax.dot_general(shi, lo, TDOT, preferred_element_type=F32)
               + lax.dot_general(slo, hi, TDOT, preferred_element_type=F32))
        )

    def tile(j):
        return gpart.at[
            pl.ds(pl.multiple_of((z % 4) * 32 + (j // 4) * 8, 8), 8), pl.ds(pl.multiple_of((j % 4) * 128, 128), 128)]

    def g_copy(k):
        peer = (m + k) % NM
        return pltpu.make_async_remote_copy(
            src_ref=tile(peer // 2), dst_ref=grecv.at[m],
            send_sem=g_send.at[k], recv_sem=g_recv.at[k], device_id=member(peer), device_id_type=MESH,
        )

    @pl.loop(1, NM)
    def _(k):
        g_copy(k).start()

    own_g = pltpu.make_async_copy(tile(chip), grecv.at[m], local_sem.at[2])
    own_g.start()

    wpart[...] = jnp.zeros_like(wpart)

    @pl.loop(0, COLS // CHUNK)
    def _(i):
        rows = pl.ds(pl.multiple_of(i * CHUNK, CHUNK), CHUNK)
        y = yall[rows, :]
        hi = y.astype(BF16)
        lo = (y - hi.astype(F32)).astype(BF16)
        b = recv_b[:, rows]
        wpart[...] += jnp.dot(b, hi, preferred_element_type=F32) + jnp.dot(b, lo, preferred_element_type=F32)

    own_g.wait()

    @pl.loop(1, NM)
    def _(k):
        g_copy(k).wait()

    gz[z] = jnp.sum(grecv[...], axis=0)

    def gz_copy(k):
        return pltpu.make_async_remote_copy(
            src_ref=gz.at[z], dst_ref=gz.at[z], send_sem=gz_send.at[k], recv_sem=gz_recv.at[k],
            device_id=at_z((z + k) % NZ), device_id_type=MESH,
        )

    def gz_arrived(k):
        piece = gz.at[mod(z - k, NZ)]
        pltpu.make_async_remote_copy(
            src_ref=piece, dst_ref=piece, send_sem=gz_send.at[k], recv_sem=gz_recv.at[k],
            device_id=at_z((z + k) % NZ), device_id_type=MESH,
        ).wait_recv()

    @pl.loop(1, NZ)
    def _(k):
        gz_copy(k).start()

    def w_copy(k):
        peer = (m + k) % NM
        return pltpu.make_async_remote_copy(
            src_ref=wpart.at[pl.ds(pl.multiple_of(peer * WIDE, WIDE), WIDE)], dst_ref=wrecv.at[m],
            send_sem=w_send.at[k], recv_sem=w_recv.at[k], device_id=member(peer), device_id_type=MESH,
        )

    own_w = pltpu.make_async_copy(
        wpart.at[pl.ds(pl.multiple_of(m * WIDE, WIDE), WIDE)], wrecv.at[m], local_sem.at[3])

    @pl.loop(1, NZ)
    def _(k):
        gz_arrived(k)

    def gp_copy(k):
        peer = (chip + k) % (NM // 2)
        return pltpu.make_async_remote_copy(
            src_ref=gz, dst_ref=gall_out.at[chip], send_sem=gp_send.at[k], recv_sem=gp_recv.at[k],
            device_id=member(peer * 2 + core), device_id_type=MESH,
        )

    @pl.loop(1, NM // 2)
    def _(k):
        gp_copy(k).start()

    own_w.start()

    @pl.loop(1, NM)
    def _(k):
        w_copy(k).start()

    gall_out[chip] = gz[...]
    own_w.wait()

    @pl.loop(1, NM)
    def _(k):
        w_copy(k).wait()

    rhs_out[pl.ds(BLK, WIDE), :] = jnp.sum(wrecv[...], axis=0)

    @pl.loop(1, NM // 2)
    def _(k):
        gp_copy(k).wait()

    @pl.loop(1, NZ)
    def _(k):
        gz_copy(k).wait_send()

    for chain in chains:
        first = chain[3]
        _, way, h, _ = chain
        buf = rup if way == 1 else rdn

        @pl.loop(first, 8)
        def _(s):
            rs_copy(chain, s, buf.at[s, :, halves[h]]).wait_send()

        @pl.loop(0, 8 - first)
        def _(s):
            ag_copy(chain, s).wait_send()


def exchange(packed, s_piece):
    vmem = pl.BlockSpec(memory_space=pltpu.VMEM)
    dma = pltpu.SemaphoreType.DMA
    return pl.pallas_call(
        comm_kernel,
        out_shape=(
            jax.ShapeDtypeStruct((NM // 2, NZ, 8, 128), F32),
            jax.ShapeDtypeStruct((BLK + WIDE, RANK), F32),
        ),
        in_specs=[vmem, vmem],
        out_specs=(vmem, vmem),
        scratch_shapes=[
            pltpu.VMEM((PW, COLS), BF16),
            pltpu.VMEM((NX, NT, WIDE, RANK), BF16),
            pltpu.VMEM((COLS, RANK), F32),
            pltpu.VMEM((COLS, RANK), F32),
            pltpu.VMEM((8, BLK, RANK), F32),
            pltpu.VMEM((8, BLK, RANK), F32),
            pltpu.VMEM((PW, RANK), F32),
            pltpu.VMEM((NM, WIDE, RANK), F32),
            pltpu.VMEM((128, RANK), F32),
            pltpu.VMEM((NM, 8, 128), F32),
            pltpu.VMEM((NZ, 8, 128), F32),
            dma((4,)),
            dma((NM,)), dma((NM,)),
            dma((NT,)), dma((NT,)),
            dma((4, 8)), dma((4, 8)),
            dma((4, 8)), dma((4, 8)),
            dma((NM,)), dma((NM,)),
            dma((NM,)), dma((NM,)),
            dma((NZ,)), dma((NZ,)),
            dma((NM // 2,)), dma((NM // 2,)),
        ],
        compiler_params=pltpu.CompilerParams(
            collective_id=0, has_side_effects=True, vmem_limit_bytes=48 * 1024 * 1024),
    )(packed, s_piece)


def invert_factor(work):
    for s in range(0, NB, GROUP):
        n = NB - s
        row = lax.broadcasted_iota(jnp.int32, (GROUP, NB), 0)
        lane = lax.broadcasted_iota(jnp.int32, (GROUP, NB), 1)
        rest = work[s:, :]
        cols = [jnp.broadcast_to(rest[:, s + k : s + k + 1], (n, NB)) for k in range(GROUP)]
        top = jnp.where((lane >= s) & (lane < s + GROUP), jnp.where(lane - s == row, 1.0, 0.0), rest[:GROUP])
        below = rest[GROUP:]
        if n > GROUP:
            lane_b = lax.broadcasted_iota(jnp.int32, (n - GROUP, NB), 1)
            below = jnp.where((lane_b >= s) & (lane_b < s + GROUP), 0.0, below)
        for k in range(GROUP):
            r = lax.rsqrt(jnp.broadcast_to(cols[k][k : k + 1], (GROUP, NB)))
            mult = cols[k] * jnp.broadcast_to(r[:1], (n, NB))
            for q in range(k + 1, GROUP):
                cols[q] = cols[q] - mult * jnp.broadcast_to(mult[q : q + 1], (n, NB))
            u = jnp.broadcast_to(top[k : k + 1], (GROUP, NB)) * r
            top = jnp.where(row == k, u, jnp.where(row > k, top - mult[:GROUP] * u, top))
            if n > GROUP:
                below = below - mult[GROUP:] * jnp.broadcast_to(u[:1], (n - GROUP, NB))
        work[s : s + GROUP, :] = top
        if n > GROUP:
            work[s + GROUP :, :] = below


def finish_kernel(gall, rhs, basis_out, proj_out, mat, work, solved, outbox, inbox, sends, recvs):
    dp = lax.axis_index("dp")
    t = lax.axis_index("tensor")

    barrier = pltpu.get_barrier_semaphore()

    @pl.loop(1, N_DP)
    def _(k):
        pl.semaphore_signal(barrier, inc=1, device_id=((dp + k) % N_DP, t), device_id_type=MESH)

    @pl.loop(0, NZ)
    def _(z):
        for j in range(NM // 2):
            mat[pl.ds(pl.multiple_of(z * 32 + (j // 4) * 8, 8), 8), pl.ds((j % 4) * 128, 128)] = gall[j, z]

    mat[:, RANK:] = rhs[...].T

    @pl.loop(0, RANK // NB)
    def _(j):
        rows = pl.ds(pl.multiple_of(j * NB, NB), NB)
        work[...] = mat[rows, rows]
        invert_factor(work)
        row = lax.broadcasted_iota(jnp.int32, (NB, NB), 0)
        lane = lax.broadcasted_iota(jnp.int32, (NB, NB), 1)
        inverse = jnp.where(lane <= row, work[...], 0.0)
        upper = jnp.dot(inverse, mat[rows, :], precision=HIGHEST, preferred_element_type=F32)
        solved[rows, :] = upper[:, RANK:]
        for i in range(1, RANK // NB):
            @pl.when(i > j)
            def _():
                mat[i * NB : (i + 1) * NB, :] -= lax.dot_general(
                    upper[:, i * NB : (i + 1) * NB], upper, TDOT, precision=HIGHEST, preferred_element_type=F32)

    packed = jnp.zeros((N_DP, NB), F32)
    lane = lax.broadcasted_iota(jnp.int32, (N_DP, NB), 1)
    for r in range(PER_DP):
        part = solved[pl.ds(r, N_DP, stride=PER_DP), :]
        slot = PER_DP - 1 - r
        packed = jnp.where(lane // WIDE == slot, pltpu.roll(part, (WIDE * slot - BLK) % NB, 1), packed)
    outbox[...] = packed.reshape(N_DP, 1, NB)

    pl.semaphore_wait(barrier, N_DP - 1)

    def copy(k):
        peer = (dp + k) % N_DP
        return pltpu.make_async_remote_copy(
            src_ref=outbox.at[peer], dst_ref=inbox.at[dp], send_sem=sends.at[k], recv_sem=recvs.at[k],
            device_id=(peer, t), device_id_type=MESH,
        )

    @pl.loop(1, N_DP)
    def _(k):
        copy(k).start()

    inbox[dp] = outbox[dp]
    basis_out[...] = (solved[:, :BLK] * math.sqrt(ROWS)).astype(BF16)

    @pl.loop(1, N_DP)
    def _(k):
        copy(k).wait()

    per_tile = NB // WIDE
    lane = lax.broadcasted_iota(jnp.int32, (PER_DP, NB), 1)
    for q in range(N_DP // per_tile):
        tile = jnp.zeros((PER_DP, NB), F32)
        for i in range(per_tile):
            line = jnp.broadcast_to(inbox[q * per_tile + i], (PER_DP, NB))
            line = pltpu.roll(line, 0, 1, stride=WIDE, stride_axis=0)
            line = pltpu.roll(line, (WIDE * (i + 1)) % NB, 1)
            tile = jnp.where(lane // WIDE == i, line, tile)
        proj_out[:, q * NB : (q + 1) * NB] = tile.astype(BF16)


def finish(gall, rhs):
    vmem = pl.BlockSpec(memory_space=pltpu.VMEM)
    return pl.pallas_call(
        finish_kernel,
        out_shape=(
            jax.ShapeDtypeStruct((RANK, BLK), BF16),
            jax.ShapeDtypeStruct((PER_DP, N_DP * WIDE), BF16),
        ),
        in_specs=[vmem, vmem],
        out_specs=(vmem, vmem),
        scratch_shapes=[
            pltpu.VMEM((RANK, RANK + NB), F32),
            pltpu.VMEM((NB, NB), F32),
            pltpu.VMEM((RANK, NB), F32),
            pltpu.VMEM((N_DP, 1, NB), F32),
            pltpu.VMEM((N_DP, 1, NB), F32),
            pltpu.SemaphoreType.DMA((N_DP,)),
            pltpu.SemaphoreType.DMA((N_DP,)),
        ],
        compiler_params=pltpu.CompilerParams(
            collective_id=1, has_side_effects=True, vmem_limit_bytes=32 * 1024 * 1024),
    )(gall, rhs)


def shards(grad_buckets, sketch):
    z = lax.axis_index("dp") // NX
    packed = grad_buckets.reshape(WIDE, NZ, NM, BLK).transpose(2, 0, 1, 3).reshape(NM, WIDE, COLS)
    s_piece = lax.dynamic_slice_in_dim(sketch, z * (NX * WIDE), NX * WIDE, 0).reshape(NX, WIDE, RANK)
    return finish(*exchange(packed, s_piece))


def solution(mesh):
    in_specs = (P(("tensor", "dp"), None), P("tensor", None))
    out_specs = (P(None, ("dp", "tensor")), P("dp", "tensor"))
    return jax.shard_map(shards, mesh=mesh, in_specs=in_specs, out_specs=out_specs, check_vma=False)
```

```python
import math

import jax
import jax.numpy as jnp
from jax import lax
from jax.experimental import pallas as pl
from jax.experimental.pallas import tpu as pltpu
from jax.sharding import PartitionSpec as P

MESH = pl.DeviceIdType.MESH
F32 = jnp.float32
BF16 = jnp.bfloat16
NZ, NX, NT = 16, 4, 8
NM = NX * NT
ROWS = 57344
RANK = 512
WIDE = 16
BLK = ROWS // (NZ * NM)
COLS = BLK * NZ
PW = WIDE * NM
HALF = RANK // 2
PARTS = (0, 384, 896, 1280, 1792)
N_DP = NZ * NX
PER_DP = RANK // N_DP
NB = 128
GROUP = 8
HIGHEST = lax.Precision.HIGHEST
TDOT = (((0,), (0,)), ((), ()))


def mod(a, n):
    return lax.rem(a + n, n)


def near(k):
    if k == 0:
        return NZ - 1
    if abs(k) == NZ // 2:
        return 0
    return NZ - 1 - 2 * k if k > 0 else NZ + 2 * k


ORDER = sorted(range(1 - NZ // 2, NZ // 2 + 1), key=near)


def await_bytes(ref, sem):
    pltpu.make_async_copy(ref, ref, sem).wait()


def comm_kernel(
    grad, sketch, gall_out, rhs_out,
    packed, recv_b, recv_s, ypart, yall, rup, rdn, wpart, wsib, wrecv, gpart, grecv, gz,
    local_sem, a2a_send, a2a_recv, s_send, s_recv, rs_send, rs_recv, ag_send, ag_recv,
    g_send, g_recv, pair_send, pair_recv, w_send, w_recv, gz_send, gz_recv, gp_send, gp_recv, gs_send, gs_recv,
):
    dp = lax.axis_index("dp")
    t = lax.axis_index("tensor")
    z = dp // NX
    x = dp % NX
    m = x * NT + t
    chip = m // 2
    core = m % 2

    def member(i):
        return (z * NX + i // NT, i % NT)

    def at_z(i):
        return (i * NX + x, t)

    zup, zdn = at_z(mod(z + 1, NZ)), at_z(mod(z - 1, NZ))
    sibling = (dp, t + 1 - 2 * core)

    barrier = pltpu.get_barrier_semaphore()

    @pl.loop(1, NM)
    def _(k):
        pl.semaphore_signal(barrier, inc=1, device_id=member((m + k) % NM), device_id_type=MESH)

    @pl.loop(1, NZ)
    def _(k):
        pl.semaphore_signal(barrier, inc=1, device_id=at_z((z + k) % NZ), device_id_type=MESH)

    mine = pl.ds(pl.multiple_of(m * WIDE, WIDE), WIDE)

    def pack(c):
        @pl.loop(0, NM // 8)
        def _(q):
            for place in range(4 * c, 4 * c + 4):
                first = ((z + ORDER[place] + NZ) % NZ) * (NM * BLK) + q * (8 * BLK)
                part = grad[:, pl.ds(pl.multiple_of(first, 128), 8 * BLK)]
                for i in range(8):
                    packed[q * 8 + i, :, place * BLK : (place + 1) * BLK] = part[:, i * BLK : (i + 1) * BLK]

    def b_copy(c, k):
        peer = (m + k) % NM
        lanes = pl.ds(PARTS[c], PARTS[c + 1] - PARTS[c])
        return pltpu.make_async_remote_copy(
            src_ref=packed.at[peer, :, lanes], dst_ref=recv_b.at[mine, lanes],
            send_sem=a2a_send.at[c], recv_sem=a2a_recv.at[c], device_id=member(peer), device_id_type=MESH,
        )

    def s_copy(k):
        peer = (t + k) % NT
        return pltpu.make_async_remote_copy(
            src_ref=sketch.at[z], dst_ref=recv_s.at[:, t],
            send_sem=s_send.at[k], recv_sem=s_recv.at[k], device_id=(dp, peer), device_id_type=MESH,
        )

    own_s = pltpu.make_async_copy(sketch.at[z], recv_s.at[:, t], local_sem.at[0])
    own_s.start()
    for c in range(4):
        pack(c)
        if c == 0:
            pl.semaphore_wait(barrier, NM - 1 + NZ - 1)

            @pl.loop(1, NT)
            def _(k):
                s_copy(k).start()

        @pl.loop(1, NM)
        def _(k):
            b_copy(c, k).start()

    own_b = pltpu.make_async_copy(packed.at[m], recv_b.at[mine], local_sem.at[1])
    own_b.start()
    own_b.wait()
    own_s.wait()

    @pl.loop(1, NT)
    def _(k):
        s_copy(k).wait()

    def rows_of(k):
        return pl.ds(near(k) * BLK, BLK)

    halves = (pl.ds(0, HALF), pl.ds(HALF, HALF))
    chains = ((0, 1, 0, 0), (1, -1, 1, 0), (2, 1, 1, 1), (3, -1, 0, 1))

    def rs_copy(chain, s, src):
        name, way, h, _ = chain
        buf = rup if way == 1 else rdn
        return pltpu.make_async_remote_copy(
            src_ref=src, dst_ref=buf.at[s, :, halves[h]],
            send_sem=rs_send.at[name, s], recv_sem=rs_recv.at[name, s],
            device_id=zup if way == 1 else zdn, device_id_type=MESH,
        )

    def rs_step(s):
        for chain in chains:
            _, way, h, first = chain
            rows = rows_of(way * (8 - s))
            if s == first:
                rs_copy(chain, s, ypart.at[rows, halves[h]]).start()
            elif s > first:
                buf = rup if way == 1 else rdn
                slot = buf.at[s - 1, :, halves[h]]
                rs_copy(chain, s - 1, slot).wait_recv()
                buf[s - 1, :, halves[h]] += ypart[rows, halves[h]]
                rs_copy(chain, s, slot).start()

    for c in range(4):
        lanes = pl.ds(PARTS[c], PARTS[c + 1] - PARTS[c])
        await_bytes(recv_b.at[pl.ds(0, (NM - 1) * WIDE), lanes], a2a_recv.at[c])
        ypart[lanes, :] = lax.dot_general(
            recv_b[:, lanes], recv_s[...].reshape(PW, RANK), TDOT, preferred_element_type=F32)
        rs_step(2 * c)
        rs_step(2 * c + 1)

    own = rows_of(0)
    for chain in chains:
        _, way, h, _ = chain
        rs_copy(chain, 7, (rup if way == 1 else rdn).at[7, :, halves[h]]).wait_recv()
    yall[own, :] = ypart[own, :] + rup[7] + rdn[7]

    def ag_copy(chain, s):
        name, way, h, _ = chain
        return pltpu.make_async_remote_copy(
            src_ref=yall.at[rows_of(-way * s), halves[h]], dst_ref=yall.at[rows_of(-way * (s + 1)), halves[h]],
            send_sem=ag_send.at[name, s], recv_sem=ag_recv.at[name, s],
            device_id=zup if way == 1 else zdn, device_id_type=MESH,
        )

    gcols = pl.ds(pl.multiple_of((z // 4) * 128, 128), 128)

    def use(c):
        rows = pl.ds(PARTS[c], PARTS[c + 1] - PARTS[c])
        y = yall[rows, :]
        hi = y.astype(BF16)
        lo = (y - hi.astype(F32)).astype(BF16)
        ys = yall[rows, gcols]
        shi = ys.astype(BF16)
        slo = (ys - shi.astype(F32)).astype(BF16)
        b = recv_b[:, rows]
        g = (
            lax.dot_general(shi, hi, TDOT, preferred_element_type=F32)
            + (lax.dot_general(shi, lo, TDOT, preferred_element_type=F32)
               + lax.dot_general(slo, hi, TDOT, preferred_element_type=F32))
        )
        w = jnp.dot(b, hi, preferred_element_type=F32) + jnp.dot(b, lo, preferred_element_type=F32)
        w = w.reshape(NM // 2, 2, WIDE, RANK)
        if c == 3:
            gpart[...] = g
            wpart[...] = w
        else:
            gpart[...] += g
            wpart[...] += w

    for s in range(8):
        for chain in chains:
            if s < 8 - chain[3]:
                if s:
                    ag_copy(chain, s - 1).wait_recv()
                ag_copy(chain, s).start()
        if s == 0:
            rhs_out[pl.ds(0, BLK), :] = yall[own, :]
        if s in (2, 4, 6):
            use(4 - s // 2)
    for chain in chains:
        ag_copy(chain, 7 - chain[3]).wait_recv()
    use(0)

    def tile(j):
        return gpart.at[
            pl.ds(pl.multiple_of((z % 4) * 32 + (j // 4) * 8, 8), 8), pl.ds(pl.multiple_of((j % 4) * 128, 128), 128)]

    def g_copy(k):
        peer = (m + k) % NM
        return pltpu.make_async_remote_copy(
            src_ref=tile(peer // 2), dst_ref=grecv.at[m],
            send_sem=g_send.at[k], recv_sem=g_recv.at[k], device_id=member(peer), device_id_type=MESH,
        )

    @pl.loop(1, NM)
    def _(k):
        g_copy(k).start()

    pair = pltpu.make_async_remote_copy(
        src_ref=wpart.at[:, 1 - core], dst_ref=wsib, send_sem=pair_send, recv_sem=pair_recv,
        device_id=sibling, device_id_type=MESH)
    pair.start()
    own_g = pltpu.make_async_copy(tile(chip), grecv.at[m], local_sem.at[2])
    own_g.start()
    own_g.wait()

    @pl.loop(1, NM)
    def _(k):
        g_copy(k).wait()

    gz[z] = jnp.sum(grecv[...], axis=0)

    def gz_copy(k):
        return pltpu.make_async_remote_copy(
            src_ref=gz.at[z], dst_ref=gz.at[z], send_sem=gz_send.at[k], recv_sem=gz_recv.at[k],
            device_id=at_z((z + k) % NZ), device_id_type=MESH,
        )

    def gz_arrived(k):
        piece = gz.at[mod(z - k, NZ)]
        pltpu.make_async_remote_copy(
            src_ref=piece, dst_ref=piece, send_sem=gz_send.at[k], recv_sem=gz_recv.at[k],
            device_id=at_z((z + k) % NZ), device_id_type=MESH,
        ).wait_recv()

    @pl.loop(1, NZ)
    def _(k):
        gz_copy(k).start()

    pair.wait()
    wsib[...] += wpart[:, core]

    def w_copy(k):
        peer = (chip + k) % (NM // 2)
        return pltpu.make_async_remote_copy(
            src_ref=wsib.at[peer], dst_ref=wrecv.at[chip],
            send_sem=w_send.at[k], recv_sem=w_recv.at[k], device_id=member(peer * 2 + core), device_id_type=MESH,
        )

    @pl.loop(1, NZ)
    def _(k):
        gz_arrived(k)

    half = pl.ds(core * (NZ // 2), NZ // 2)

    def gp_copy(k):
        peer = (chip + k) % (NM // 2)
        return pltpu.make_async_remote_copy(
            src_ref=gz.at[half], dst_ref=gall_out.at[chip, half],
            send_sem=gp_send.at[k], recv_sem=gp_recv.at[k],
            device_id=member(peer * 2 + core), device_id_type=MESH,
        )

    @pl.loop(1, NM // 2)
    def _(k):
        gp_copy(k).start()

    @pl.loop(1, NM // 2)
    def _(k):
        w_copy(k).start()

    gall_out[chip] = gz[...]
    wrecv[chip] = wsib[chip]

    def gs_copy(k):
        piece = gall_out.at[mod(chip - k, NM // 2), half]
        return pltpu.make_async_remote_copy(
            src_ref=piece, dst_ref=piece, send_sem=gs_send.at[k], recv_sem=gs_recv.at[k],
            device_id=sibling, device_id_type=MESH,
        )

    def gs_arrived(k):
        piece = gall_out.at[mod(chip - k, NM // 2), pl.ds((1 - core) * (NZ // 2), NZ // 2)]
        pltpu.make_async_remote_copy(
            src_ref=piece, dst_ref=piece, send_sem=gs_send.at[k], recv_sem=gs_recv.at[k],
            device_id=sibling, device_id_type=MESH,
        ).wait_recv()

    @pl.loop(1, NM // 2)
    def _(k):
        gp_copy(k).wait()
        gs_copy(k).start()

    @pl.loop(1, NM // 2)
    def _(k):
        gs_arrived(k)

    @pl.loop(1, NM // 2)
    def _(k):
        w_copy(k).wait()

    rhs_out[pl.ds(BLK, WIDE), :] = jnp.sum(wrecv[...], axis=0)

    @pl.loop(1, NM // 2)
    def _(k):
        gs_copy(k).wait_send()

    @pl.loop(1, NZ)
    def _(k):
        gz_copy(k).wait_send()

    for c in range(4):
        await_bytes(recv_b.at[pl.ds(0, (NM - 1) * WIDE), pl.ds(PARTS[c], PARTS[c + 1] - PARTS[c])], a2a_send.at[c])
    for chain in chains:
        _, way, h, first = chain
        for s in range(first, 8):
            rs_copy(chain, s, (rup if way == 1 else rdn).at[s, :, halves[h]]).wait_send()
        for s in range(0, 8 - first):
            ag_copy(chain, s).wait_send()


def exchange(grad_buckets, sketch):
    vmem = pl.BlockSpec(memory_space=pltpu.VMEM)
    dma = pltpu.SemaphoreType.DMA
    return pl.pallas_call(
        comm_kernel,
        out_shape=(
            jax.ShapeDtypeStruct((NM // 2, NZ, 8, 128), F32),
            jax.ShapeDtypeStruct((BLK + WIDE, RANK), F32),
        ),
        in_specs=[vmem, pl.BlockSpec(memory_space=pl.ANY)],
        out_specs=(vmem, vmem),
        scratch_shapes=[
            pltpu.VMEM((NM, WIDE, COLS), BF16),
            pltpu.VMEM((PW, COLS), BF16),
            pltpu.VMEM((NX, NT, WIDE, RANK), BF16),
            pltpu.VMEM((COLS, RANK), F32),
            pltpu.VMEM((COLS, RANK), F32),
            pltpu.VMEM((8, BLK, RANK), F32),
            pltpu.VMEM((8, BLK, RANK), F32),
            pltpu.VMEM((NM // 2, 2, WIDE, RANK), F32),
            pltpu.VMEM((NM // 2, WIDE, RANK), F32),
            pltpu.VMEM((NM // 2, WIDE, RANK), F32),
            pltpu.VMEM((128, RANK), F32),
            pltpu.VMEM((NM, 8, 128), F32),
            pltpu.VMEM((NZ, 8, 128), F32),
            dma((3,)),
            dma((4,)), dma((4,)),
            dma((NT,)), dma((NT,)),
            dma((4, 8)), dma((4, 8)),
            dma((4, 8)), dma((4, 8)),
            dma((NM,)), dma((NM,)),
            dma, dma,
            dma((NM // 2,)), dma((NM // 2,)),
            dma((NZ,)), dma((NZ,)),
            dma((NM // 2,)), dma((NM // 2,)),
            dma((NM // 2,)), dma((NM // 2,)),
        ],
        compiler_params=pltpu.CompilerParams(
            collective_id=0, has_side_effects=True, vmem_limit_bytes=48 * 1024 * 1024),
    )(grad_buckets, sketch)


def invert_factor(work):
    for s in range(0, NB, GROUP):
        n = NB - s
        row = lax.broadcasted_iota(jnp.int32, (GROUP, NB), 0)
        lane = lax.broadcasted_iota(jnp.int32, (GROUP, NB), 1)
        rest = work[s:, :]
        cols = [jnp.broadcast_to(rest[:, s + k : s + k + 1], (n, NB)) for k in range(GROUP)]
        top = jnp.where((lane >= s) & (lane < s + GROUP), jnp.where(lane - s == row, 1.0, 0.0), rest[:GROUP])
        below = rest[GROUP:]
        if n > GROUP:
            lane_b = lax.broadcasted_iota(jnp.int32, (n - GROUP, NB), 1)
            below = jnp.where((lane_b >= s) & (lane_b < s + GROUP), 0.0, below)
        for k in range(GROUP):
            r = lax.rsqrt(jnp.broadcast_to(cols[k][k : k + 1], (GROUP, NB)))
            mult = cols[k] * jnp.broadcast_to(r[:1], (n, NB))
            for q in range(k + 1, GROUP):
                cols[q] = cols[q] - mult * jnp.broadcast_to(mult[q : q + 1], (n, NB))
            u = jnp.broadcast_to(top[k : k + 1], (GROUP, NB)) * r
            top = jnp.where(row == k, u, jnp.where(row > k, top - mult[:GROUP] * u, top))
            if n > GROUP:
                below = below - mult[GROUP:] * jnp.broadcast_to(u[:1], (n - GROUP, NB))
        work[s : s + GROUP, :] = top
        if n > GROUP:
            work[s + GROUP :, :] = below


def finish_kernel(gall, rhs, basis_out, proj_out, mat, work, solved, outbox, inbox, sends, recvs):
    dp = lax.axis_index("dp")
    t = lax.axis_index("tensor")

    barrier = pltpu.get_barrier_semaphore()

    @pl.loop(1, N_DP)
    def _(k):
        pl.semaphore_signal(barrier, inc=1, device_id=((dp + k) % N_DP, t), device_id_type=MESH)

    @pl.loop(0, NZ)
    def _(z):
        for j in range(NM // 2):
            mat[pl.ds(pl.multiple_of(z * 32 + (j // 4) * 8, 8), 8), pl.ds((j % 4) * 128, 128)] = gall[j, z]

    mat[:, RANK:] = rhs[...].T

    @pl.loop(0, RANK // NB)
    def _(j):
        rows = pl.ds(pl.multiple_of(j * NB, NB), NB)
        work[...] = mat[rows, rows]
        invert_factor(work)
        row = lax.broadcasted_iota(jnp.int32, (NB, NB), 0)
        lane = lax.broadcasted_iota(jnp.int32, (NB, NB), 1)
        inverse = jnp.where(lane <= row, work[...], 0.0)
        upper = jnp.dot(inverse, mat[rows, :], precision=HIGHEST, preferred_element_type=F32)
        solved[rows, :] = upper[:, RANK:]
        for i in range(1, RANK // NB):
            @pl.when(i > j)
            def _():
                mat[i * NB : (i + 1) * NB, :] -= lax.dot_general(
                    upper[:, i * NB : (i + 1) * NB], upper, TDOT, precision=HIGHEST, preferred_element_type=F32)

    packed = jnp.zeros((N_DP, NB), F32)
    lane = lax.broadcasted_iota(jnp.int32, (N_DP, NB), 1)
    for r in range(PER_DP):
        part = solved[pl.ds(r, N_DP, stride=PER_DP), :]
        slot = PER_DP - 1 - r
        packed = jnp.where(lane // WIDE == slot, pltpu.roll(part, (WIDE * slot - BLK) % NB, 1), packed)
    outbox[...] = packed.reshape(N_DP, 1, NB)

    pl.semaphore_wait(barrier, N_DP - 1)

    def copy(k):
        peer = (dp + k) % N_DP
        return pltpu.make_async_remote_copy(
            src_ref=outbox.at[peer], dst_ref=inbox.at[dp], send_sem=sends.at[k], recv_sem=recvs.at[k],
            device_id=(peer, t), device_id_type=MESH,
        )

    @pl.loop(1, N_DP)
    def _(k):
        copy(k).start()

    inbox[dp] = outbox[dp]
    basis_out[...] = (solved[:, :BLK] * math.sqrt(ROWS)).astype(BF16)

    @pl.loop(1, N_DP)
    def _(k):
        copy(k).wait()

    per_tile = NB // WIDE
    lane = lax.broadcasted_iota(jnp.int32, (PER_DP, NB), 1)
    for q in range(N_DP // per_tile):
        tile = jnp.zeros((PER_DP, NB), F32)
        for i in range(per_tile):
            line = jnp.broadcast_to(inbox[q * per_tile + i], (PER_DP, NB))
            line = pltpu.roll(line, 0, 1, stride=WIDE, stride_axis=0)
            line = pltpu.roll(line, (WIDE * (i + 1)) % NB, 1)
            tile = jnp.where(lane // WIDE == i, line, tile)
        proj_out[:, q * NB : (q + 1) * NB] = tile.astype(BF16)


def finish(gall, rhs):
    vmem = pl.BlockSpec(memory_space=pltpu.VMEM)
    return pl.pallas_call(
        finish_kernel,
        out_shape=(
            jax.ShapeDtypeStruct((RANK, BLK), BF16),
            jax.ShapeDtypeStruct((PER_DP, N_DP * WIDE), BF16),
        ),
        in_specs=[vmem, vmem],
        out_specs=(vmem, vmem),
        scratch_shapes=[
            pltpu.VMEM((RANK, RANK + NB), F32),
            pltpu.VMEM((NB, NB), F32),
            pltpu.VMEM((RANK, NB), F32),
            pltpu.VMEM((N_DP, 1, NB), F32),
            pltpu.VMEM((N_DP, 1, NB), F32),
            pltpu.SemaphoreType.DMA((N_DP,)),
            pltpu.SemaphoreType.DMA((N_DP,)),
        ],
        compiler_params=pltpu.CompilerParams(
            collective_id=1, has_side_effects=True, vmem_limit_bytes=32 * 1024 * 1024),
    )(gall, rhs)


def shards(grad_buckets, sketch):
    return finish(*exchange(grad_buckets, sketch.reshape(NZ, NX, WIDE, RANK)))


def solution(mesh):
    in_specs = (P(("tensor", "dp"), None), P("tensor", None))
    out_specs = (P(None, ("dp", "tensor")), P("dp", "tensor"))
    return jax.shard_map(shards, mesh=mesh, in_specs=in_specs, out_specs=out_specs, check_vma=False)
```

```python
import math

import jax
import jax.numpy as jnp
from jax import lax
from jax.experimental import pallas as pl
from jax.experimental.pallas import tpu as pltpu
from jax.sharding import PartitionSpec as P

MESH = pl.DeviceIdType.MESH
F32 = jnp.float32
BF16 = jnp.bfloat16
NZ, NX, NT = 16, 4, 8
NM = NX * NT
NCHIP = NM // 2
ROWS = 57344
RANK = 512
WIDE = 16
BLK = ROWS // (NZ * NM)
COLS = BLK * NZ
PW = WIDE * NM
HALF = RANK // 2
PARTS = (0, 384, 896, 1280, 1792)
N_DP = NZ * NX
PER_DP = RANK // N_DP
NB = 128
GROUP = 8
HIGHEST = lax.Precision.HIGHEST
TDOT = (((0,), (0,)), ((), ()))


def mod(a, n):
    return lax.rem(a + n, n)


def near(k):
    if k == 0:
        return NZ - 1
    if abs(k) == NZ // 2:
        return 0
    return NZ - 1 - 2 * k if k > 0 else NZ + 2 * k


ORDER = sorted(range(1 - NZ // 2, NZ // 2 + 1), key=near)


def await_bytes(ref, sem):
    pltpu.make_async_copy(ref, ref, sem).wait()


def invert_factor(work):
    for s in range(0, NB, GROUP):
        n = NB - s
        row = lax.broadcasted_iota(jnp.int32, (GROUP, NB), 0)
        lane = lax.broadcasted_iota(jnp.int32, (GROUP, NB), 1)
        rest = work[s:, :]
        cols = [jnp.broadcast_to(rest[:, s + k : s + k + 1], (n, NB)) for k in range(GROUP)]
        top = jnp.where((lane >= s) & (lane < s + GROUP), jnp.where(lane - s == row, 1.0, 0.0), rest[:GROUP])
        below = rest[GROUP:]
        if n > GROUP:
            lane_b = lax.broadcasted_iota(jnp.int32, (n - GROUP, NB), 1)
            below = jnp.where((lane_b >= s) & (lane_b < s + GROUP), 0.0, below)
        for k in range(GROUP):
            r = lax.rsqrt(jnp.broadcast_to(cols[k][k : k + 1], (GROUP, NB)))
            mult = cols[k] * jnp.broadcast_to(r[:1], (n, NB))
            for q in range(k + 1, GROUP):
                cols[q] = cols[q] - mult * jnp.broadcast_to(mult[q : q + 1], (n, NB))
            u = jnp.broadcast_to(top[k : k + 1], (GROUP, NB)) * r
            top = jnp.where(row == k, u, jnp.where(row > k, top - mult[:GROUP] * u, top))
            if n > GROUP:
                below = below - mult[GROUP:] * jnp.broadcast_to(u[:1], (n - GROUP, NB))
        work[s : s + GROUP, :] = top
        if n > GROUP:
            work[s + GROUP :, :] = below


def kernel(
    grad, sketch, basis_out, proj_out,
    packed, recv_b, recv_s, ypart, yall, rup, rdn, wpart, wsib, wrecv,
    gown, gsib, grecv, gzs, gzr, gza, gall, rhs, mat, work, inverses, solved, outbox, inbox_x, inbox_z,
    local_sem, a2a_send, a2a_recv, s_send, s_recv, rs_send, rs_recv, ag_send, ag_recv,
    pair_send, pair_recv, w_send, w_recv, g_send, g_recv, gzs_send, gzs_recv, gza_send, gza_recv,
    gp_send, gp_recv, gs_send, gs_recv, x_send, x_recv, z_send, z_recv,
):
    dp = lax.axis_index("dp")
    t = lax.axis_index("tensor")
    z = dp // NX
    x = dp % NX
    m = x * NT + t
    chip = m // 2
    core = m % 2

    def member(i):
        return (z * NX + i // NT, i % NT)

    def at_z(i):
        return (i * NX + x, t)

    zup, zdn = at_z(mod(z + 1, NZ)), at_z(mod(z - 1, NZ))
    sibling = (dp, t + 1 - 2 * core)

    barrier = pltpu.get_barrier_semaphore()

    @pl.loop(1, NM)
    def _(k):
        pl.semaphore_signal(barrier, inc=1, device_id=member((m + k) % NM), device_id_type=MESH)

    @pl.loop(1, NZ)
    def _(k):
        pl.semaphore_signal(barrier, inc=1, device_id=at_z((z + k) % NZ), device_id_type=MESH)

    mine = pl.ds(pl.multiple_of(m * WIDE, WIDE), WIDE)

    def pack(c):
        @pl.loop(0, NM // 8)
        def _(q):
            for place in range(4 * c, 4 * c + 4):
                first = ((z + ORDER[place] + NZ) % NZ) * (NM * BLK) + q * (8 * BLK)
                part = grad[:, pl.ds(pl.multiple_of(first, 128), 8 * BLK)]
                for i in range(8):
                    packed[q * 8 + i, :, place * BLK : (place + 1) * BLK] = part[:, i * BLK : (i + 1) * BLK]

    def b_copy(c, k):
        peer = (m + k) % NM
        lanes = pl.ds(PARTS[c], PARTS[c + 1] - PARTS[c])
        return pltpu.make_async_remote_copy(
            src_ref=packed.at[peer, :, lanes], dst_ref=recv_b.at[mine, lanes],
            send_sem=a2a_send.at[c], recv_sem=a2a_recv.at[c], device_id=member(peer), device_id_type=MESH,
        )

    def s_copy(k):
        peer = (t + k) % NT
        return pltpu.make_async_remote_copy(
            src_ref=sketch.at[z], dst_ref=recv_s.at[:, t],
            send_sem=s_send.at[k], recv_sem=s_recv.at[k], device_id=(dp, peer), device_id_type=MESH,
        )

    own_s = pltpu.make_async_copy(sketch.at[z], recv_s.at[:, t], local_sem.at[0])
    own_s.start()

    def send(c):
        @pl.loop(1, NM)
        def _(k):
            b_copy(c, k).start()

    pack(0)
    pl.semaphore_wait(barrier, NM - 1 + NZ - 1)

    @pl.loop(1, NT)
    def _(k):
        s_copy(k).start()

    send(0)
    pack(1)
    send(1)
    pack(2)
    pack(3)

    own_b = pltpu.make_async_copy(packed.at[m], recv_b.at[mine], local_sem.at[1])
    own_b.start()
    own_b.wait()
    own_s.wait()

    @pl.loop(1, NT)
    def _(k):
        s_copy(k).wait()

    def rows_of(k):
        return pl.ds(near(k) * BLK, BLK)

    halves = (pl.ds(0, HALF), pl.ds(HALF, HALF))
    chains = ((0, 1, 0, 0), (1, -1, 1, 0), (2, 1, 1, 1), (3, -1, 0, 1))

    def rs_copy(chain, s, src):
        name, way, h, _ = chain
        buf = rup if way == 1 else rdn
        return pltpu.make_async_remote_copy(
            src_ref=src, dst_ref=buf.at[s, :, halves[h]],
            send_sem=rs_send.at[name, s], recv_sem=rs_recv.at[name, s],
            device_id=zup if way == 1 else zdn, device_id_type=MESH,
        )

    def rs_step(s):
        for chain in chains:
            _, way, h, first = chain
            rows = rows_of(way * (8 - s))
            if s == first:
                rs_copy(chain, s, ypart.at[rows, halves[h]]).start()
            elif s > first:
                buf = rup if way == 1 else rdn
                slot = buf.at[s - 1, :, halves[h]]
                rs_copy(chain, s - 1, slot).wait_recv()
                buf[s - 1, :, halves[h]] += ypart[rows, halves[h]]
                rs_copy(chain, s, slot).start()

    for c in range(4):
        lanes = pl.ds(PARTS[c], PARTS[c + 1] - PARTS[c])
        await_bytes(recv_b.at[pl.ds(0, (NM - 1) * WIDE), lanes], a2a_recv.at[c])
        ypart[lanes, :] = lax.dot_general(
            recv_b[:, lanes], recv_s[...].reshape(PW, RANK), TDOT, preferred_element_type=F32)
        rs_step(2 * c)
        if c < 2:
            send(c + 2)
        rs_step(2 * c + 1)

    own = rows_of(0)
    for chain in chains:
        _, way, h, _ = chain
        rs_copy(chain, 7, (rup if way == 1 else rdn).at[7, :, halves[h]]).wait_recv()
    yall[own, :] = ypart[own, :] + rup[7] + rdn[7]

    def ag_copy(chain, s):
        name, way, h, _ = chain
        return pltpu.make_async_remote_copy(
            src_ref=yall.at[rows_of(-way * s), halves[h]], dst_ref=yall.at[rows_of(-way * (s + 1)), halves[h]],
            send_sem=ag_send.at[name, s], recv_sem=ag_recv.at[name, s],
            device_id=zup if way == 1 else zdn, device_id_type=MESH,
        )

    def use(c):
        rows = pl.ds(PARTS[c], PARTS[c + 1] - PARTS[c])
        y = yall[rows, :]
        hi = y.astype(BF16)
        lo = (y - hi.astype(F32)).astype(BF16)
        b = recv_b[:, rows]
        w = jnp.dot(b, hi, preferred_element_type=F32) + jnp.dot(b, lo, preferred_element_type=F32)
        w = w.reshape(NCHIP, 2, WIDE, RANK)
        if c == 3:
            wpart[...] = w
        else:
            wpart[...] += w

    def to_sibling(src, dst, send_sem, recv_sem):
        return pltpu.make_async_remote_copy(
            src_ref=src, dst_ref=dst, send_sem=send_sem, recv_sem=recv_sem, device_id=sibling, device_id_type=MESH)

    g_pair = to_sibling(gown.at[1 - core], gsib, pair_send.at[0], pair_recv.at[0])
    w_pair = to_sibling(wpart.at[:, 1 - core], wsib, pair_send.at[1], pair_recv.at[1])

    def plane_copy(k, src, dst, send_sem, recv_sem):
        return pltpu.make_async_remote_copy(
            src_ref=src, dst_ref=dst, send_sem=send_sem, recv_sem=recv_sem,
            device_id=member(((chip + k) % NCHIP) * 2 + core), device_id_type=MESH)

    def z_copy(k, src, dst, send_sem, recv_sem):
        return pltpu.make_async_remote_copy(
            src_ref=src, dst_ref=dst, send_sem=send_sem, recv_sem=recv_sem,
            device_id=at_z((z + k) % NZ), device_id_type=MESH)

    def gram_1():
        y = yall[own, :]
        rhs[pl.ds(0, BLK), :] = y
        rhs[pl.ds(BLK, WIDE), :] = jnp.zeros((WIDE, RANK), F32)
        gram = lax.dot_general(y, y, TDOT, precision=HIGHEST, preferred_element_type=F32)
        gown[...] = gram.reshape(2, NCHIP, NZ, RANK)
        g_pair.start()

    def gram_2():
        g_pair.wait()
        gsib[...] += gown[core]

        @pl.loop(1, NCHIP)
        def _(k):
            plane_copy(k, gsib.at[(chip + k) % NCHIP], grecv.at[chip], g_send, g_recv).start()

        grecv[chip] = gsib[chip]

    def gram_3():
        await_bytes(grecv.at[pl.ds(0, NCHIP - 1)], g_recv)
        gzs[...] = jnp.sum(grecv[...], axis=0).reshape(NZ, 1, RANK)

        @pl.loop(1, NZ)
        def _(k):
            z_copy(k, gzs.at[(z + k) % NZ], gzr.at[z], gzs_send, gzs_recv).start()

        gzr[z] = gzs[z]

    def gram_4():
        await_bytes(gzr.at[pl.ds(0, NZ - 1)], gzs_recv)
        gza[z] = jnp.sum(gzr[...], axis=0)

        @pl.loop(1, NZ)
        def _(k):
            z_copy(k, gza.at[z], gza.at[z], gza_send, gza_recv).start()

    def gp_copy(k):
        piece = gall.at[core, chip]
        return plane_copy(k, piece, piece, gp_send.at[k], gp_recv.at[k])

    def gs_copy(k):
        piece = gall.at[core, mod(chip - k, NCHIP)]
        return to_sibling(piece, piece, gs_send.at[k], gs_recv.at[k])

    def gram_5():
        await_bytes(gza.at[pl.ds(0, NZ - 1)], gza_recv)
        gall[core, chip] = gza[...].reshape(NZ, RANK)

        @pl.loop(1, NCHIP)
        def _(k):
            gp_copy(k).start()

        gs_copy(0).start()

    def gram_6():
        @pl.loop(1, NCHIP)
        def _(k):
            piece = gall.at[core, mod(chip - k, NCHIP)]
            plane_copy(k, piece, piece, gp_send.at[k], gp_recv.at[k]).wait_recv()
            gs_copy(k).start()

    def gram_7():
        @pl.loop(0, NCHIP)
        def _(k):
            piece = gall.at[1 - core, mod(chip - k, NCHIP)]
            to_sibling(piece, piece, gs_send.at[k], gs_recv.at[k]).wait_recv()

    beside = (gram_1, gram_2, lambda: use(3), gram_3, gram_4, lambda: use(2), gram_5, lambda: use(1))

    for s in range(8):
        for chain in chains:
            if s < 8 - chain[3]:
                if s:
                    ag_copy(chain, s - 1).wait_recv()
                ag_copy(chain, s).start()
        beside[s]()
    for chain in chains:
        ag_copy(chain, 7 - chain[3]).wait_recv()
    use(0)
    w_pair.start()
    gram_6()
    gram_7()

    def w_send_off():
        w_pair.wait()
        wsib[...] += wpart[:, core]

        @pl.loop(1, NCHIP)
        def _(k):
            plane_copy(k, wsib.at[(chip + k) % NCHIP], wrecv.at[chip], w_send, w_recv).start()

        wrecv[chip] = wsib[chip]

    def below(i):
        return pl.ds(i * NB, NB)

    def w_catch_up(steps):
        await_bytes(wrecv.at[pl.ds(0, NCHIP - 1)], w_recv)
        w = jnp.concatenate([jnp.zeros((BLK, RANK), F32), jnp.sum(wrecv[...], axis=0)], axis=0).T
        for j in range(steps):
            part = jnp.dot(inverses[j], w[:NB], precision=HIGHEST, preferred_element_type=F32)
            solved[below(j), :] += part
            w = w[NB:] - lax.dot_general(
                mat[below(j), (j + 1) * NB : RANK], part, TDOT, precision=HIGHEST, preferred_element_type=F32)
        mat[steps * NB :, RANK:] += w

    mat[:, :RANK] = gall[...].reshape(RANK, RANK)
    mat[:, RANK:] = rhs[...].T

    @pl.loop(0, RANK // NB)
    def _(j):
        rows = pl.ds(pl.multiple_of(j * NB, NB), NB)
        work[...] = mat[rows, rows]
        invert_factor(work)

        @pl.when(j == 0)
        def _():
            w_send_off()

        @pl.when(j == 2)
        def _():
            w_catch_up(2)

        row = lax.broadcasted_iota(jnp.int32, (NB, NB), 0)
        lane = lax.broadcasted_iota(jnp.int32, (NB, NB), 1)
        inverse = jnp.where(lane <= row, work[...], 0.0)
        inverses[j] = inverse
        upper = jnp.dot(inverse, mat[rows, :], precision=HIGHEST, preferred_element_type=F32)
        mat[rows, :] = upper
        solved[rows, :] = upper[:, RANK:]
        for i in range(1, RANK // NB):
            @pl.when(i > j)
            def _():
                mat[below(i), :] -= lax.dot_general(
                    upper[:, i * NB : (i + 1) * NB], upper, TDOT, precision=HIGHEST, preferred_element_type=F32)

    packed_p = jnp.zeros((N_DP, NB), F32)
    lane = lax.broadcasted_iota(jnp.int32, (N_DP, NB), 1)
    for r in range(PER_DP):
        part = solved[pl.ds(r, N_DP, stride=PER_DP), :]
        slot = PER_DP - 1 - r
        packed_p = jnp.where(lane // WIDE == slot, pltpu.roll(part, (WIDE * slot - BLK) % NB, 1), packed_p)
    outbox[...] = packed_p.reshape(NZ, NX, 1, NB)

    def x_copy(k):
        peer = (x + k) % NX
        return pltpu.make_async_remote_copy(
            src_ref=outbox.at[:, peer], dst_ref=inbox_x.at[x], send_sem=x_send.at[k], recv_sem=x_recv.at[k],
            device_id=(z * NX + peer, t), device_id_type=MESH,
        )

    for k in range(1, NX):
        x_copy(k).start()
    inbox_x[x] = outbox[:, x]
    basis_out[...] = (solved[:, :BLK] * math.sqrt(ROWS)).astype(BF16)
    for k in range(1, NX):
        x_copy(k).wait()

    @pl.loop(1, NZ)
    def _(k):
        z_copy(k, inbox_x.at[:, (z + k) % NZ], inbox_z.at[z], z_send, z_recv).start()

    inbox_z[z] = inbox_x[:, z]

    for ref, sem in (
        (grecv.at[pl.ds(0, NCHIP - 1)], g_send), (wrecv.at[pl.ds(0, NCHIP - 1)], w_send),
        (gzr.at[pl.ds(0, NZ - 1)], gzs_send), (gza.at[pl.ds(0, NZ - 1)], gza_send),
    ):
        await_bytes(ref, sem)

    @pl.loop(0, NCHIP)
    def _(k):
        gs_copy(k).wait_send()

    @pl.loop(1, NCHIP)
    def _(k):
        gp_copy(k).wait_send()

    for c in range(4):
        await_bytes(recv_b.at[pl.ds(0, (NM - 1) * WIDE), pl.ds(PARTS[c], PARTS[c + 1] - PARTS[c])], a2a_send.at[c])
    for chain in chains:
        _, way, h, first = chain
        for s in range(first, 8):
            rs_copy(chain, s, (rup if way == 1 else rdn).at[s, :, halves[h]]).wait_send()
        for s in range(0, 8 - first):
            ag_copy(chain, s).wait_send()

    await_bytes(inbox_z.at[pl.ds(0, NZ - 1)], z_send)
    await_bytes(inbox_z.at[pl.ds(0, NZ - 1)], z_recv)
    per_tile = NB // WIDE
    lane = lax.broadcasted_iota(jnp.int32, (PER_DP, NB), 1)
    for q in range(N_DP // per_tile):
        tile = jnp.zeros((PER_DP, NB), F32)
        for i in range(per_tile):
            src = q * per_tile + i
            line = jnp.broadcast_to(inbox_z[src // NX, src % NX], (PER_DP, NB))
            line = pltpu.roll(line, 0, 1, stride=WIDE, stride_axis=0)
            line = pltpu.roll(line, (WIDE * (i + 1)) % NB, 1)
            tile = jnp.where(lane // WIDE == i, line, tile)
        proj_out[:, q * NB : (q + 1) * NB] = tile.astype(BF16)


def project(grad_buckets, sketch):
    vmem = pl.BlockSpec(memory_space=pltpu.VMEM)
    dma = pltpu.SemaphoreType.DMA
    return pl.pallas_call(
        kernel,
        out_shape=(
            jax.ShapeDtypeStruct((RANK, BLK), BF16),
            jax.ShapeDtypeStruct((PER_DP, N_DP * WIDE), BF16),
        ),
        in_specs=[vmem, pl.BlockSpec(memory_space=pl.ANY)],
        out_specs=(vmem, vmem),
        scratch_shapes=[
            pltpu.VMEM((NM, WIDE, COLS), BF16),
            pltpu.VMEM((PW, COLS), BF16),
            pltpu.VMEM((NX, NT, WIDE, RANK), BF16),
            pltpu.VMEM((COLS, RANK), F32),
            pltpu.VMEM((COLS, RANK), F32),
            pltpu.VMEM((8, BLK, RANK), F32),
            pltpu.VMEM((8, BLK, RANK), F32),
            pltpu.VMEM((NCHIP, 2, WIDE, RANK), F32),
            pltpu.VMEM((NCHIP, WIDE, RANK), F32),
            pltpu.VMEM((NCHIP, WIDE, RANK), F32),
            pltpu.VMEM((2, NCHIP, NZ, RANK), F32),
            pltpu.VMEM((NCHIP, NZ, RANK), F32),
            pltpu.VMEM((NCHIP, NZ, RANK), F32),
            pltpu.VMEM((NZ, 1, RANK), F32),
            pltpu.VMEM((NZ, 1, RANK), F32),
            pltpu.VMEM((NZ, 1, RANK), F32),
            pltpu.VMEM((2, NCHIP, NZ, RANK), F32),
            pltpu.VMEM((BLK + WIDE, RANK), F32),
            pltpu.VMEM((RANK, RANK + NB), F32),
            pltpu.VMEM((NB, NB), F32),
            pltpu.VMEM((RANK // NB, NB, NB), F32),
            pltpu.VMEM((RANK, NB), F32),
            pltpu.VMEM((NZ, NX, 1, NB), F32),
            pltpu.VMEM((NX, NZ, 1, NB), F32),
            pltpu.VMEM((NZ, NX, 1, NB), F32),
            dma((2,)),
            dma((4,)), dma((4,)),
            dma((NT,)), dma((NT,)),
            dma((4, 8)), dma((4, 8)),
            dma((4, 8)), dma((4, 8)),
            dma((2,)), dma((2,)),
            dma, dma, dma, dma, dma, dma, dma, dma,
            dma((NCHIP,)), dma((NCHIP,)),
            dma((NCHIP,)), dma((NCHIP,)),
            dma((NX,)), dma((NX,)),
            dma, dma,
        ],
        compiler_params=pltpu.CompilerParams(
            collective_id=0, has_side_effects=True, vmem_limit_bytes=56 * 1024 * 1024),
    )(grad_buckets, sketch)


def shards(grad_buckets, sketch):
    return project(grad_buckets, sketch.reshape(NZ, NX, WIDE, RANK))


def solution(mesh):
    in_specs = (P(("tensor", "dp"), None), P("tensor", None))
    out_specs = (P(None, ("dp", "tensor")), P("dp", "tensor"))
    return jax.shard_map(shards, mesh=mesh, in_specs=in_specs, out_specs=out_specs, check_vma=False)
```

```python
import math

import jax
import jax.numpy as jnp
from jax import lax
from jax.experimental import pallas as pl
from jax.experimental.pallas import tpu as pltpu
from jax.sharding import PartitionSpec as P

MESH = pl.DeviceIdType.MESH
F32 = jnp.float32
BF16 = jnp.bfloat16
NZ, NX, NT = 16, 4, 8
NM = NX * NT
NCHIP = NM // 2
ROWS = 57344
RANK = 512
WIDE = 16
BLK = ROWS // (NZ * NM)
COLS = BLK * NZ
PW = WIDE * NM
HALF = RANK // 2
PARTS = (0, 128, 384, 896, 1280, 1792)
STEPS = ((0,), (1,), (2, 3), (4, 5), (6, 7))
USES = (0, 384, 896, 1280, 1792)
N_DP = NZ * NX
PER_DP = RANK // N_DP
NB = 128
GROUP = 8
HIGHEST = lax.Precision.HIGHEST
TDOT = (((0,), (0,)), ((), ()))


def mod(a, n):
    return lax.rem(a + n, n)


def near(k):
    if k == 0:
        return NZ - 1
    if abs(k) == NZ // 2:
        return 0
    return NZ - 1 - 2 * k if k > 0 else NZ + 2 * k


ORDER = sorted(range(1 - NZ // 2, NZ // 2 + 1), key=near)


def await_bytes(ref, sem):
    pltpu.make_async_copy(ref, ref, sem).wait()


def invert_factor(work, halfway):
    for s in range(0, NB, GROUP):
        if s == NB // 2:
            halfway()
        n = NB - s
        row = lax.broadcasted_iota(jnp.int32, (GROUP, NB), 0)
        lane = lax.broadcasted_iota(jnp.int32, (GROUP, NB), 1)
        rest = work[s:, :]
        cols = [jnp.broadcast_to(rest[:, s + k : s + k + 1], (n, NB)) for k in range(GROUP)]
        top = jnp.where((lane >= s) & (lane < s + GROUP), jnp.where(lane - s == row, 1.0, 0.0), rest[:GROUP])
        below = rest[GROUP:]
        if n > GROUP:
            lane_b = lax.broadcasted_iota(jnp.int32, (n - GROUP, NB), 1)
            below = jnp.where((lane_b >= s) & (lane_b < s + GROUP), 0.0, below)
        for k in range(GROUP):
            r = lax.rsqrt(jnp.broadcast_to(cols[k][k : k + 1], (GROUP, NB)))
            mult = cols[k] * jnp.broadcast_to(r[:1], (n, NB))
            for q in range(k + 1, GROUP):
                cols[q] = cols[q] - mult * jnp.broadcast_to(mult[q : q + 1], (n, NB))
            u = jnp.broadcast_to(top[k : k + 1], (GROUP, NB)) * r
            top = jnp.where(row == k, u, jnp.where(row > k, top - mult[:GROUP] * u, top))
            if n > GROUP:
                below = below - mult[GROUP:] * jnp.broadcast_to(u[:1], (n - GROUP, NB))
        work[s : s + GROUP, :] = top
        if n > GROUP:
            work[s + GROUP :, :] = below


def kernel(
    grad, sketch, basis_out, proj_out,
    packed, recv_b, recv_s, ypart, yall, rup, rdn, wpart, wsib, wrecv,
    gown, gsib, grecv, gzs, gzr, gza, gall, rhs, mat, work, inverses, solved, outbox, inbox_x, inbox_z,
    local_sem, a2a_send, a2a_recv, s_send, s_recv, rs_send, rs_recv, ag_send, ag_recv,
    pair_send, pair_recv, w_send, w_recv, g_send, g_recv, gzs_send, gzs_recv, gza_send, gza_recv,
    gp_send, gp_recv, gs_send, gs_recv, x_send, x_recv, z_send, z_recv,
):
    dp = lax.axis_index("dp")
    t = lax.axis_index("tensor")
    z = dp // NX
    x = dp % NX
    m = x * NT + t
    chip = m // 2
    core = m % 2

    def member(i):
        return (z * NX + i // NT, i % NT)

    def at_z(i):
        return (i * NX + x, t)

    zup, zdn = at_z(mod(z + 1, NZ)), at_z(mod(z - 1, NZ))
    sibling = (dp, t + 1 - 2 * core)

    barrier = pltpu.get_barrier_semaphore()

    @pl.loop(1, NM)
    def _(k):
        pl.semaphore_signal(barrier, inc=1, device_id=member((m + k) % NM), device_id_type=MESH)

    @pl.loop(1, NZ)
    def _(k):
        pl.semaphore_signal(barrier, inc=1, device_id=at_z((z + k) % NZ), device_id_type=MESH)

    mine = pl.ds(pl.multiple_of(m * WIDE, WIDE), WIDE)

    def pack(c):
        @pl.loop(0, NM // 8)
        def _(q):
            for place in range(4 * c, 4 * c + 4):
                first = ((z + ORDER[place] + NZ) % NZ) * (NM * BLK) + q * (8 * BLK)
                part = grad[:, pl.ds(pl.multiple_of(first, 128), 8 * BLK)]
                for i in range(8):
                    packed[q * 8 + i, :, place * BLK : (place + 1) * BLK] = part[:, i * BLK : (i + 1) * BLK]

    def b_copy(c, k):
        peer = (m + k) % NM
        lanes = pl.ds(PARTS[c], PARTS[c + 1] - PARTS[c])
        return pltpu.make_async_remote_copy(
            src_ref=packed.at[peer, :, lanes], dst_ref=recv_b.at[mine, lanes],
            send_sem=a2a_send.at[c], recv_sem=a2a_recv.at[c], device_id=member(peer), device_id_type=MESH,
        )

    def s_copy(k):
        peer = (t + k) % NT
        return pltpu.make_async_remote_copy(
            src_ref=sketch.at[z], dst_ref=recv_s.at[:, t],
            send_sem=s_send.at[k], recv_sem=s_recv.at[k], device_id=(dp, peer), device_id_type=MESH,
        )

    own_s = pltpu.make_async_copy(sketch.at[z], recv_s.at[:, t], local_sem.at[0])
    own_s.start()

    def send(c):
        @pl.loop(1, NM)
        def _(k):
            b_copy(c, k).start()

    pack(0)
    pl.semaphore_wait(barrier, NM - 1 + NZ - 1)

    @pl.loop(1, NT)
    def _(k):
        s_copy(k).start()

    send(0)
    send(1)
    pack(1)
    pack(2)
    pack(3)

    own_b = pltpu.make_async_copy(packed.at[m], recv_b.at[mine], local_sem.at[1])
    own_b.start()
    own_b.wait()
    own_s.wait()

    @pl.loop(1, NT)
    def _(k):
        s_copy(k).wait()

    def rows_of(k):
        return pl.ds(near(k) * BLK, BLK)

    halves = (pl.ds(0, HALF), pl.ds(HALF, HALF))
    chains = ((0, 1, 0, 0), (1, -1, 1, 0), (2, 1, 1, 1), (3, -1, 0, 1))

    def rs_copy(chain, s, src):
        name, way, h, _ = chain
        buf = rup if way == 1 else rdn
        return pltpu.make_async_remote_copy(
            src_ref=src, dst_ref=buf.at[s, :, halves[h]],
            send_sem=rs_send.at[name, s], recv_sem=rs_recv.at[name, s],
            device_id=zup if way == 1 else zdn, device_id_type=MESH,
        )

    def rs_step(s):
        for chain in chains:
            _, way, h, first = chain
            rows = rows_of(way * (8 - s))
            if s == first:
                rs_copy(chain, s, ypart.at[rows, halves[h]]).start()
            elif s > first:
                buf = rup if way == 1 else rdn
                slot = buf.at[s - 1, :, halves[h]]
                rs_copy(chain, s - 1, slot).wait_recv()
                buf[s - 1, :, halves[h]] += ypart[rows, halves[h]]
                rs_copy(chain, s, slot).start()

    for c in range(len(STEPS)):
        lanes = pl.ds(PARTS[c], PARTS[c + 1] - PARTS[c])
        await_bytes(recv_b.at[pl.ds(0, (NM - 1) * WIDE), lanes], a2a_recv.at[c])
        if 0 < c < len(STEPS) - 1:
            send(c + 1)
        ypart[lanes, :] = lax.dot_general(
            recv_b[:, lanes], recv_s[...].reshape(PW, RANK), TDOT, preferred_element_type=F32)
        for s in STEPS[c]:
            rs_step(s)

    own = rows_of(0)
    for chain in chains:
        _, way, h, _ = chain
        rs_copy(chain, 7, (rup if way == 1 else rdn).at[7, :, halves[h]]).wait_recv()
    yall[own, :] = ypart[own, :] + rup[7] + rdn[7]

    def ag_copy(chain, s):
        name, way, h, _ = chain
        return pltpu.make_async_remote_copy(
            src_ref=yall.at[rows_of(-way * s), halves[h]], dst_ref=yall.at[rows_of(-way * (s + 1)), halves[h]],
            send_sem=ag_send.at[name, s], recv_sem=ag_recv.at[name, s],
            device_id=zup if way == 1 else zdn, device_id_type=MESH,
        )

    def use(c):
        rows = pl.ds(USES[c], USES[c + 1] - USES[c])
        y = yall[rows, :]
        hi = y.astype(BF16)
        lo = (y - hi.astype(F32)).astype(BF16)
        b = recv_b[:, rows]
        w = jnp.dot(b, hi, preferred_element_type=F32) + jnp.dot(b, lo, preferred_element_type=F32)
        w = w.reshape(NCHIP, 2, WIDE, RANK)
        if c == 3:
            wpart[...] = w
        else:
            wpart[...] += w

    def to_sibling(src, dst, send_sem, recv_sem):
        return pltpu.make_async_remote_copy(
            src_ref=src, dst_ref=dst, send_sem=send_sem, recv_sem=recv_sem, device_id=sibling, device_id_type=MESH)

    g_pair = to_sibling(gown.at[1 - core], gsib, pair_send.at[0], pair_recv.at[0])
    w_pair = to_sibling(wpart.at[:, 1 - core], wsib, pair_send.at[1], pair_recv.at[1])

    def plane_copy(k, src, dst, send_sem, recv_sem):
        return pltpu.make_async_remote_copy(
            src_ref=src, dst_ref=dst, send_sem=send_sem, recv_sem=recv_sem,
            device_id=member(((chip + k) % NCHIP) * 2 + core), device_id_type=MESH)

    def z_copy(k, src, dst, send_sem, recv_sem):
        return pltpu.make_async_remote_copy(
            src_ref=src, dst_ref=dst, send_sem=send_sem, recv_sem=recv_sem,
            device_id=at_z((z + k) % NZ), device_id_type=MESH)

    def gram_1():
        y = yall[own, :]
        rhs[pl.ds(0, BLK), :] = y
        rhs[pl.ds(BLK, WIDE), :] = jnp.zeros((WIDE, RANK), F32)
        gram = lax.dot_general(y, y, TDOT, precision=HIGHEST, preferred_element_type=F32)
        gown[...] = gram.reshape(2, NCHIP, NZ, RANK)
        g_pair.start()

    def gram_2():
        g_pair.wait()
        gsib[...] += gown[core]

        @pl.loop(1, NCHIP)
        def _(k):
            plane_copy(k, gsib.at[(chip + k) % NCHIP], grecv.at[chip], g_send, g_recv).start()

        grecv[chip] = gsib[chip]

    def gram_3():
        await_bytes(grecv.at[pl.ds(0, NCHIP - 1)], g_recv)
        gzs[...] = jnp.sum(grecv[...], axis=0).reshape(NZ, 1, RANK)

        @pl.loop(1, NZ)
        def _(k):
            z_copy(k, gzs.at[(z + k) % NZ], gzr.at[z], gzs_send, gzs_recv).start()

        gzr[z] = gzs[z]

    def gram_4():
        await_bytes(gzr.at[pl.ds(0, NZ - 1)], gzs_recv)
        gza[z] = jnp.sum(gzr[...], axis=0)

        @pl.loop(1, NZ)
        def _(k):
            z_copy(k, gza.at[z], gza.at[z], gza_send, gza_recv).start()

    def gp_copy(k):
        piece = gall.at[core, chip]
        return plane_copy(k, piece, piece, gp_send.at[k], gp_recv.at[k])

    def gs_copy(k):
        piece = gall.at[core, mod(chip - k, NCHIP)]
        return to_sibling(piece, piece, gs_send.at[k], gs_recv.at[k])

    def gram_5():
        await_bytes(gza.at[pl.ds(0, NZ - 1)], gza_recv)
        gall[core, chip] = gza[...].reshape(NZ, RANK)

        @pl.loop(1, NCHIP)
        def _(k):
            gp_copy(k).start()

        gs_copy(0).start()

    def gram_6():
        @pl.loop(1, NCHIP)
        def _(k):
            piece = gall.at[core, mod(chip - k, NCHIP)]
            plane_copy(k, piece, piece, gp_send.at[k], gp_recv.at[k]).wait_recv()
            gs_copy(k).start()

    def gram_7():
        @pl.loop(0, NCHIP)
        def _(k):
            piece = gall.at[1 - core, mod(chip - k, NCHIP)]
            to_sibling(piece, piece, gs_send.at[k], gs_recv.at[k]).wait_recv()

    def gather_step(s):
        for chain in chains:
            if s < 8 - chain[3]:
                if s:
                    ag_copy(chain, s - 1).wait_recv()
                ag_copy(chain, s).start()

    def gather_end():
        for chain in chains:
            ag_copy(chain, 7 - chain[3]).wait_recv()

    gather_step(0)
    gram_1()
    gather_step(1)
    gram_2()
    gather_step(2)
    gram_3()
    gather_step(3)
    gram_4()
    use(3)
    gather_step(4)
    gram_5()
    use(2)
    gather_step(5)
    gram_6()
    gather_step(6)
    use(1)
    gram_7()

    def w_send_off():
        w_pair.wait()
        wsib[...] += wpart[:, core]

        @pl.loop(1, NCHIP)
        def _(k):
            plane_copy(k, wsib.at[(chip + k) % NCHIP], wrecv.at[chip], w_send, w_recv).start()

        wrecv[chip] = wsib[chip]

    def below(i):
        return pl.ds(i * NB, NB)

    def w_solve():
        await_bytes(wrecv.at[pl.ds(0, NCHIP - 1)], w_recv)
        w = jnp.concatenate([jnp.zeros((BLK, RANK), F32), jnp.sum(wrecv[...], axis=0)], axis=0).T
        for j in range(RANK // NB):
            part = jnp.dot(inverses[j], w[:NB], precision=HIGHEST, preferred_element_type=F32)
            solved[below(j), :] += part
            if j + 1 < RANK // NB:
                w = w[NB:] - lax.dot_general(
                    mat[below(j), (j + 1) * NB : RANK], part, TDOT, precision=HIGHEST, preferred_element_type=F32)

    def at(j, now, work_beside):
        @pl.when(j == now)
        def _():
            work_beside()

    mat[:, :RANK] = gall[...].reshape(RANK, RANK)
    mat[:, RANK:] = rhs[...].T

    @pl.loop(0, RANK // NB)
    def _(j):
        rows = pl.ds(pl.multiple_of(j * NB, NB), NB)
        work[...] = mat[rows, rows]

        def halfway():
            at(j, 0, lambda: gather_step(7))
            at(j, 2, w_send_off)

        invert_factor(work, halfway)

        def last_of_w():
            gather_end()
            use(0)
            w_pair.start()

        at(j, 1, last_of_w)
        row = lax.broadcasted_iota(jnp.int32, (NB, NB), 0)
        lane = lax.broadcasted_iota(jnp.int32, (NB, NB), 1)
        inverse = jnp.where(lane <= row, work[...], 0.0)
        inverses[j] = inverse
        upper = jnp.dot(inverse, mat[rows, :], precision=HIGHEST, preferred_element_type=F32)
        mat[rows, :] = upper
        solved[rows, :] = upper[:, RANK:]
        for i in range(1, RANK // NB):
            @pl.when(i > j)
            def _():
                mat[below(i), :] -= lax.dot_general(
                    upper[:, i * NB : (i + 1) * NB], upper, TDOT, precision=HIGHEST, preferred_element_type=F32)

    w_solve()

    packed_p = jnp.zeros((N_DP, NB), F32)
    lane = lax.broadcasted_iota(jnp.int32, (N_DP, NB), 1)
    for r in range(PER_DP):
        part = solved[pl.ds(r, N_DP, stride=PER_DP), :]
        slot = PER_DP - 1 - r
        packed_p = jnp.where(lane // WIDE == slot, pltpu.roll(part, (WIDE * slot - BLK) % NB, 1), packed_p)
    outbox[...] = packed_p.reshape(NZ, NX, 1, NB)

    def x_copy(k):
        peer = (x + k) % NX
        return pltpu.make_async_remote_copy(
            src_ref=outbox.at[:, peer], dst_ref=inbox_x.at[x], send_sem=x_send.at[k], recv_sem=x_recv.at[k],
            device_id=(z * NX + peer, t), device_id_type=MESH,
        )

    for k in range(1, NX):
        x_copy(k).start()
    inbox_x[x] = outbox[:, x]
    basis_out[...] = (solved[:, :BLK] * math.sqrt(ROWS)).astype(BF16)
    for k in range(1, NX):
        x_copy(k).wait()

    @pl.loop(1, NZ)
    def _(k):
        z_copy(k, inbox_x.at[:, (z + k) % NZ], inbox_z.at[z], z_send, z_recv).start()

    inbox_z[z] = inbox_x[:, z]

    for ref, sem in (
        (grecv.at[pl.ds(0, NCHIP - 1)], g_send), (wrecv.at[pl.ds(0, NCHIP - 1)], w_send),
        (gzr.at[pl.ds(0, NZ - 1)], gzs_send), (gza.at[pl.ds(0, NZ - 1)], gza_send),
    ):
        await_bytes(ref, sem)

    @pl.loop(0, NCHIP)
    def _(k):
        gs_copy(k).wait_send()

    @pl.loop(1, NCHIP)
    def _(k):
        gp_copy(k).wait_send()

    for c in range(len(STEPS)):
        await_bytes(recv_b.at[pl.ds(0, (NM - 1) * WIDE), pl.ds(PARTS[c], PARTS[c + 1] - PARTS[c])], a2a_send.at[c])
    for chain in chains:
        _, way, h, first = chain
        for s in range(first, 8):
            rs_copy(chain, s, (rup if way == 1 else rdn).at[s, :, halves[h]]).wait_send()
        for s in range(0, 8 - first):
            ag_copy(chain, s).wait_send()

    await_bytes(inbox_z.at[pl.ds(0, NZ - 1)], z_send)
    await_bytes(inbox_z.at[pl.ds(0, NZ - 1)], z_recv)
    per_tile = NB // WIDE
    lane = lax.broadcasted_iota(jnp.int32, (PER_DP, NB), 1)
    for q in range(N_DP // per_tile):
        tile = jnp.zeros((PER_DP, NB), F32)
        for i in range(per_tile):
            src = q * per_tile + i
            line = jnp.broadcast_to(inbox_z[src // NX, src % NX], (PER_DP, NB))
            line = pltpu.roll(line, 0, 1, stride=WIDE, stride_axis=0)
            line = pltpu.roll(line, (WIDE * (i + 1)) % NB, 1)
            tile = jnp.where(lane // WIDE == i, line, tile)
        proj_out[:, q * NB : (q + 1) * NB] = tile.astype(BF16)


def project(grad_buckets, sketch):
    vmem = pl.BlockSpec(memory_space=pltpu.VMEM)
    dma = pltpu.SemaphoreType.DMA
    return pl.pallas_call(
        kernel,
        out_shape=(
            jax.ShapeDtypeStruct((RANK, BLK), BF16),
            jax.ShapeDtypeStruct((PER_DP, N_DP * WIDE), BF16),
        ),
        in_specs=[vmem, pl.BlockSpec(memory_space=pl.ANY)],
        out_specs=(vmem, vmem),
        scratch_shapes=[
            pltpu.VMEM((NM, WIDE, COLS), BF16),
            pltpu.VMEM((PW, COLS), BF16),
            pltpu.VMEM((NX, NT, WIDE, RANK), BF16),
            pltpu.VMEM((COLS, RANK), F32),
            pltpu.VMEM((COLS, RANK), F32),
            pltpu.VMEM((8, BLK, RANK), F32),
            pltpu.VMEM((8, BLK, RANK), F32),
            pltpu.VMEM((NCHIP, 2, WIDE, RANK), F32),
            pltpu.VMEM((NCHIP, WIDE, RANK), F32),
            pltpu.VMEM((NCHIP, WIDE, RANK), F32),
            pltpu.VMEM((2, NCHIP, NZ, RANK), F32),
            pltpu.VMEM((NCHIP, NZ, RANK), F32),
            pltpu.VMEM((NCHIP, NZ, RANK), F32),
            pltpu.VMEM((NZ, 1, RANK), F32),
            pltpu.VMEM((NZ, 1, RANK), F32),
            pltpu.VMEM((NZ, 1, RANK), F32),
            pltpu.VMEM((2, NCHIP, NZ, RANK), F32),
            pltpu.VMEM((BLK + WIDE, RANK), F32),
            pltpu.VMEM((RANK, RANK + NB), F32),
            pltpu.VMEM((NB, NB), F32),
            pltpu.VMEM((RANK // NB, NB, NB), F32),
            pltpu.VMEM((RANK, NB), F32),
            pltpu.VMEM((NZ, NX, 1, NB), F32),
            pltpu.VMEM((NX, NZ, 1, NB), F32),
            pltpu.VMEM((NZ, NX, 1, NB), F32),
            dma((2,)),
            dma((len(STEPS),)), dma((len(STEPS),)),
            dma((NT,)), dma((NT,)),
            dma((4, 8)), dma((4, 8)),
            dma((4, 8)), dma((4, 8)),
            dma((2,)), dma((2,)),
            dma, dma, dma, dma, dma, dma, dma, dma,
            dma((NCHIP,)), dma((NCHIP,)),
            dma((NCHIP,)), dma((NCHIP,)),
            dma((NX,)), dma((NX,)),
            dma, dma,
        ],
        compiler_params=pltpu.CompilerParams(
            collective_id=0, has_side_effects=True, vmem_limit_bytes=56 * 1024 * 1024),
    )(grad_buckets, sketch)


def shards(grad_buckets, sketch):
    return project(grad_buckets, sketch.reshape(NZ, NX, WIDE, RANK))


def solution(mesh):
    in_specs = (P(("tensor", "dp"), None), P("tensor", None))
    out_specs = (P(None, ("dp", "tensor")), P("dp", "tensor"))
    return jax.shard_map(shards, mesh=mesh, in_specs=in_specs, out_specs=out_specs, check_vma=False)
```

```python
import math

import jax
import jax.numpy as jnp
from jax import lax
from jax.experimental import pallas as pl
from jax.experimental.pallas import tpu as pltpu
from jax.sharding import PartitionSpec as P

MESH = pl.DeviceIdType.MESH
F32 = jnp.float32
BF16 = jnp.bfloat16
NZ, NX, NT = 16, 4, 8
NM = NX * NT
NCHIP = NM // 2
ROWS = 57344
RANK = 512
WIDE = 16
BLK = ROWS // (NZ * NM)
COLS = BLK * NZ
PW = WIDE * NM
HALF = RANK // 2
PARTS = (0, 128, 384, 896, 1280, 1792)
STEPS = ((0,), (1,), (2, 3), (4, 5), (6, 7))
USES = (0, 384, 896, 1280, 1792)
N_DP = NZ * NX
PER_DP = RANK // N_DP
NB = 128
GROUP = 8
GR, GL = 8, 640
HIGHEST = lax.Precision.HIGHEST
TDOT = (((0,), (0,)), ((), ()))


def mod(a, n):
    return lax.rem(a + n, n)


def near(k):
    if k == 0:
        return NZ - 1
    if abs(k) == NZ // 2:
        return 0
    return NZ - 1 - 2 * k if k > 0 else NZ + 2 * k


ORDER = sorted(range(1 - NZ // 2, NZ // 2 + 1), key=near)


def await_bytes(ref, sem):
    pltpu.make_async_copy(ref, ref, sem).wait()


def invert_factor(work, halfway):
    for s in range(0, NB, GROUP):
        if s == NB // 2:
            halfway()
        n = NB - s
        row = lax.broadcasted_iota(jnp.int32, (GROUP, NB), 0)
        lane = lax.broadcasted_iota(jnp.int32, (GROUP, NB), 1)
        rest = work[s:, :]
        cols = [jnp.broadcast_to(rest[:, s + k : s + k + 1], (n, NB)) for k in range(GROUP)]
        top = jnp.where((lane >= s) & (lane < s + GROUP), jnp.where(lane - s == row, 1.0, 0.0), rest[:GROUP])
        below = rest[GROUP:]
        if n > GROUP:
            lane_b = lax.broadcasted_iota(jnp.int32, (n - GROUP, NB), 1)
            below = jnp.where((lane_b >= s) & (lane_b < s + GROUP), 0.0, below)
        for k in range(GROUP):
            r = lax.rsqrt(jnp.broadcast_to(cols[k][k : k + 1], (GROUP, NB)))
            mult = cols[k] * jnp.broadcast_to(r[:1], (n, NB))
            for q in range(k + 1, GROUP):
                cols[q] = cols[q] - mult * jnp.broadcast_to(mult[q : q + 1], (n, NB))
            u = jnp.broadcast_to(top[k : k + 1], (GROUP, NB)) * r
            top = jnp.where(row == k, u, jnp.where(row > k, top - mult[:GROUP] * u, top))
            if n > GROUP:
                below = below - mult[GROUP:] * jnp.broadcast_to(u[:1], (n - GROUP, NB))
        work[s : s + GROUP, :] = top
        if n > GROUP:
            work[s + GROUP :, :] = below


def kernel(
    grad_hbm, sketch, basis_out, proj_out,
    grad, packed, recv_b, recv_s, ypart, yall, rup, rdn, wpart, wsib, wrecv,
    ysib, gown, grecv, gzs, gzr, gza, gall, rhs, mat, work, inverses, solved, outbox, inbox_x, inbox_z,
    local_sem, a2a_send, a2a_recv, s_send, s_recv, rs_send, rs_recv, ag_send, ag_recv,
    pair_send, pair_recv, w_send, w_recv, g_send, g_recv, gzs_send, gzs_recv, gza_send, gza_recv,
    gp_send, gp_recv, gs_send, gs_recv, x_send, x_recv, z_send, z_recv,
):
    dp = lax.axis_index("dp")
    t = lax.axis_index("tensor")
    z = dp // NX
    x = dp % NX
    m = x * NT + t
    chip = m // 2
    core = m % 2

    def member(i):
        return (z * NX + i // NT, i % NT)

    def at_z(i):
        return (i * NX + x, t)

    zup, zdn = at_z(mod(z + 1, NZ)), at_z(mod(z - 1, NZ))
    sibling = (dp, t + 1 - 2 * core)

    grad_in = pltpu.make_async_copy(grad_hbm, grad, local_sem.at[2])
    grad_in.start()

    barrier = pltpu.get_barrier_semaphore()

    @pl.loop(1, NM)
    def _(k):
        pl.semaphore_signal(barrier, inc=1, device_id=member((m + k) % NM), device_id_type=MESH)

    @pl.loop(1, NZ)
    def _(k):
        pl.semaphore_signal(barrier, inc=1, device_id=at_z((z + k) % NZ), device_id_type=MESH)

    mine = pl.ds(pl.multiple_of(m * WIDE, WIDE), WIDE)

    def pack(c):
        @pl.loop(0, NM // 8)
        def _(q):
            for place in range(4 * c, 4 * c + 4):
                first = ((z + ORDER[place] + NZ) % NZ) * (NM * BLK) + q * (8 * BLK)
                part = grad[:, pl.ds(pl.multiple_of(first, 128), 8 * BLK)]
                for i in range(8):
                    packed[q * 8 + i, :, place * BLK : (place + 1) * BLK] = part[:, i * BLK : (i + 1) * BLK]

    def b_copy(c, k):
        peer = (m + k) % NM
        lanes = pl.ds(PARTS[c], PARTS[c + 1] - PARTS[c])
        return pltpu.make_async_remote_copy(
            src_ref=packed.at[peer, :, lanes], dst_ref=recv_b.at[mine, lanes],
            send_sem=a2a_send.at[c], recv_sem=a2a_recv.at[c], device_id=member(peer), device_id_type=MESH,
        )

    def s_copy(k):
        peer = (t + k) % NT
        return pltpu.make_async_remote_copy(
            src_ref=sketch.at[z], dst_ref=recv_s.at[:, t],
            send_sem=s_send.at[k], recv_sem=s_recv.at[k], device_id=(dp, peer), device_id_type=MESH,
        )

    own_s = pltpu.make_async_copy(sketch.at[z], recv_s.at[:, t], local_sem.at[0])
    own_s.start()

    def send(c):
        @pl.loop(1, NM)
        def _(k):
            b_copy(c, k).start()

    grad_in.wait()
    pack(0)
    pl.semaphore_wait(barrier, NM - 1 + NZ - 1)

    @pl.loop(1, NT)
    def _(k):
        s_copy(k).start()

    send(0)
    send(1)
    pack(1)
    pack(2)
    pack(3)

    own_b = pltpu.make_async_copy(packed.at[m], recv_b.at[mine], local_sem.at[1])
    own_b.start()
    own_b.wait()
    own_s.wait()

    @pl.loop(1, NT)
    def _(k):
        s_copy(k).wait()

    def rows_of(k):
        return pl.ds(near(k) * BLK, BLK)

    halves = (pl.ds(0, HALF), pl.ds(HALF, HALF))
    chains = ((0, 1, 0, 0), (1, -1, 1, 0), (2, 1, 1, 1), (3, -1, 0, 1))

    def rs_copy(chain, s, src):
        name, way, h, _ = chain
        buf = rup if way == 1 else rdn
        return pltpu.make_async_remote_copy(
            src_ref=src, dst_ref=buf.at[s, :, halves[h]],
            send_sem=rs_send.at[name, s], recv_sem=rs_recv.at[name, s],
            device_id=zup if way == 1 else zdn, device_id_type=MESH,
        )

    def rs_step(s):
        for chain in chains:
            _, way, h, first = chain
            rows = rows_of(way * (8 - s))
            if s == first:
                rs_copy(chain, s, ypart.at[rows, halves[h]]).start()
            elif s > first:
                buf = rup if way == 1 else rdn
                slot = buf.at[s - 1, :, halves[h]]
                rs_copy(chain, s - 1, slot).wait_recv()
                buf[s - 1, :, halves[h]] += ypart[rows, halves[h]]
                rs_copy(chain, s, slot).start()

    for c in range(len(STEPS)):
        lanes = pl.ds(PARTS[c], PARTS[c + 1] - PARTS[c])
        await_bytes(recv_b.at[pl.ds(0, (NM - 1) * WIDE), lanes], a2a_recv.at[c])
        if 0 < c < len(STEPS) - 1:
            send(c + 1)
        ypart[lanes, :] = lax.dot_general(
            recv_b[:, lanes], recv_s[...].reshape(PW, RANK), TDOT, preferred_element_type=F32)
        for s in STEPS[c]:
            rs_step(s)

    own = rows_of(0)

    def ag_copy(chain, s):
        name, way, h, _ = chain
        return pltpu.make_async_remote_copy(
            src_ref=yall.at[rows_of(-way * s), halves[h]], dst_ref=yall.at[rows_of(-way * (s + 1)), halves[h]],
            send_sem=ag_send.at[name, s], recv_sem=ag_recv.at[name, s],
            device_id=zup if way == 1 else zdn, device_id_type=MESH,
        )

    def use(c):
        rows = pl.ds(USES[c], USES[c + 1] - USES[c])
        y = yall[rows, :]
        hi = y.astype(BF16)
        lo = (y - hi.astype(F32)).astype(BF16)
        b = recv_b[:, rows]
        w = jnp.dot(b, hi, preferred_element_type=F32) + jnp.dot(b, lo, preferred_element_type=F32)
        w = w.reshape(NCHIP, 2, WIDE, RANK)
        if c == 3:
            wpart[...] = w
        else:
            wpart[...] += w

    def to_sibling(src, dst, send_sem, recv_sem):
        return pltpu.make_async_remote_copy(
            src_ref=src, dst_ref=dst, send_sem=send_sem, recv_sem=recv_sem, device_id=sibling, device_id_type=MESH)

    g_pair = to_sibling(yall.at[own], ysib, pair_send.at[0], pair_recv.at[0])
    w_pair = to_sibling(wpart.at[:, 1 - core], wsib, pair_send.at[1], pair_recv.at[1])

    def plane_copy(k, src, dst, send_sem, recv_sem):
        return pltpu.make_async_remote_copy(
            src_ref=src, dst_ref=dst, send_sem=send_sem, recv_sem=recv_sem,
            device_id=member(((chip + k) % NCHIP) * 2 + core), device_id_type=MESH)

    def z_copy(k, src, dst, send_sem, recv_sem):
        return pltpu.make_async_remote_copy(
            src_ref=src, dst_ref=dst, send_sem=send_sem, recv_sem=recv_sem,
            device_id=at_z((z + k) % NZ), device_id_type=MESH)

    def gram_1():
        g_pair.start()
        rhs[pl.ds(0, BLK), :] = yall[own, :]
        rhs[pl.ds(BLK, WIDE), :] = jnp.zeros((WIDE, RANK), F32)

    def gram_2():
        g_pair.wait()
        y = jnp.concatenate([yall[own, :], ysib[...]], axis=0)

        def blocks(i, first, count):
            return lax.dot_general(
                y[:, i * NB : (i + 1) * NB], y[:, first * NB : (first + count) * NB], TDOT,
                precision=HIGHEST, preferred_element_type=F32).reshape(NCHIP, GR, count * NB)

        @pl.when(core == 0)
        def _():
            gown[:, :, : 4 * NB] = blocks(0, 0, 4)
            gown[:, :, 4 * NB :] = blocks(1, 1, 1)

        @pl.when(core == 1)
        def _():
            gown[:, :, : 2 * NB] = blocks(1, 2, 2)
            gown[:, :, 2 * NB : 4 * NB] = blocks(2, 2, 2)
            gown[:, :, 4 * NB :] = blocks(3, 3, 1)

        @pl.loop(1, NCHIP)
        def _(k):
            plane_copy(k, gown.at[(chip + k) % NCHIP], grecv.at[chip], g_send, g_recv).start()

        grecv[chip] = gown[chip]

    def gram_3():
        await_bytes(grecv.at[pl.ds(0, NCHIP - 1)], g_recv)
        gzs[...] = jnp.sum(grecv[...], axis=0).reshape(GR, 1, GL)

        @pl.loop(1, NZ)
        def _(k):
            peer = (z + k) % NZ

            @pl.when(peer < GR)
            def _():
                z_copy(k, gzs.at[peer], gzr.at[z], gzs_send, gzs_recv).start()

        @pl.when(z < GR)
        def _():
            gzr[z] = gzs[z]

    def gram_4():
        @pl.when(z < GR)
        def _():
            await_bytes(gzr.at[pl.ds(0, NZ - 1)], gzs_recv)
            gza[z] = jnp.sum(gzr[...], axis=0)

            @pl.loop(1, NZ)
            def _(k):
                z_copy(k, gza.at[z], gza.at[z], gza_send, gza_recv).start()

    def gp_copy(k):
        piece = gall.at[core, chip]
        return plane_copy(k, piece, piece, gp_send.at[k], gp_recv.at[k])

    def gs_copy(k):
        piece = gall.at[core, mod(chip - k, NCHIP)]
        return to_sibling(piece, piece, gs_send.at[k], gs_recv.at[k])

    def gram_5():
        @pl.when(z < GR)
        def _():
            await_bytes(gza.at[pl.ds(0, GR - 1)], gza_recv)

        @pl.when(z >= GR)
        def _():
            await_bytes(gza, gza_recv)

        gall[core, chip] = gza[...].reshape(GR, GL)

        @pl.loop(1, NCHIP)
        def _(k):
            gp_copy(k).start()

        gs_copy(0).start()

    def gram_6():
        @pl.loop(1, NCHIP)
        def _(k):
            piece = gall.at[core, mod(chip - k, NCHIP)]
            plane_copy(k, piece, piece, gp_send.at[k], gp_recv.at[k]).wait_recv()
            gs_copy(k).start()

    def gram_7():
        @pl.loop(0, NCHIP)
        def _(k):
            piece = gall.at[1 - core, mod(chip - k, NCHIP)]
            to_sibling(piece, piece, gs_send.at[k], gs_recv.at[k]).wait_recv()

    def gather_step(s, which):
        for chain in which:
            if s < 8 - chain[3]:
                if s:
                    ag_copy(chain, s - 1).wait_recv()
                ag_copy(chain, s).start()

    def gather_end():
        for chain in chains:
            ag_copy(chain, 7 - chain[3]).wait_recv()

    for h in range(2):
        ends = [chain for chain in chains if chain[2] == h]
        for chain in ends:
            rs_copy(chain, 7, (rup if chain[1] == 1 else rdn).at[7, :, halves[h]]).wait_recv()
        yall[own, halves[h]] = ypart[own, halves[h]] + rup[7, :, halves[h]] + rdn[7, :, halves[h]]
        gather_step(0, ends)
    gram_1()
    one, two = chains[:2], chains[2:]
    gram_2()
    gather_step(1, chains)
    gather_step(2, chains)
    gram_3()
    gather_step(3, chains)
    gram_4()
    gather_step(4, one)
    use(3)
    gather_step(4, two)
    gram_5()
    use(2)
    gather_step(5, chains)
    gram_6()
    gather_step(6, one)
    gram_7()
    gather_step(6, two)
    use(1)

    def w_send_off():
        w_pair.wait()
        wsib[...] += wpart[:, core]

        @pl.loop(1, NCHIP)
        def _(k):
            plane_copy(k, wsib.at[(chip + k) % NCHIP], wrecv.at[chip], w_send, w_recv).start()

        wrecv[chip] = wsib[chip]

    def below(i):
        return pl.ds(i * NB, NB)

    def w_solve():
        await_bytes(wrecv.at[pl.ds(0, NCHIP - 1)], w_recv)
        w = jnp.concatenate([jnp.zeros((BLK, RANK), F32), jnp.sum(wrecv[...], axis=0)], axis=0).T
        for j in range(RANK // NB):
            part = jnp.dot(inverses[j], w[:NB], precision=HIGHEST, preferred_element_type=F32)
            solved[below(j), :] += part
            if j + 1 < RANK // NB:
                w = w[NB:] - lax.dot_general(
                    mat[below(j), (j + 1) * NB : RANK], part, TDOT, precision=HIGHEST, preferred_element_type=F32)

    def at(j, now, work_beside):
        @pl.when(j == now)
        def _():
            work_beside()

    upper_blocks = [gall[i].reshape(NB, GL) for i in range(2)]
    mat[:, :RANK] = jnp.zeros((RANK, RANK), F32)
    mat[below(0), :RANK] = upper_blocks[0][:, :RANK]
    mat[below(1), NB : 2 * NB] = upper_blocks[0][:, RANK:]
    mat[below(1), 2 * NB : RANK] = upper_blocks[1][:, : 2 * NB]
    mat[below(2), 2 * NB : RANK] = upper_blocks[1][:, 2 * NB : 4 * NB]
    mat[below(3), 3 * NB : RANK] = upper_blocks[1][:, 4 * NB :]
    mat[:, RANK:] = rhs[...].T

    @pl.loop(0, RANK // NB)
    def _(j):
        rows = pl.ds(pl.multiple_of(j * NB, NB), NB)
        work[...] = mat[rows, rows]
        at(j, 1, lambda: gather_step(7, chains))

        def last_of_w():
            gather_end()
            use(0)
            w_pair.start()

        at(j, 2, last_of_w)

        def halfway():
            at(j, 2, w_send_off)

        invert_factor(work, halfway)

        row = lax.broadcasted_iota(jnp.int32, (NB, NB), 0)
        lane = lax.broadcasted_iota(jnp.int32, (NB, NB), 1)
        inverse = jnp.where(lane <= row, work[...], 0.0)
        inverses[j] = inverse
        upper = jnp.dot(inverse, mat[rows, :], precision=HIGHEST, preferred_element_type=F32)
        mat[rows, :] = upper
        solved[rows, :] = upper[:, RANK:]
        for i in range(1, RANK // NB):
            @pl.when(i > j)
            def _():
                mat[below(i), :] -= lax.dot_general(
                    upper[:, i * NB : (i + 1) * NB], upper, TDOT, precision=HIGHEST, preferred_element_type=F32)

    w_solve()

    packed_p = jnp.zeros((N_DP, NB), F32)
    lane = lax.broadcasted_iota(jnp.int32, (N_DP, NB), 1)
    for r in range(PER_DP):
        part = solved[pl.ds(r, N_DP, stride=PER_DP), :]
        slot = PER_DP - 1 - r
        packed_p = jnp.where(lane // WIDE == slot, pltpu.roll(part, (WIDE * slot - BLK) % NB, 1), packed_p)
    outbox[...] = packed_p.reshape(NZ, NX, 1, NB)

    def x_copy(k):
        peer = (x + k) % NX
        return pltpu.make_async_remote_copy(
            src_ref=outbox.at[:, peer], dst_ref=inbox_x.at[x], send_sem=x_send.at[k], recv_sem=x_recv.at[k],
            device_id=(z * NX + peer, t), device_id_type=MESH,
        )

    for k in range(1, NX):
        x_copy(k).start()
    inbox_x[x] = outbox[:, x]
    basis_out[...] = (solved[...].T[:BLK] * math.sqrt(ROWS)).astype(BF16)
    for k in range(1, NX):
        x_copy(k).wait()

    @pl.loop(1, NZ)
    def _(k):
        z_copy(k, inbox_x.at[:, (z + k) % NZ], inbox_z.at[z], z_send, z_recv).start()

    inbox_z[z] = inbox_x[:, z]

    for ref, sem in (
        (grecv.at[pl.ds(0, NCHIP - 1)], g_send), (wrecv.at[pl.ds(0, NCHIP - 1)], w_send),
    ):
        await_bytes(ref, sem)

    @pl.when(z < GR)
    def _():
        await_bytes(gza.at[pl.ds(0, GR - 1)], gzs_send)
        await_bytes(gzr.at[pl.ds(0, NZ - 1)], gza_send)

    @pl.when(z >= GR)
    def _():
        await_bytes(gza, gzs_send)

    @pl.loop(0, NCHIP)
    def _(k):
        gs_copy(k).wait_send()

    @pl.loop(1, NCHIP)
    def _(k):
        gp_copy(k).wait_send()

    for c in range(len(STEPS)):
        await_bytes(recv_b.at[pl.ds(0, (NM - 1) * WIDE), pl.ds(PARTS[c], PARTS[c + 1] - PARTS[c])], a2a_send.at[c])
    for chain in chains:
        _, way, h, first = chain
        for s in range(first, 8):
            rs_copy(chain, s, (rup if way == 1 else rdn).at[s, :, halves[h]]).wait_send()
        for s in range(0, 8 - first):
            ag_copy(chain, s).wait_send()

    await_bytes(inbox_z.at[pl.ds(0, NZ - 1)], z_send)
    await_bytes(inbox_z.at[pl.ds(0, NZ - 1)], z_recv)
    per_tile = NB // WIDE
    lane = lax.broadcasted_iota(jnp.int32, (PER_DP, NB), 1)
    for q in range(N_DP // per_tile):
        tile = jnp.zeros((PER_DP, NB), F32)
        for i in range(per_tile):
            src = q * per_tile + i
            line = jnp.broadcast_to(inbox_z[src // NX, src % NX], (PER_DP, NB))
            line = pltpu.roll(line, 0, 1, stride=WIDE, stride_axis=0)
            line = pltpu.roll(line, (WIDE * (i + 1)) % NB, 1)
            tile = jnp.where(lane // WIDE == i, line, tile)
        proj_out[:, q * NB : (q + 1) * NB] = tile.astype(BF16)


def project(grad_buckets, sketch):
    vmem = pl.BlockSpec(memory_space=pltpu.VMEM)
    dma = pltpu.SemaphoreType.DMA
    return pl.pallas_call(
        kernel,
        out_shape=(
            jax.ShapeDtypeStruct((BLK, RANK), BF16),
            jax.ShapeDtypeStruct((PER_DP, N_DP * WIDE), BF16),
        ),
        in_specs=[pl.BlockSpec(memory_space=pl.ANY)] * 2,
        out_specs=(vmem, vmem),
        scratch_shapes=[
            pltpu.VMEM((WIDE, ROWS), BF16),
            pltpu.VMEM((NM, WIDE, COLS), BF16),
            pltpu.VMEM((PW, COLS), BF16),
            pltpu.VMEM((NX, NT, WIDE, RANK), BF16),
            pltpu.VMEM((COLS, RANK), F32),
            pltpu.VMEM((COLS, RANK), F32),
            pltpu.VMEM((8, BLK, RANK), F32),
            pltpu.VMEM((8, BLK, RANK), F32),
            pltpu.VMEM((NCHIP, 2, WIDE, RANK), F32),
            pltpu.VMEM((NCHIP, WIDE, RANK), F32),
            pltpu.VMEM((NCHIP, WIDE, RANK), F32),
            pltpu.VMEM((BLK, RANK), F32),
            pltpu.VMEM((NCHIP, GR, GL), F32),
            pltpu.VMEM((NCHIP, GR, GL), F32),
            pltpu.VMEM((GR, 1, GL), F32),
            pltpu.VMEM((NZ, 1, GL), F32),
            pltpu.VMEM((GR, 1, GL), F32),
            pltpu.VMEM((2, NCHIP, GR, GL), F32),
            pltpu.VMEM((BLK + WIDE, RANK), F32),
            pltpu.VMEM((RANK, RANK + NB), F32),
            pltpu.VMEM((NB, NB), F32),
            pltpu.VMEM((RANK // NB, NB, NB), F32),
            pltpu.VMEM((RANK, NB), F32),
            pltpu.VMEM((NZ, NX, 1, NB), F32),
            pltpu.VMEM((NX, NZ, 1, NB), F32),
            pltpu.VMEM((NZ, NX, 1, NB), F32),
            dma((3,)),
            dma((len(STEPS),)), dma((len(STEPS),)),
            dma((NT,)), dma((NT,)),
            dma((4, 8)), dma((4, 8)),
            dma((4, 8)), dma((4, 8)),
            dma((2,)), dma((2,)),
            dma, dma, dma, dma, dma, dma, dma, dma,
            dma((NCHIP,)), dma((NCHIP,)),
            dma((NCHIP,)), dma((NCHIP,)),
            dma((NX,)), dma((NX,)),
            dma, dma,
        ],
        compiler_params=pltpu.CompilerParams(
            collective_id=0, has_side_effects=True, vmem_limit_bytes=56 * 1024 * 1024),
    )(grad_buckets, sketch)


def shards(grad_buckets, sketch):
    basis, projected = project(grad_buckets, sketch.reshape(NZ, NX, WIDE, RANK))
    return basis.T, projected


def solution(mesh):
    in_specs = (P(("tensor", "dp"), None), P("tensor", None))
    out_specs = (P(None, ("dp", "tensor")), P("dp", "tensor"))
    return jax.shard_map(shards, mesh=mesh, in_specs=in_specs, out_specs=out_specs, check_vma=False)
```

```python
import math

import jax
import jax.numpy as jnp
from jax import lax
from jax.experimental import pallas as pl
from jax.experimental.pallas import tpu as pltpu
from jax.sharding import PartitionSpec as P

MESH = pl.DeviceIdType.MESH
F32 = jnp.float32
BF16 = jnp.bfloat16
NZ, NX, NT = 16, 4, 8
NM = NX * NT
NCHIP = NM // 2
ROWS = 57344
RANK = 512
WIDE = 16
BLK = ROWS // (NZ * NM)
COLS = BLK * NZ
PW = WIDE * NM
HALF = RANK // 2
PARTS = (0, 128, 384, 896, 1280, 1792)
STEPS = ((0,), (1,), (2, 3), (4, 5), (6, 7))
USES = (0, 384, 896, 1280, 1792)
N_DP = NZ * NX
PER_DP = RANK // N_DP
NB = 128
GROUP = 8
GR, GL = 8, 640
HIGHEST = lax.Precision.HIGHEST
TDOT = (((0,), (0,)), ((), ()))


def mod(a, n):
    return lax.rem(a + n, n)


def near(k):
    if k == 0:
        return NZ - 1
    if abs(k) == NZ // 2:
        return 0
    return NZ - 1 - 2 * k if k > 0 else NZ + 2 * k


ORDER = sorted(range(1 - NZ // 2, NZ // 2 + 1), key=near)


def await_bytes(ref, sem):
    pltpu.make_async_copy(ref, ref, sem).wait()


def invert_factor(work, halfway):
    for s in range(0, NB, GROUP):
        if s == NB // 2:
            halfway()
        n = NB - s
        row = lax.broadcasted_iota(jnp.int32, (GROUP, NB), 0)
        lane = lax.broadcasted_iota(jnp.int32, (GROUP, NB), 1)
        rest = work[s:, :]
        cols = [jnp.broadcast_to(rest[:, s + k : s + k + 1], (n, NB)) for k in range(GROUP)]
        top = jnp.where((lane >= s) & (lane < s + GROUP), jnp.where(lane - s == row, 1.0, 0.0), rest[:GROUP])
        below = rest[GROUP:]
        if n > GROUP:
            lane_b = lax.broadcasted_iota(jnp.int32, (n - GROUP, NB), 1)
            below = jnp.where((lane_b >= s) & (lane_b < s + GROUP), 0.0, below)
        for k in range(GROUP):
            r = lax.rsqrt(jnp.broadcast_to(cols[k][k : k + 1], (GROUP, NB)))
            mult = cols[k] * jnp.broadcast_to(r[:1], (n, NB))
            for q in range(k + 1, GROUP):
                cols[q] = cols[q] - mult * jnp.broadcast_to(mult[q : q + 1], (n, NB))
            u = jnp.broadcast_to(top[k : k + 1], (GROUP, NB)) * r
            top = jnp.where(row == k, u, jnp.where(row > k, top - mult[:GROUP] * u, top))
            if n > GROUP:
                below = below - mult[GROUP:] * jnp.broadcast_to(u[:1], (n - GROUP, NB))
        work[s : s + GROUP, :] = top
        if n > GROUP:
            work[s + GROUP :, :] = below


def kernel(
    grad_hbm, sketch, basis_out, proj_out,
    grad, packed, recv_b, recv_s, ypart, yall, rup, rdn, wpart, wsib, wrecv,
    ysib, gown, grecv, gzs, gzr, gza, gall, rhs, mat, work, inverses, solved, solved_w, outbox, inbox_x, inbox_z,
    local_sem, a2a_send, a2a_recv, s_send, s_recv, rs_send, rs_recv, ag_send, ag_recv,
    pair_send, pair_recv, w_send, w_recv, g_send, g_recv, gzs_send, gzs_recv, gza_send, gza_recv,
    gp_send, gp_recv, gs_send, gs_recv, x_send, x_recv, z_send, z_recv,
):
    dp = lax.axis_index("dp")
    t = lax.axis_index("tensor")
    z = dp // NX
    x = dp % NX
    m = x * NT + t
    chip = m // 2
    core = m % 2

    def member(i):
        return (z * NX + i // NT, i % NT)

    def at_z(i):
        return (i * NX + x, t)

    zup, zdn = at_z(mod(z + 1, NZ)), at_z(mod(z - 1, NZ))
    sibling = (dp, t + 1 - 2 * core)

    grad_in = pltpu.make_async_copy(grad_hbm, grad, local_sem.at[2])
    grad_in.start()

    barrier = pltpu.get_barrier_semaphore()

    @pl.loop(1, NM)
    def _(k):
        pl.semaphore_signal(barrier, inc=1, device_id=member((m + k) % NM), device_id_type=MESH)

    @pl.loop(1, NZ)
    def _(k):
        pl.semaphore_signal(barrier, inc=1, device_id=at_z((z + k) % NZ), device_id_type=MESH)

    mine = pl.ds(pl.multiple_of(m * WIDE, WIDE), WIDE)

    def pack(c):
        @pl.loop(0, NM // 8)
        def _(q):
            for place in range(4 * c, 4 * c + 4):
                first = ((z + ORDER[place] + NZ) % NZ) * (NM * BLK) + q * (8 * BLK)
                part = grad[:, pl.ds(pl.multiple_of(first, 128), 8 * BLK)]
                for i in range(8):
                    packed[q * 8 + i, :, place * BLK : (place + 1) * BLK] = part[:, i * BLK : (i + 1) * BLK]

    def b_copy(c, k):
        peer = (m + k) % NM
        lanes = pl.ds(PARTS[c], PARTS[c + 1] - PARTS[c])
        return pltpu.make_async_remote_copy(
            src_ref=packed.at[peer, :, lanes], dst_ref=recv_b.at[mine, lanes],
            send_sem=a2a_send.at[c], recv_sem=a2a_recv.at[c], device_id=member(peer), device_id_type=MESH,
        )

    halves = (pl.ds(0, HALF), pl.ds(HALF, HALF))

    def s_y(h, d):
        return pltpu.make_async_remote_copy(
            src_ref=sketch.at[z, :, :, halves[h]], dst_ref=recv_s.at[:, t, :, halves[h]],
            send_sem=s_send.at[h, d], recv_sem=s_recv.at[h, d],
            device_id=(dp, (t + 2 * d) % NT), device_id_type=MESH,
        )

    def s_sibling(h, d):
        piece = recv_s.at[:, mod(t - 2 * d, NT), :, halves[h]]
        return pltpu.make_async_remote_copy(
            src_ref=sketch.at[z, :, :, halves[h]] if d == 0 else piece, dst_ref=piece,
            send_sem=s_send.at[h, NT // 2 + d], recv_sem=s_recv.at[h, NT // 2 + d],
            device_id=sibling, device_id_type=MESH,
        )

    def s_forward(h):
        for d in range(1, NT // 2):
            s_y(h, d).wait_recv()
            s_sibling(h, d).start()

    own_s = pltpu.make_async_copy(sketch.at[z], recv_s.at[:, t], local_sem.at[0])
    own_s.start()

    def send(c):
        @pl.loop(1, NM)
        def _(k):
            b_copy(c, k).start()

    grad_in.wait()
    pack(0)
    pl.semaphore_wait(barrier, NM - 1 + NZ - 1)

    for h in range(2):
        for d in range(1, NT // 2):
            s_y(h, d).start()
        s_sibling(h, 0).start()
    send(0)
    pack(1)
    s_forward(0)
    send(1)
    s_forward(1)
    pack(2)
    pack(3)

    own_b = pltpu.make_async_copy(packed.at[m], recv_b.at[mine], local_sem.at[1])
    own_b.start()
    own_b.wait()
    own_s.wait()

    def rows_of(k):
        return pl.ds(near(k) * BLK, BLK)

    chains = ((0, 1, 0, 0), (1, -1, 1, 0), (2, 1, 1, 1), (3, -1, 0, 1))

    def rs_copy(chain, s, src):
        name, way, h, _ = chain
        buf = rup if way == 1 else rdn
        return pltpu.make_async_remote_copy(
            src_ref=src, dst_ref=buf.at[s, :, halves[h]],
            send_sem=rs_send.at[name, s], recv_sem=rs_recv.at[name, s],
            device_id=zup if way == 1 else zdn, device_id_type=MESH,
        )

    def rs_first(chain):
        _, way, h, s = chain
        rs_copy(chain, s, ypart.at[rows_of(way * (8 - s)), halves[h]]).start()

    def rs_step(s):
        for chain in chains:
            _, way, h, first = chain
            rows = rows_of(way * (8 - s))
            if s == first:
                rs_first(chain)
            elif s > first:
                buf = rup if way == 1 else rdn
                slot = buf.at[s - 1, :, halves[h]]
                rs_copy(chain, s - 1, slot).wait_recv()
                buf[s - 1, :, halves[h]] += ypart[rows, halves[h]]
                rs_copy(chain, s, slot).start()

    for c in range(len(STEPS)):
        lanes = pl.ds(PARTS[c], PARTS[c + 1] - PARTS[c])
        await_bytes(recv_b.at[pl.ds(0, (NM - 1) * WIDE), lanes], a2a_recv.at[c])
        if 0 < c < len(STEPS) - 1:
            send(c + 1)
        if c == 0:
            for h in range(2):
                for d in range(NT // 2):
                    s_sibling(h, d).wait_recv()
                ypart[lanes, halves[h]] = lax.dot_general(
                    recv_b[:, lanes], recv_s[:, :, :, halves[h]].reshape(PW, HALF), TDOT,
                    preferred_element_type=F32)
                rs_first(chains[h])
        else:
            ypart[lanes, :] = lax.dot_general(
                recv_b[:, lanes], recv_s[...].reshape(PW, RANK), TDOT, preferred_element_type=F32)
            for s in STEPS[c]:
                rs_step(s)

    own = rows_of(0)

    def ag_copy(chain, s):
        name, way, h, _ = chain
        return pltpu.make_async_remote_copy(
            src_ref=yall.at[rows_of(-way * s), halves[h]], dst_ref=yall.at[rows_of(-way * (s + 1)), halves[h]],
            send_sem=ag_send.at[name, s], recv_sem=ag_recv.at[name, s],
            device_id=zup if way == 1 else zdn, device_id_type=MESH,
        )

    def use(c):
        rows = pl.ds(USES[c], USES[c + 1] - USES[c])
        y = yall[rows, :]
        hi = y.astype(BF16)
        lo = (y - hi.astype(F32)).astype(BF16)
        b = recv_b[:, rows]
        w = jnp.dot(b, hi, preferred_element_type=F32) + jnp.dot(b, lo, preferred_element_type=F32)
        w = w.reshape(NCHIP, 2, WIDE, RANK)
        if c == 3:
            wpart[...] = w
        else:
            wpart[...] += w

    def to_sibling(src, dst, send_sem, recv_sem):
        return pltpu.make_async_remote_copy(
            src_ref=src, dst_ref=dst, send_sem=send_sem, recv_sem=recv_sem, device_id=sibling, device_id_type=MESH)

    g_pair = to_sibling(yall.at[own], ysib, pair_send.at[0], pair_recv.at[0])
    w_pair = to_sibling(wpart.at[:, 1 - core], wsib, pair_send.at[1], pair_recv.at[1])

    def plane_copy(k, src, dst, send_sem, recv_sem):
        return pltpu.make_async_remote_copy(
            src_ref=src, dst_ref=dst, send_sem=send_sem, recv_sem=recv_sem,
            device_id=member(((chip + k) % NCHIP) * 2 + core), device_id_type=MESH)

    def z_copy(k, src, dst, send_sem, recv_sem):
        return pltpu.make_async_remote_copy(
            src_ref=src, dst_ref=dst, send_sem=send_sem, recv_sem=recv_sem,
            device_id=at_z((z + k) % NZ), device_id_type=MESH)

    def gram_1():
        g_pair.start()
        rhs[pl.ds(0, BLK), :] = yall[own, :]
        rhs[pl.ds(BLK, WIDE), :] = jnp.zeros((WIDE, RANK), F32)

    def gram_2():
        g_pair.wait()
        y = jnp.concatenate([yall[own, :], ysib[...]], axis=0)

        def blocks(i, first, count):
            return lax.dot_general(
                y[:, i * NB : (i + 1) * NB], y[:, first * NB : (first + count) * NB], TDOT,
                precision=HIGHEST, preferred_element_type=F32).reshape(NCHIP, GR, count * NB)

        @pl.when(core == 0)
        def _():
            gown[:, :, : 4 * NB] = blocks(0, 0, 4)
            gown[:, :, 4 * NB :] = blocks(1, 1, 1)

        @pl.when(core == 1)
        def _():
            gown[:, :, : 2 * NB] = blocks(1, 2, 2)
            gown[:, :, 2 * NB : 4 * NB] = blocks(2, 2, 2)
            gown[:, :, 4 * NB :] = blocks(3, 3, 1)

        @pl.loop(1, NCHIP)
        def _(k):
            plane_copy(k, gown.at[(chip + k) % NCHIP], grecv.at[chip], g_send, g_recv).start()

        grecv[chip] = gown[chip]

    def gram_3():
        await_bytes(grecv.at[pl.ds(0, NCHIP - 1)], g_recv)
        gzs[...] = jnp.sum(grecv[...], axis=0).reshape(GR, 1, GL)

        @pl.loop(1, NZ)
        def _(k):
            peer = (z + k) % NZ

            @pl.when(peer < GR)
            def _():
                z_copy(k, gzs.at[peer], gzr.at[z], gzs_send, gzs_recv).start()

        @pl.when(z < GR)
        def _():
            gzr[z] = gzs[z]

    def gram_4():
        @pl.when(z < GR)
        def _():
            await_bytes(gzr.at[pl.ds(0, NZ - 1)], gzs_recv)
            gza[z] = jnp.sum(gzr[...], axis=0)

            @pl.loop(1, NZ)
            def _(k):
                z_copy(k, gza.at[z], gza.at[z], gza_send, gza_recv).start()

    def gp_copy(k):
        piece = gall.at[core, chip]
        return plane_copy(k, piece, piece, gp_send.at[k], gp_recv.at[k])

    def gs_copy(k):
        piece = gall.at[core, mod(chip - k, NCHIP)]
        return to_sibling(piece, piece, gs_send.at[k], gs_recv.at[k])

    def gram_5():
        @pl.when(z < GR)
        def _():
            await_bytes(gza.at[pl.ds(0, GR - 1)], gza_recv)

        @pl.when(z >= GR)
        def _():
            await_bytes(gza, gza_recv)

        gall[core, chip] = gza[...].reshape(GR, GL)

        @pl.loop(1, NCHIP)
        def _(k):
            gp_copy(k).start()

        gs_copy(0).start()

    def gram_6():
        @pl.loop(1, NCHIP)
        def _(k):
            piece = gall.at[core, mod(chip - k, NCHIP)]
            plane_copy(k, piece, piece, gp_send.at[k], gp_recv.at[k]).wait_recv()
            gs_copy(k).start()

    def gram_7():
        @pl.loop(0, NCHIP)
        def _(k):
            piece = gall.at[1 - core, mod(chip - k, NCHIP)]
            to_sibling(piece, piece, gs_send.at[k], gs_recv.at[k]).wait_recv()

    def gather_step(s, which):
        for chain in which:
            if s < 8 - chain[3]:
                if s:
                    ag_copy(chain, s - 1).wait_recv()
                ag_copy(chain, s).start()

    def gather_end():
        for chain in chains:
            ag_copy(chain, 7 - chain[3]).wait_recv()

    for h in range(2):
        ends = [chain for chain in chains if chain[2] == h]
        for chain in ends:
            rs_copy(chain, 7, (rup if chain[1] == 1 else rdn).at[7, :, halves[h]]).wait_recv()
        yall[own, halves[h]] = ypart[own, halves[h]] + rup[7, :, halves[h]] + rdn[7, :, halves[h]]
        gather_step(0, ends)
    gram_1()
    one, two = chains[:2], chains[2:]
    gram_2()
    gather_step(1, chains)
    gather_step(2, chains)
    gram_3()
    gather_step(3, chains)
    gram_4()
    gather_step(4, one)
    use(3)
    gather_step(4, two)
    gram_5()
    use(2)
    gather_step(5, chains)
    gram_6()
    gather_step(6, one)
    gram_7()
    gather_step(6, two)
    use(1)

    def w_send_off():
        w_pair.wait()
        wsib[...] += wpart[:, core]

        @pl.loop(1, NCHIP)
        def _(k):
            plane_copy(k, wsib.at[(chip + k) % NCHIP], wrecv.at[chip], w_send, w_recv).start()

        wrecv[chip] = wsib[chip]

    def below(i):
        return pl.ds(i * NB, NB)

    def w_solve():
        await_bytes(wrecv.at[pl.ds(0, NCHIP - 1)], w_recv)
        w = jnp.sum(wrecv[...], axis=0)
        parts = []
        for j in range(RANK // NB):
            part = lax.dot_general(
                w[:, :NB], inverses[j], (((1,), (1,)), ((), ())), precision=HIGHEST, preferred_element_type=F32)
            parts.append(part)
            if j + 1 < RANK // NB:
                w = w[:, NB:] - jnp.dot(
                    part, mat[below(j), (j + 1) * NB : RANK], precision=HIGHEST, preferred_element_type=F32)
        rhs[pl.ds(BLK, WIDE), :] = jnp.concatenate(parts, axis=1)
        solved_w[...] = rhs[...].T

    def at(j, now, work_beside):
        @pl.when(j == now)
        def _():
            work_beside()

    upper_blocks = [gall[i].reshape(NB, GL) for i in range(2)]
    mat[:, :RANK] = jnp.zeros((RANK, RANK), F32)
    mat[below(0), :RANK] = upper_blocks[0][:, :RANK]
    mat[below(1), NB : 2 * NB] = upper_blocks[0][:, RANK:]
    mat[below(1), 2 * NB : RANK] = upper_blocks[1][:, : 2 * NB]
    mat[below(2), 2 * NB : RANK] = upper_blocks[1][:, 2 * NB : 4 * NB]
    mat[below(3), 3 * NB : RANK] = upper_blocks[1][:, 4 * NB :]
    mat[:, RANK:] = rhs[...].T

    @pl.loop(0, RANK // NB)
    def _(j):
        rows = pl.ds(pl.multiple_of(j * NB, NB), NB)
        work[...] = mat[rows, rows]
        at(j, 1, lambda: gather_step(7, chains))

        def last_of_w():
            gather_end()
            use(0)
            w_pair.start()

        at(j, 2, last_of_w)

        def halfway():
            at(j, 2, w_send_off)

        invert_factor(work, halfway)

        row = lax.broadcasted_iota(jnp.int32, (NB, NB), 0)
        lane = lax.broadcasted_iota(jnp.int32, (NB, NB), 1)
        inverse = jnp.where(lane <= row, work[...], 0.0)
        inverses[j] = inverse
        upper = jnp.dot(inverse, mat[rows, :], precision=HIGHEST, preferred_element_type=F32)
        mat[rows, :] = upper
        solved[rows, :] = upper[:, RANK:]
        for i in range(1, RANK // NB):
            @pl.when(i > j)
            def _():
                mat[below(i), :] -= lax.dot_general(
                    upper[:, i * NB : (i + 1) * NB], upper, TDOT, precision=HIGHEST, preferred_element_type=F32)

    w_solve()

    packed_p = jnp.zeros((N_DP, NB), F32)
    lane = lax.broadcasted_iota(jnp.int32, (N_DP, NB), 1)
    for r in range(PER_DP):
        part = solved_w[pl.ds(r, N_DP, stride=PER_DP), :]
        slot = PER_DP - 1 - r
        packed_p = jnp.where(lane // WIDE == slot, pltpu.roll(part, (WIDE * slot - BLK) % NB, 1), packed_p)
    outbox[...] = packed_p.reshape(NZ, NX, 1, NB)

    def x_copy(k):
        peer = (x + k) % NX
        return pltpu.make_async_remote_copy(
            src_ref=outbox.at[:, peer], dst_ref=inbox_x.at[x], send_sem=x_send.at[k], recv_sem=x_recv.at[k],
            device_id=(z * NX + peer, t), device_id_type=MESH,
        )

    for k in range(1, NX):
        x_copy(k).start()
    inbox_x[x] = outbox[:, x]
    basis_out[...] = (solved[...].T[:BLK] * math.sqrt(ROWS)).astype(BF16)
    for k in range(1, NX):
        x_copy(k).wait()

    @pl.loop(1, NZ)
    def _(k):
        z_copy(k, inbox_x.at[:, (z + k) % NZ], inbox_z.at[z], z_send, z_recv).start()

    inbox_z[z] = inbox_x[:, z]

    for h in range(2):
        for d in range(NT // 2):
            s_sibling(h, d).wait_send()
        for d in range(1, NT // 2):
            s_y(h, d).wait_send()

    for ref, sem in (
        (grecv.at[pl.ds(0, NCHIP - 1)], g_send), (wrecv.at[pl.ds(0, NCHIP - 1)], w_send),
    ):
        await_bytes(ref, sem)

    @pl.when(z < GR)
    def _():
        await_bytes(gza.at[pl.ds(0, GR - 1)], gzs_send)
        await_bytes(gzr.at[pl.ds(0, NZ - 1)], gza_send)

    @pl.when(z >= GR)
    def _():
        await_bytes(gza, gzs_send)

    @pl.loop(0, NCHIP)
    def _(k):
        gs_copy(k).wait_send()

    @pl.loop(1, NCHIP)
    def _(k):
        gp_copy(k).wait_send()

    for c in range(len(STEPS)):
        await_bytes(recv_b.at[pl.ds(0, (NM - 1) * WIDE), pl.ds(PARTS[c], PARTS[c + 1] - PARTS[c])], a2a_send.at[c])
    for chain in chains:
        _, way, h, first = chain
        for s in range(first, 8):
            rs_copy(chain, s, (rup if way == 1 else rdn).at[s, :, halves[h]]).wait_send()
        for s in range(0, 8 - first):
            ag_copy(chain, s).wait_send()

    await_bytes(inbox_z.at[pl.ds(0, NZ - 1)], z_send)
    await_bytes(inbox_z.at[pl.ds(0, NZ - 1)], z_recv)
    per_tile = NB // WIDE
    lane = lax.broadcasted_iota(jnp.int32, (PER_DP, NB), 1)
    for q in range(N_DP // per_tile):
        tile = jnp.zeros((PER_DP, NB), F32)
        for i in range(per_tile):
            src = q * per_tile + i
            line = jnp.broadcast_to(inbox_z[src // NX, src % NX], (PER_DP, NB))
            line = pltpu.roll(line, 0, 1, stride=WIDE, stride_axis=0)
            line = pltpu.roll(line, (WIDE * (i + 1)) % NB, 1)
            tile = jnp.where(lane // WIDE == i, line, tile)
        proj_out[:, q * NB : (q + 1) * NB] = tile.astype(BF16)


def project(grad_buckets, sketch):
    vmem = pl.BlockSpec(memory_space=pltpu.VMEM)
    dma = pltpu.SemaphoreType.DMA
    return pl.pallas_call(
        kernel,
        out_shape=(
            jax.ShapeDtypeStruct((BLK, RANK), BF16),
            jax.ShapeDtypeStruct((PER_DP, N_DP * WIDE), BF16),
        ),
        in_specs=[pl.BlockSpec(memory_space=pl.ANY)] * 2,
        out_specs=(vmem, vmem),
        scratch_shapes=[
            pltpu.VMEM((WIDE, ROWS), BF16),
            pltpu.VMEM((NM, WIDE, COLS), BF16),
            pltpu.VMEM((PW, COLS), BF16),
            pltpu.VMEM((NX, NT, WIDE, RANK), BF16),
            pltpu.VMEM((COLS, RANK), F32),
            pltpu.VMEM((COLS, RANK), F32),
            pltpu.VMEM((8, BLK, RANK), F32),
            pltpu.VMEM((8, BLK, RANK), F32),
            pltpu.VMEM((NCHIP, 2, WIDE, RANK), F32),
            pltpu.VMEM((NCHIP, WIDE, RANK), F32),
            pltpu.VMEM((NCHIP, WIDE, RANK), F32),
            pltpu.VMEM((BLK, RANK), F32),
            pltpu.VMEM((NCHIP, GR, GL), F32),
            pltpu.VMEM((NCHIP, GR, GL), F32),
            pltpu.VMEM((GR, 1, GL), F32),
            pltpu.VMEM((NZ, 1, GL), F32),
            pltpu.VMEM((GR, 1, GL), F32),
            pltpu.VMEM((2, NCHIP, GR, GL), F32),
            pltpu.VMEM((BLK + WIDE, RANK), F32),
            pltpu.VMEM((RANK, RANK + NB), F32),
            pltpu.VMEM((NB, NB), F32),
            pltpu.VMEM((RANK // NB, NB, NB), F32),
            pltpu.VMEM((RANK, NB), F32),
            pltpu.VMEM((RANK, NB), F32),
            pltpu.VMEM((NZ, NX, 1, NB), F32),
            pltpu.VMEM((NX, NZ, 1, NB), F32),
            pltpu.VMEM((NZ, NX, 1, NB), F32),
            dma((3,)),
            dma((len(STEPS),)), dma((len(STEPS),)),
            dma((2, NT)), dma((2, NT)),
            dma((4, 8)), dma((4, 8)),
            dma((4, 8)), dma((4, 8)),
            dma((2,)), dma((2,)),
            dma, dma, dma, dma, dma, dma, dma, dma,
            dma((NCHIP,)), dma((NCHIP,)),
            dma((NCHIP,)), dma((NCHIP,)),
            dma((NX,)), dma((NX,)),
            dma, dma,
        ],
        compiler_params=pltpu.CompilerParams(
            collective_id=0, has_side_effects=True, vmem_limit_bytes=56 * 1024 * 1024),
    )(grad_buckets, sketch)


def shards(grad_buckets, sketch):
    basis, projected = project(grad_buckets, sketch.reshape(NZ, NX, WIDE, RANK))
    return basis.T, projected


def solution(mesh):
    in_specs = (P(("tensor", "dp"), None), P("tensor", None))
    out_specs = (P(None, ("dp", "tensor")), P("dp", "tensor"))
    return jax.shard_map(shards, mesh=mesh, in_specs=in_specs, out_specs=out_specs, check_vma=False)
```

```python
import math

import jax
import jax.numpy as jnp
from jax import lax
from jax.experimental import pallas as pl
from jax.experimental.pallas import tpu as pltpu
from jax.sharding import PartitionSpec as P

MESH = pl.DeviceIdType.MESH
F32 = jnp.float32
BF16 = jnp.bfloat16
NZ, NX, NT = 16, 4, 8
NM = NX * NT
NCHIP = NM // 2
ROWS = 57344
RANK = 512
WIDE = 16
BLK = ROWS // (NZ * NM)
COLS = BLK * NZ
PW = WIDE * NM
HALF = RANK // 2
PARTS = (0, 128, 384, 896, 1280, 1792)
STEPS = ((0,), (1,), (2, 3), (4, 5), (6, 7))
USES = (0, 384, 896, 1280, 1792)
N_DP = NZ * NX
PER_DP = RANK // N_DP
NB = 128
GROUP = 8
GR, GL = 8, 640
HIGHEST = lax.Precision.HIGHEST
TDOT = (((0,), (0,)), ((), ()))


def mod(a, n):
    return lax.rem(a + n, n)


def near(k):
    if k == 0:
        return NZ - 1
    if abs(k) == NZ // 2:
        return 0
    return NZ - 1 - 2 * k if k > 0 else NZ + 2 * k


ORDER = sorted(range(1 - NZ // 2, NZ // 2 + 1), key=near)


def far_first(i):
    return NZ // 2 + (i // 2) * (2 * (i % 2) - 1)


def await_bytes(ref, sem):
    pltpu.make_async_copy(ref, ref, sem).wait()


def invert_factor(work, halfway):
    for s in range(0, NB, GROUP):
        if s == NB // 2:
            halfway()
        n = NB - s
        row = lax.broadcasted_iota(jnp.int32, (GROUP, NB), 0)
        lane = lax.broadcasted_iota(jnp.int32, (GROUP, NB), 1)
        rest = work[s:, :]
        cols = [jnp.broadcast_to(rest[:, s + k : s + k + 1], (n, NB)) for k in range(GROUP)]
        top = jnp.where((lane >= s) & (lane < s + GROUP), jnp.where(lane - s == row, 1.0, 0.0), rest[:GROUP])
        below = rest[GROUP:]
        if n > GROUP:
            lane_b = lax.broadcasted_iota(jnp.int32, (n - GROUP, NB), 1)
            below = jnp.where((lane_b >= s) & (lane_b < s + GROUP), 0.0, below)
        for k in range(GROUP):
            r = lax.rsqrt(jnp.broadcast_to(cols[k][k : k + 1], (GROUP, NB)))
            mult = cols[k] * jnp.broadcast_to(r[:1], (n, NB))
            for q in range(k + 1, GROUP):
                cols[q] = cols[q] - mult * jnp.broadcast_to(mult[q : q + 1], (n, NB))
            u = jnp.broadcast_to(top[k : k + 1], (GROUP, NB)) * r
            top = jnp.where(row == k, u, jnp.where(row > k, top - mult[:GROUP] * u, top))
            if n > GROUP:
                below = below - mult[GROUP:] * jnp.broadcast_to(u[:1], (n - GROUP, NB))
        work[s : s + GROUP, :] = top
        if n > GROUP:
            work[s + GROUP :, :] = below


def kernel(
    grad_hbm, sketch, basis_out, proj_out,
    grad, packed, recv_b, recv_s, ypart, yall, rup, rdn, wpart, wsib, wrecv,
    ysib, gown, grecv, gzs, gzr, gza, gall, rhs, mat, work, inverses, solved, solved_w, outbox, inbox_x, inbox_z,
    local_sem, a2a_send, a2a_recv, s_send, s_recv, rs_send, rs_recv, ag_send, ag_recv,
    pair_send, pair_recv, w_send, w_recv, g_send, g_recv, gzs_send, gzs_recv, gza_send, gza_recv,
    gp_send, gp_recv, gs_send, gs_recv, x_send, x_recv, z_send, z_recv,
):
    dp = lax.axis_index("dp")
    t = lax.axis_index("tensor")
    z = dp // NX
    x = dp % NX
    m = x * NT + t
    chip = m // 2
    core = m % 2

    def member(i):
        return (z * NX + i // NT, i % NT)

    def at_z(i):
        return (i * NX + x, t)

    zup, zdn = at_z(mod(z + 1, NZ)), at_z(mod(z - 1, NZ))
    sibling = (dp, t + 1 - 2 * core)

    grad_in = pltpu.make_async_copy(grad_hbm, grad, local_sem.at[2])
    grad_in.start()

    barrier = pltpu.get_barrier_semaphore()

    @pl.loop(1, NM)
    def _(k):
        pl.semaphore_signal(barrier, inc=1, device_id=member((m + k) % NM), device_id_type=MESH)

    @pl.loop(1, NZ)
    def _(k):
        pl.semaphore_signal(barrier, inc=1, device_id=at_z((z + k) % NZ), device_id_type=MESH)

    mine = pl.ds(pl.multiple_of(m * WIDE, WIDE), WIDE)

    def pack(c):
        @pl.loop(0, NM // 8)
        def _(q):
            for place in range(4 * c, 4 * c + 4):
                first = ((z + ORDER[place] + NZ) % NZ) * (NM * BLK) + q * (8 * BLK)
                part = grad[:, pl.ds(pl.multiple_of(first, 128), 8 * BLK)]
                for i in range(8):
                    packed[q * 8 + i, :, place * BLK : (place + 1) * BLK] = part[:, i * BLK : (i + 1) * BLK]

    def b_copy(c, k):
        peer = (m + k) % NM
        lanes = pl.ds(PARTS[c], PARTS[c + 1] - PARTS[c])
        return pltpu.make_async_remote_copy(
            src_ref=packed.at[peer, :, lanes], dst_ref=recv_b.at[mine, lanes],
            send_sem=a2a_send.at[c], recv_sem=a2a_recv.at[c], device_id=member(peer), device_id_type=MESH,
        )

    halves = (pl.ds(0, HALF), pl.ds(HALF, HALF))

    def s_y(h, d):
        return pltpu.make_async_remote_copy(
            src_ref=sketch.at[z, :, :, halves[h]], dst_ref=recv_s.at[:, t, :, halves[h]],
            send_sem=s_send.at[h, d], recv_sem=s_recv.at[h, d],
            device_id=(dp, (t + 2 * d) % NT), device_id_type=MESH,
        )

    def s_sibling(h, d):
        piece = recv_s.at[:, mod(t - 2 * d, NT), :, halves[h]]
        return pltpu.make_async_remote_copy(
            src_ref=sketch.at[z, :, :, halves[h]] if d == 0 else piece, dst_ref=piece,
            send_sem=s_send.at[h, NT // 2 + d], recv_sem=s_recv.at[h, NT // 2 + d],
            device_id=sibling, device_id_type=MESH,
        )

    def s_forward(h):
        for d in range(1, NT // 2):
            s_y(h, d).wait_recv()
            s_sibling(h, d).start()

    own_s = pltpu.make_async_copy(sketch.at[z], recv_s.at[:, t], local_sem.at[0])
    own_s.start()

    def send(c):
        @pl.loop(1, NM)
        def _(k):
            b_copy(c, k).start()

    grad_in.wait()
    pack(0)
    pl.semaphore_wait(barrier, NM - 1 + NZ - 1)

    for h in range(2):
        for d in range(1, NT // 2):
            s_y(h, d).start()
        s_sibling(h, 0).start()
    send(0)
    pack(1)
    s_forward(0)
    send(1)
    s_forward(1)
    pack(2)
    pack(3)

    own_b = pltpu.make_async_copy(packed.at[m], recv_b.at[mine], local_sem.at[1])
    own_b.start()
    own_b.wait()
    own_s.wait()

    def rows_of(k):
        return pl.ds(near(k) * BLK, BLK)

    chains = ((0, 1, 0, 0), (1, -1, 1, 0), (2, 1, 1, 1), (3, -1, 0, 1))

    def rs_copy(chain, s, src):
        name, way, h, _ = chain
        buf = rup if way == 1 else rdn
        return pltpu.make_async_remote_copy(
            src_ref=src, dst_ref=buf.at[s, :, halves[h]],
            send_sem=rs_send.at[name, s], recv_sem=rs_recv.at[name, s],
            device_id=zup if way == 1 else zdn, device_id_type=MESH,
        )

    def rs_first(chain):
        _, way, h, s = chain
        rs_copy(chain, s, ypart.at[rows_of(way * (8 - s)), halves[h]]).start()

    def rs_step(s):
        for chain in chains:
            _, way, h, first = chain
            rows = rows_of(way * (8 - s))
            if s == first:
                rs_first(chain)
            elif s > first:
                buf = rup if way == 1 else rdn
                slot = buf.at[s - 1, :, halves[h]]
                rs_copy(chain, s - 1, slot).wait_recv()
                buf[s - 1, :, halves[h]] += ypart[rows, halves[h]]
                rs_copy(chain, s, slot).start()

    for c in range(len(STEPS)):
        lanes = pl.ds(PARTS[c], PARTS[c + 1] - PARTS[c])
        await_bytes(recv_b.at[pl.ds(0, (NM - 1) * WIDE), lanes], a2a_recv.at[c])
        if 0 < c < len(STEPS) - 1:
            send(c + 1)
        if c == 0:
            for h in range(2):
                for d in range(NT // 2):
                    s_sibling(h, d).wait_recv()
                ypart[lanes, halves[h]] = lax.dot_general(
                    recv_b[:, lanes], recv_s[:, :, :, halves[h]].reshape(PW, HALF), TDOT,
                    preferred_element_type=F32)
                rs_first(chains[h])
        else:
            ypart[lanes, :] = lax.dot_general(
                recv_b[:, lanes], recv_s[...].reshape(PW, RANK), TDOT, preferred_element_type=F32)
            for s in STEPS[c]:
                rs_step(s)

    own = rows_of(0)

    def ag_copy(chain, s):
        name, way, h, _ = chain
        return pltpu.make_async_remote_copy(
            src_ref=yall.at[rows_of(-way * s), halves[h]], dst_ref=yall.at[rows_of(-way * (s + 1)), halves[h]],
            send_sem=ag_send.at[name, s], recv_sem=ag_recv.at[name, s],
            device_id=zup if way == 1 else zdn, device_id_type=MESH,
        )

    def use(c):
        rows = pl.ds(USES[c], USES[c + 1] - USES[c])
        y = yall[rows, :]
        hi = y.astype(BF16)
        lo = (y - hi.astype(F32)).astype(BF16)
        b = recv_b[:, rows]
        w = jnp.dot(b, hi, preferred_element_type=F32) + jnp.dot(b, lo, preferred_element_type=F32)
        w = w.reshape(NCHIP, 2, WIDE, RANK)
        if c == 3:
            wpart[...] = w
        else:
            wpart[...] += w

    def to_sibling(src, dst, send_sem, recv_sem):
        return pltpu.make_async_remote_copy(
            src_ref=src, dst_ref=dst, send_sem=send_sem, recv_sem=recv_sem, device_id=sibling, device_id_type=MESH)

    g_pair = to_sibling(yall.at[own], ysib, pair_send.at[0], pair_recv.at[0])
    w_pair = to_sibling(wpart.at[:, 1 - core], wsib, pair_send.at[1], pair_recv.at[1])

    def plane_copy(k, src, dst, send_sem, recv_sem):
        return pltpu.make_async_remote_copy(
            src_ref=src, dst_ref=dst, send_sem=send_sem, recv_sem=recv_sem,
            device_id=member(((chip + k) % NCHIP) * 2 + core), device_id_type=MESH)

    def z_copy(k, src, dst, send_sem, recv_sem):
        return pltpu.make_async_remote_copy(
            src_ref=src, dst_ref=dst, send_sem=send_sem, recv_sem=recv_sem,
            device_id=at_z((z + k) % NZ), device_id_type=MESH)

    def gram_1():
        g_pair.start()
        rhs[pl.ds(0, BLK), :] = yall[own, :]
        rhs[pl.ds(BLK, WIDE), :] = jnp.zeros((WIDE, RANK), F32)

    def gram_2():
        g_pair.wait()
        y = jnp.concatenate([yall[own, :], ysib[...]], axis=0)

        def blocks(i, first, count):
            return lax.dot_general(
                y[:, i * NB : (i + 1) * NB], y[:, first * NB : (first + count) * NB], TDOT,
                precision=HIGHEST, preferred_element_type=F32).reshape(NCHIP, GR, count * NB)

        @pl.when(core == 0)
        def _():
            gown[:, :, : 4 * NB] = blocks(0, 0, 4)
            gown[:, :, 4 * NB :] = blocks(1, 1, 1)

        @pl.when(core == 1)
        def _():
            gown[:, :, : 2 * NB] = blocks(1, 2, 2)
            gown[:, :, 2 * NB : 4 * NB] = blocks(2, 2, 2)
            gown[:, :, 4 * NB :] = blocks(3, 3, 1)

        @pl.loop(1, NCHIP)
        def _(k):
            plane_copy(k, gown.at[(chip + k) % NCHIP], grecv.at[chip], g_send, g_recv).start()

        grecv[chip] = gown[chip]

    def left_early():
        for h in range(2):
            for d in range(NT // 2):
                s_sibling(h, d).wait_send()
            for d in range(1, NT // 2):
                s_y(h, d).wait_send()
        for c in range(len(STEPS)):
            await_bytes(recv_b.at[pl.ds(0, (NM - 1) * WIDE), pl.ds(PARTS[c], PARTS[c + 1] - PARTS[c])], a2a_send.at[c])
        for chain in chains:
            for s in range(chain[3], 8):
                rs_copy(chain, s, (rup if chain[1] == 1 else rdn).at[s, :, halves[chain[2]]]).wait_send()

    def left_late():
        for ref, sem in (
            (grecv.at[pl.ds(0, NCHIP - 1)], g_send), (wrecv.at[pl.ds(0, NCHIP - 1)], w_send),
        ):
            await_bytes(ref, sem)

        @pl.when(z < GR)
        def _():
            await_bytes(gza.at[pl.ds(0, GR - 1)], gzs_send)
            await_bytes(gzr.at[pl.ds(0, NZ - 1)], gza_send)

        @pl.when(z >= GR)
        def _():
            await_bytes(gza, gzs_send)

        @pl.loop(0, NCHIP)
        def _(k):
            gs_copy(k).wait_send()

        @pl.loop(1, NCHIP)
        def _(k):
            gp_copy(k).wait_send()

        for chain in chains:
            for s in range(0, 8 - chain[3]):
                ag_copy(chain, s).wait_send()

    def gram_3():
        await_bytes(grecv.at[pl.ds(0, NCHIP - 1)], g_recv)
        gzs[...] = jnp.sum(grecv[...], axis=0).reshape(GR, 1, GL)

        @pl.loop(1, NZ)
        def _(i):
            k = far_first(i)
            peer = (z + k) % NZ

            @pl.when(peer < GR)
            def _():
                z_copy(k, gzs.at[peer], gzr.at[z], gzs_send, gzs_recv).start()

        @pl.when(z < GR)
        def _():
            gzr[z] = gzs[z]

    def gram_4():
        @pl.when(z < GR)
        def _():
            await_bytes(gzr.at[pl.ds(0, NZ - 1)], gzs_recv)
            gza[z] = jnp.sum(gzr[...], axis=0)

            @pl.loop(1, NZ)
            def _(i):
                k = far_first(i)
                z_copy(k, gza.at[z], gza.at[z], gza_send, gza_recv).start()

    def gp_copy(k):
        piece = gall.at[core, chip]
        return plane_copy(k, piece, piece, gp_send.at[k], gp_recv.at[k])

    def gs_copy(k):
        piece = gall.at[core, mod(chip - k, NCHIP)]
        return to_sibling(piece, piece, gs_send.at[k], gs_recv.at[k])

    def gram_5():
        @pl.when(z < GR)
        def _():
            await_bytes(gza.at[pl.ds(0, GR - 1)], gza_recv)

        @pl.when(z >= GR)
        def _():
            await_bytes(gza, gza_recv)

        gall[core, chip] = gza[...].reshape(GR, GL)

        @pl.loop(1, NCHIP)
        def _(k):
            gp_copy(k).start()

        gs_copy(0).start()

    def gram_6():
        @pl.loop(1, NCHIP)
        def _(k):
            piece = gall.at[core, mod(chip - k, NCHIP)]
            plane_copy(k, piece, piece, gp_send.at[k], gp_recv.at[k]).wait_recv()
            gs_copy(k).start()

    def gram_7():
        @pl.loop(0, NCHIP)
        def _(k):
            piece = gall.at[1 - core, mod(chip - k, NCHIP)]
            to_sibling(piece, piece, gs_send.at[k], gs_recv.at[k]).wait_recv()

    def gather_step(s, which):
        for chain in which:
            if s < 8 - chain[3]:
                if s:
                    ag_copy(chain, s - 1).wait_recv()
                ag_copy(chain, s).start()

    def gather_end():
        for chain in chains:
            ag_copy(chain, 7 - chain[3]).wait_recv()

    for h in range(2):
        ends = [chain for chain in chains if chain[2] == h]
        for chain in ends:
            rs_copy(chain, 7, (rup if chain[1] == 1 else rdn).at[7, :, halves[h]]).wait_recv()
        yall[own, halves[h]] = ypart[own, halves[h]] + rup[7, :, halves[h]] + rdn[7, :, halves[h]]
        gather_step(0, ends)
    gram_1()
    one, two = chains[:2], chains[2:]
    gram_2()
    gather_step(1, chains)
    left_early()
    gather_step(2, chains)
    gram_3()
    gather_step(3, chains)
    gram_4()
    gather_step(4, one)
    use(3)
    gather_step(4, two)
    gram_5()
    use(2)
    gather_step(5, chains)
    gram_6()
    gather_step(6, one)
    gram_7()
    gather_step(6, two)
    use(1)

    def w_send_off():
        w_pair.wait()
        wsib[...] += wpart[:, core]

        @pl.loop(1, NCHIP)
        def _(k):
            plane_copy(k, wsib.at[(chip + k) % NCHIP], wrecv.at[chip], w_send, w_recv).start()

        wrecv[chip] = wsib[chip]

    def below(i):
        return pl.ds(i * NB, NB)

    def w_solve():
        await_bytes(wrecv.at[pl.ds(0, NCHIP - 1)], w_recv)
        w = jnp.sum(wrecv[...], axis=0)
        parts = []
        for j in range(RANK // NB):
            part = lax.dot_general(
                w[:, :NB], inverses[j], (((1,), (1,)), ((), ())), precision=HIGHEST, preferred_element_type=F32)
            parts.append(part)
            if j + 1 < RANK // NB:
                w = w[:, NB:] - jnp.dot(
                    part, mat[below(j), (j + 1) * NB : RANK], precision=HIGHEST, preferred_element_type=F32)
        rhs[pl.ds(BLK, WIDE), :] = jnp.concatenate(parts, axis=1)
        solved_w[...] = rhs[...].T

    def at(j, now, work_beside):
        @pl.when(j == now)
        def _():
            work_beside()

    upper_blocks = [gall[i].reshape(NB, GL) for i in range(2)]
    mat[:, :RANK] = jnp.zeros((RANK, RANK), F32)
    mat[below(0), :RANK] = upper_blocks[0][:, :RANK]
    mat[below(1), NB : 2 * NB] = upper_blocks[0][:, RANK:]
    mat[below(1), 2 * NB : RANK] = upper_blocks[1][:, : 2 * NB]
    mat[below(2), 2 * NB : RANK] = upper_blocks[1][:, 2 * NB : 4 * NB]
    mat[below(3), 3 * NB : RANK] = upper_blocks[1][:, 4 * NB :]
    mat[:, RANK:] = rhs[...].T

    @pl.loop(0, RANK // NB)
    def _(j):
        rows = pl.ds(pl.multiple_of(j * NB, NB), NB)
        work[...] = mat[rows, rows]
        at(j, 1, lambda: gather_step(7, chains))

        def last_of_w():
            gather_end()
            use(0)
            w_pair.start()

        at(j, 2, last_of_w)

        def halfway():
            at(j, 2, w_send_off)

        invert_factor(work, halfway)

        row = lax.broadcasted_iota(jnp.int32, (NB, NB), 0)
        lane = lax.broadcasted_iota(jnp.int32, (NB, NB), 1)
        inverse = jnp.where(lane <= row, work[...], 0.0)
        inverses[j] = inverse
        upper = jnp.dot(inverse, mat[rows, :], precision=HIGHEST, preferred_element_type=F32)
        mat[rows, :] = upper
        solved[rows, :] = upper[:, RANK:]
        for i in range(1, RANK // NB):
            @pl.when(i > j)
            def _():
                mat[below(i), :] -= lax.dot_general(
                    upper[:, i * NB : (i + 1) * NB], upper, TDOT, precision=HIGHEST, preferred_element_type=F32)

    basis_out[...] = (solved[...].T[:BLK] * math.sqrt(ROWS)).astype(BF16)
    left_late()
    w_solve()

    packed_p = jnp.zeros((N_DP, NB), F32)
    lane = lax.broadcasted_iota(jnp.int32, (N_DP, NB), 1)
    for r in range(PER_DP):
        part = solved_w[pl.ds(r, N_DP, stride=PER_DP), :]
        slot = PER_DP - 1 - r
        packed_p = jnp.where(lane // WIDE == slot, pltpu.roll(part, (WIDE * slot - BLK) % NB, 1), packed_p)
    outbox[...] = packed_p.reshape(NZ, NX, 1, NB)

    def x_copy(k):
        peer = (x + k) % NX
        return pltpu.make_async_remote_copy(
            src_ref=outbox.at[:, peer], dst_ref=inbox_x.at[x], send_sem=x_send.at[k], recv_sem=x_recv.at[k],
            device_id=(z * NX + peer, t), device_id_type=MESH,
        )

    for k in range(1, NX):
        x_copy(k).start()
    inbox_x[x] = outbox[:, x]
    for k in range(1, NX):
        x_copy(k).wait()

    @pl.loop(1, NZ)
    def _(i):
        k = far_first(i)
        z_copy(k, inbox_x.at[:, (z + k) % NZ], inbox_z.at[z], z_send, z_recv).start()

    inbox_z[z] = inbox_x[:, z]

    await_bytes(inbox_z.at[pl.ds(0, NZ - 1)], z_send)
    await_bytes(inbox_z.at[pl.ds(0, NZ - 1)], z_recv)
    per_tile = NB // WIDE
    lane = lax.broadcasted_iota(jnp.int32, (PER_DP, NB), 1)
    for q in range(N_DP // per_tile):
        tile = jnp.zeros((PER_DP, NB), F32)
        for i in range(per_tile):
            src = q * per_tile + i
            line = jnp.broadcast_to(inbox_z[src // NX, src % NX], (PER_DP, NB))
            line = pltpu.roll(line, 0, 1, stride=WIDE, stride_axis=0)
            line = pltpu.roll(line, (WIDE * (i + 1)) % NB, 1)
            tile = jnp.where(lane // WIDE == i, line, tile)
        proj_out[:, q * NB : (q + 1) * NB] = tile.astype(BF16)


def project(grad_buckets, sketch):
    vmem = pl.BlockSpec(memory_space=pltpu.VMEM)
    dma = pltpu.SemaphoreType.DMA
    return pl.pallas_call(
        kernel,
        out_shape=(
            jax.ShapeDtypeStruct((BLK, RANK), BF16),
            jax.ShapeDtypeStruct((PER_DP, N_DP * WIDE), BF16),
        ),
        in_specs=[pl.BlockSpec(memory_space=pl.ANY)] * 2,
        out_specs=(vmem, vmem),
        scratch_shapes=[
            pltpu.VMEM((WIDE, ROWS), BF16),
            pltpu.VMEM((NM, WIDE, COLS), BF16),
            pltpu.VMEM((PW, COLS), BF16),
            pltpu.VMEM((NX, NT, WIDE, RANK), BF16),
            pltpu.VMEM((COLS, RANK), F32),
            pltpu.VMEM((COLS, RANK), F32),
            pltpu.VMEM((8, BLK, RANK), F32),
            pltpu.VMEM((8, BLK, RANK), F32),
            pltpu.VMEM((NCHIP, 2, WIDE, RANK), F32),
            pltpu.VMEM((NCHIP, WIDE, RANK), F32),
            pltpu.VMEM((NCHIP, WIDE, RANK), F32),
            pltpu.VMEM((BLK, RANK), F32),
            pltpu.VMEM((NCHIP, GR, GL), F32),
            pltpu.VMEM((NCHIP, GR, GL), F32),
            pltpu.VMEM((GR, 1, GL), F32),
            pltpu.VMEM((NZ, 1, GL), F32),
            pltpu.VMEM((GR, 1, GL), F32),
            pltpu.VMEM((2, NCHIP, GR, GL), F32),
            pltpu.VMEM((BLK + WIDE, RANK), F32),
            pltpu.VMEM((RANK, RANK + NB), F32),
            pltpu.VMEM((NB, NB), F32),
            pltpu.VMEM((RANK // NB, NB, NB), F32),
            pltpu.VMEM((RANK, NB), F32),
            pltpu.VMEM((RANK, NB), F32),
            pltpu.VMEM((NZ, NX, 1, NB), F32),
            pltpu.VMEM((NX, NZ, 1, NB), F32),
            pltpu.VMEM((NZ, NX, 1, NB), F32),
            dma((3,)),
            dma((len(STEPS),)), dma((len(STEPS),)),
            dma((2, NT)), dma((2, NT)),
            dma((4, 8)), dma((4, 8)),
            dma((4, 8)), dma((4, 8)),
            dma((2,)), dma((2,)),
            dma, dma, dma, dma, dma, dma, dma, dma,
            dma((NCHIP,)), dma((NCHIP,)),
            dma((NCHIP,)), dma((NCHIP,)),
            dma((NX,)), dma((NX,)),
            dma, dma,
        ],
        compiler_params=pltpu.CompilerParams(
            collective_id=0, has_side_effects=True, vmem_limit_bytes=56 * 1024 * 1024),
    )(grad_buckets, sketch)


def shards(grad_buckets, sketch):
    basis, projected = project(grad_buckets, sketch.reshape(NZ, NX, WIDE, RANK))
    return basis.T, projected


def solution(mesh):
    in_specs = (P(("tensor", "dp"), None), P("tensor", None))
    out_specs = (P(None, ("dp", "tensor")), P("dp", "tensor"))
    return jax.shard_map(shards, mesh=mesh, in_specs=in_specs, out_specs=out_specs, check_vma=False)
```

```python
import math

import jax
import jax.numpy as jnp
from jax import lax
from jax.experimental import pallas as pl
from jax.experimental.pallas import tpu as pltpu
from jax.sharding import PartitionSpec as P

MESH = pl.DeviceIdType.MESH
F32 = jnp.float32
BF16 = jnp.bfloat16
NZ, NX, NT = 16, 4, 8
NM = NX * NT
NCHIP = NM // 2
ROWS = 57344
RANK = 512
WIDE = 16
BLK = ROWS // (NZ * NM)
COLS = BLK * NZ
PW = WIDE * NM
HALF = RANK // 2
PARTS = (0, 128, 384, 896, 1280, 1792)
STEPS = ((0,), (1,), (2, 3), (4, 5), (6, 7))
USES = (0, 384, 896, 1280, 1792)
N_DP = NZ * NX
PER_DP = RANK // N_DP
NB = 128
GROUP = 8
GR, GL = 8, 640
HIGHEST = lax.Precision.HIGHEST
TDOT = (((0,), (0,)), ((), ()))


def mod(a, n):
    return lax.rem(a + n, n)


def near(k):
    if k == 0:
        return NZ - 1
    if abs(k) == NZ // 2:
        return 0
    return NZ - 1 - 2 * k if k > 0 else NZ + 2 * k


ORDER = sorted(range(1 - NZ // 2, NZ // 2 + 1), key=near)


def far_first(i):
    return NZ // 2 + (i // 2) * (2 * (i % 2) - 1)


def await_bytes(ref, sem):
    pltpu.make_async_copy(ref, ref, sem).wait()


def invert_factor(work, halfway):
    for s in range(0, NB, GROUP):
        if s == NB // 2:
            halfway()
        n = NB - s
        row = lax.broadcasted_iota(jnp.int32, (GROUP, NB), 0)
        lane = lax.broadcasted_iota(jnp.int32, (GROUP, NB), 1)
        rest = work[s:, :]
        cols = [jnp.broadcast_to(rest[:, s + k : s + k + 1], (n, NB)) for k in range(GROUP)]
        top = jnp.where((lane >= s) & (lane < s + GROUP), jnp.where(lane - s == row, 1.0, 0.0), rest[:GROUP])
        below = rest[GROUP:]
        if n > GROUP:
            lane_b = lax.broadcasted_iota(jnp.int32, (n - GROUP, NB), 1)
            below = jnp.where((lane_b >= s) & (lane_b < s + GROUP), 0.0, below)
        for k in range(GROUP):
            r = lax.rsqrt(jnp.broadcast_to(cols[k][k : k + 1], (GROUP, NB)))
            mult = cols[k] * jnp.broadcast_to(r[:1], (n, NB))
            for q in range(k + 1, GROUP):
                cols[q] = cols[q] - mult * jnp.broadcast_to(mult[q : q + 1], (n, NB))
            u = jnp.broadcast_to(top[k : k + 1], (GROUP, NB)) * r
            top = jnp.where(row == k, u, jnp.where(row > k, top - mult[:GROUP] * u, top))
            if n > GROUP:
                below = below - mult[GROUP:] * jnp.broadcast_to(u[:1], (n - GROUP, NB))
        work[s : s + GROUP, :] = top
        if n > GROUP:
            work[s + GROUP :, :] = below


def kernel(
    grad_hbm, sketch, basis_out, proj_out,
    grad, packed, recv_b, recv_s, ypart, yall, rup, rdn, wpart, wsib, wrecv,
    ysib, gown, grecv, gzs, gzr, gza, gall, rhs, mat, work, inverses, solved, solved_w, outbox, inbox_x, inbox_z,
    local_sem, a2a_send, a2a_recv, s_send, s_recv, rs_send, rs_recv, ag_send, ag_recv,
    pair_send, pair_recv, w_send, w_recv, g_send, g_recv, gzs_send, gzs_recv, gza_send, gza_recv,
    gp_send, gp_recv, gs_send, gs_recv, x_send, x_recv, z_send, z_recv,
):
    dp = lax.axis_index("dp")
    t = lax.axis_index("tensor")
    z = dp // NX
    x = dp % NX
    m = x * NT + t
    chip = m // 2
    core = m % 2

    def member(i):
        return (z * NX + i // NT, i % NT)

    def at_z(i):
        return (i * NX + x, t)

    zup, zdn = at_z(mod(z + 1, NZ)), at_z(mod(z - 1, NZ))
    sibling = (dp, t + 1 - 2 * core)

    grad_in = pltpu.make_async_copy(grad_hbm, grad, local_sem.at[2])
    grad_in.start()

    barrier = pltpu.get_barrier_semaphore()

    @pl.loop(1, NM)
    def _(k):
        pl.semaphore_signal(barrier, inc=1, device_id=member((m + k) % NM), device_id_type=MESH)

    @pl.loop(1, NZ)
    def _(k):
        pl.semaphore_signal(barrier, inc=1, device_id=at_z((z + k) % NZ), device_id_type=MESH)

    mine = pl.ds(pl.multiple_of(m * WIDE, WIDE), WIDE)

    def pack(c):
        @pl.loop(0, NM // 8)
        def _(q):
            for place in range(4 * c, 4 * c + 4):
                first = ((z + ORDER[place] + NZ) % NZ) * (NM * BLK) + q * (8 * BLK)
                part = grad[:, pl.ds(pl.multiple_of(first, 128), 8 * BLK)]
                for i in range(8):
                    packed[q * 8 + i, :, place * BLK : (place + 1) * BLK] = part[:, i * BLK : (i + 1) * BLK]

    def b_copy(c, k):
        peer = (m + k) % NM
        lanes = pl.ds(PARTS[c], PARTS[c + 1] - PARTS[c])
        return pltpu.make_async_remote_copy(
            src_ref=packed.at[peer, :, lanes], dst_ref=recv_b.at[mine, lanes],
            send_sem=a2a_send.at[c], recv_sem=a2a_recv.at[c], device_id=member(peer), device_id_type=MESH,
        )

    halves = (pl.ds(0, HALF), pl.ds(HALF, HALF))

    def s_y(h, d):
        return pltpu.make_async_remote_copy(
            src_ref=sketch.at[z, :, :, halves[h]], dst_ref=recv_s.at[:, t, :, halves[h]],
            send_sem=s_send.at[h, d], recv_sem=s_recv.at[h, d],
            device_id=(dp, (t + 2 * d) % NT), device_id_type=MESH,
        )

    def s_sibling(h, d):
        piece = recv_s.at[:, mod(t - 2 * d, NT), :, halves[h]]
        return pltpu.make_async_remote_copy(
            src_ref=sketch.at[z, :, :, halves[h]] if d == 0 else piece, dst_ref=piece,
            send_sem=s_send.at[h, NT // 2 + d], recv_sem=s_recv.at[h, NT // 2 + d],
            device_id=sibling, device_id_type=MESH,
        )

    def s_forward(h):
        for d in range(1, NT // 2):
            s_y(h, d).wait_recv()
            s_sibling(h, d).start()

    own_s = pltpu.make_async_copy(sketch.at[z], recv_s.at[:, t], local_sem.at[0])
    own_s.start()

    def send(c):
        @pl.loop(1, NM)
        def _(k):
            b_copy(c, k).start()

    grad_in.wait()
    pack(0)
    pl.semaphore_wait(barrier, NM - 1 + NZ - 1)

    for h in range(2):
        for d in range(1, NT // 2):
            s_y(h, d).start()
        s_sibling(h, 0).start()
    send(0)
    pack(1)
    s_forward(0)
    send(1)
    s_forward(1)
    pack(2)
    pack(3)

    own_b = pltpu.make_async_copy(packed.at[m], recv_b.at[mine], local_sem.at[1])
    own_b.start()
    own_b.wait()
    own_s.wait()

    def rows_of(k):
        return pl.ds(near(k) * BLK, BLK)

    chains = ((0, 1, 0, 0), (1, -1, 1, 0), (2, 1, 1, 1), (3, -1, 0, 1))

    def rs_copy(chain, s, src):
        name, way, h, _ = chain
        buf = rup if way == 1 else rdn
        return pltpu.make_async_remote_copy(
            src_ref=src, dst_ref=buf.at[s, :, halves[h]],
            send_sem=rs_send.at[name, s], recv_sem=rs_recv.at[name, s],
            device_id=zup if way == 1 else zdn, device_id_type=MESH,
        )

    def rs_first(chain):
        _, way, h, s = chain
        rs_copy(chain, s, ypart.at[rows_of(way * (8 - s)), halves[h]]).start()

    def rs_step(s):
        for chain in chains:
            _, way, h, first = chain
            rows = rows_of(way * (8 - s))
            if s == first:
                rs_first(chain)
            elif s > first:
                buf = rup if way == 1 else rdn
                slot = buf.at[s - 1, :, halves[h]]
                rs_copy(chain, s - 1, slot).wait_recv()
                buf[s - 1, :, halves[h]] += ypart[rows, halves[h]]
                rs_copy(chain, s, slot).start()

    for c in range(len(STEPS)):
        lanes = pl.ds(PARTS[c], PARTS[c + 1] - PARTS[c])
        await_bytes(recv_b.at[pl.ds(0, (NM - 1) * WIDE), lanes], a2a_recv.at[c])
        if 0 < c < len(STEPS) - 1:
            send(c + 1)
        if c == 0:
            for h in range(2):
                for d in range(NT // 2):
                    s_sibling(h, d).wait_recv()
                ypart[lanes, halves[h]] = lax.dot_general(
                    recv_b[:, lanes], recv_s[:, :, :, halves[h]].reshape(PW, HALF), TDOT,
                    preferred_element_type=F32)
                rs_first(chains[h])
        else:
            ypart[lanes, :] = lax.dot_general(
                recv_b[:, lanes], recv_s[...].reshape(PW, RANK), TDOT, preferred_element_type=F32)
            for s in STEPS[c]:
                rs_step(s)

    own = rows_of(0)

    def ag_copy(chain, s):
        name, way, h, _ = chain
        return pltpu.make_async_remote_copy(
            src_ref=yall.at[rows_of(-way * s), halves[h]], dst_ref=yall.at[rows_of(-way * (s + 1)), halves[h]],
            send_sem=ag_send.at[name, s], recv_sem=ag_recv.at[name, s],
            device_id=zup if way == 1 else zdn, device_id_type=MESH,
        )

    def use(c):
        rows = pl.ds(USES[c], USES[c + 1] - USES[c])
        y = yall[rows, :]
        hi = y.astype(BF16)
        lo = (y - hi.astype(F32)).astype(BF16)
        b = recv_b[:, rows]
        w = jnp.dot(b, hi, preferred_element_type=F32) + jnp.dot(b, lo, preferred_element_type=F32)
        w = w.reshape(NCHIP, 2, WIDE, RANK)
        if c == 3:
            wpart[...] = w
        else:
            wpart[...] += w

    def to_sibling(src, dst, send_sem, recv_sem):
        return pltpu.make_async_remote_copy(
            src_ref=src, dst_ref=dst, send_sem=send_sem, recv_sem=recv_sem, device_id=sibling, device_id_type=MESH)

    g_pair = to_sibling(yall.at[own], ysib, pair_send.at[0], pair_recv.at[0])
    w_pair = to_sibling(wpart.at[:, 1 - core], wsib, pair_send.at[1], pair_recv.at[1])

    def plane_copy(k, src, dst, send_sem, recv_sem):
        return pltpu.make_async_remote_copy(
            src_ref=src, dst_ref=dst, send_sem=send_sem, recv_sem=recv_sem,
            device_id=member(((chip + k) % NCHIP) * 2 + core), device_id_type=MESH)

    def z_copy(k, src, dst, send_sem, recv_sem):
        return pltpu.make_async_remote_copy(
            src_ref=src, dst_ref=dst, send_sem=send_sem, recv_sem=recv_sem,
            device_id=at_z((z + k) % NZ), device_id_type=MESH)

    def gram_1():
        g_pair.start()
        rhs[pl.ds(0, BLK), :] = yall[own, :]
        rhs[pl.ds(BLK, WIDE), :] = jnp.zeros((WIDE, RANK), F32)

    def gram_2():
        g_pair.wait()
        y = jnp.concatenate([yall[own, :], ysib[...]], axis=0)

        def blocks(i, first, count):
            return lax.dot_general(
                y[:, i * NB : (i + 1) * NB], y[:, first * NB : (first + count) * NB], TDOT,
                precision=HIGHEST, preferred_element_type=F32).reshape(NCHIP, GR, count * NB)

        @pl.when(core == 0)
        def _():
            gown[:, :, : 4 * NB] = blocks(0, 0, 4)
            gown[:, :, 4 * NB :] = blocks(1, 1, 1)

        @pl.when(core == 1)
        def _():
            gown[:, :, : 2 * NB] = blocks(1, 2, 2)
            gown[:, :, 2 * NB : 4 * NB] = blocks(2, 2, 2)
            gown[:, :, 4 * NB :] = blocks(3, 3, 1)

        @pl.loop(1, NCHIP)
        def _(k):
            plane_copy(k, gown.at[(chip + k) % NCHIP], grecv.at[chip], g_send, g_recv).start()

        grecv[chip] = gown[chip]

    def left_early():
        for h in range(2):
            for d in range(NT // 2):
                s_sibling(h, d).wait_send()
            for d in range(1, NT // 2):
                s_y(h, d).wait_send()
        for c in range(len(STEPS)):
            await_bytes(recv_b.at[pl.ds(0, (NM - 1) * WIDE), pl.ds(PARTS[c], PARTS[c + 1] - PARTS[c])], a2a_send.at[c])
        for chain in chains:
            for s in range(chain[3], 8):
                rs_copy(chain, s, (rup if chain[1] == 1 else rdn).at[s, :, halves[chain[2]]]).wait_send()

    def left_late():
        for ref, sem in (
            (grecv.at[pl.ds(0, NCHIP - 1)], g_send), (wrecv.at[pl.ds(0, NCHIP - 1)], w_send),
        ):
            await_bytes(ref, sem)

        @pl.when(z < GR)
        def _():
            await_bytes(gza.at[pl.ds(0, GR - 1)], gzs_send)
            await_bytes(gzr.at[pl.ds(0, NZ - 1)], gza_send)

        @pl.when(z >= GR)
        def _():
            await_bytes(gza, gzs_send)

        @pl.loop(0, NCHIP)
        def _(k):
            gs_copy(k).wait_send()

        @pl.loop(1, NCHIP)
        def _(k):
            gp_copy(k).wait_send()

        for chain in chains:
            for s in range(0, 8 - chain[3]):
                ag_copy(chain, s).wait_send()

    def gram_3():
        await_bytes(grecv.at[pl.ds(0, NCHIP - 1)], g_recv)
        gzs[...] = jnp.sum(grecv[...], axis=0).reshape(GR, 1, GL)

        @pl.loop(1, NZ)
        def _(i):
            k = far_first(i)
            peer = (z + k) % NZ

            @pl.when(peer < GR)
            def _():
                z_copy(k, gzs.at[peer], gzr.at[z], gzs_send, gzs_recv).start()

        @pl.when(z < GR)
        def _():
            gzr[z] = gzs[z]

    def gram_4():
        @pl.when(z < GR)
        def _():
            await_bytes(gzr.at[pl.ds(0, NZ - 1)], gzs_recv)
            gza[z] = jnp.sum(gzr[...], axis=0)

            @pl.loop(1, NZ)
            def _(i):
                k = far_first(i)
                z_copy(k, gza.at[z], gza.at[z], gza_send, gza_recv).start()

    def gp_copy(k):
        piece = gall.at[core, chip]
        return plane_copy(k, piece, piece, gp_send.at[k], gp_recv.at[k])

    def gs_copy(k):
        piece = gall.at[core, mod(chip - k, NCHIP)]
        return to_sibling(piece, piece, gs_send.at[k], gs_recv.at[k])

    def gram_5():
        @pl.when(z < GR)
        def _():
            await_bytes(gza.at[pl.ds(0, GR - 1)], gza_recv)

        @pl.when(z >= GR)
        def _():
            await_bytes(gza, gza_recv)

        gall[core, chip] = gza[...].reshape(GR, GL)

        @pl.loop(1, NCHIP)
        def _(k):
            gp_copy(k).start()

        gs_copy(0).start()

    def gram_6():
        @pl.loop(1, NCHIP)
        def _(k):
            piece = gall.at[core, mod(chip - k, NCHIP)]
            plane_copy(k, piece, piece, gp_send.at[k], gp_recv.at[k]).wait_recv()
            gs_copy(k).start()

    def gram_7():
        @pl.loop(0, NCHIP)
        def _(k):
            piece = gall.at[1 - core, mod(chip - k, NCHIP)]
            to_sibling(piece, piece, gs_send.at[k], gs_recv.at[k]).wait_recv()

    def gather_step(s, which):
        for chain in which:
            if s < 8 - chain[3]:
                if s:
                    ag_copy(chain, s - 1).wait_recv()
                ag_copy(chain, s).start()

    def gather_end():
        for chain in chains:
            ag_copy(chain, 7 - chain[3]).wait_recv()

    for h in range(2):
        ends = [chain for chain in chains if chain[2] == h]
        for chain in ends:
            rs_copy(chain, 7, (rup if chain[1] == 1 else rdn).at[7, :, halves[h]]).wait_recv()
        yall[own, halves[h]] = ypart[own, halves[h]] + rup[7, :, halves[h]] + rdn[7, :, halves[h]]
        gather_step(0, ends)
    gram_1()
    one, two = chains[:2], chains[2:]
    gram_2()
    gather_step(1, chains)
    left_early()
    gather_step(2, chains)
    gram_3()
    gather_step(3, chains)
    gram_4()
    gather_step(4, one)
    use(3)
    gather_step(4, two)
    gram_5()
    use(2)
    gather_step(5, chains)
    gram_6()
    gather_step(6, one)
    gram_7()
    gather_step(6, two)
    use(1)

    def w_send_off():
        w_pair.wait()
        wsib[...] += wpart[:, core]

        @pl.loop(1, NCHIP)
        def _(k):
            plane_copy(k, wsib.at[(chip + k) % NCHIP], wrecv.at[chip], w_send, w_recv).start()

        wrecv[chip] = wsib[chip]

    def below(i):
        return pl.ds(i * NB, NB)

    def w_solve():
        await_bytes(wrecv.at[pl.ds(0, NCHIP - 1)], w_recv)
        w = jnp.sum(wrecv[...], axis=0)
        parts = []
        for j in range(RANK // NB):
            part = lax.dot_general(
                w[:, :NB], inverses[j], (((1,), (1,)), ((), ())), precision=HIGHEST, preferred_element_type=F32)
            parts.append(part)
            if j + 1 < RANK // NB:
                w = w[:, NB:] - jnp.dot(
                    part, mat[below(j), (j + 1) * NB : RANK], precision=HIGHEST, preferred_element_type=F32)
        rhs[pl.ds(BLK, WIDE), :] = jnp.concatenate(parts, axis=1)
        solved_w[...] = rhs[...].T

    def at(j, now, work_beside):
        @pl.when(j == now)
        def _():
            work_beside()

    upper_blocks = [gall[i].reshape(NB, GL) for i in range(2)]
    mat[:, :RANK] = jnp.zeros((RANK, RANK), F32)
    mat[below(0), :RANK] = upper_blocks[0][:, :RANK]
    mat[below(1), NB : 2 * NB] = upper_blocks[0][:, RANK:]
    mat[below(1), 2 * NB : RANK] = upper_blocks[1][:, : 2 * NB]
    mat[below(2), 2 * NB : RANK] = upper_blocks[1][:, 2 * NB : 4 * NB]
    mat[below(3), 3 * NB : RANK] = upper_blocks[1][:, 4 * NB :]
    mat[:, RANK:] = rhs[...].T

    @pl.loop(0, RANK // NB)
    def _(j):
        rows = pl.ds(pl.multiple_of(j * NB, NB), NB)
        work[...] = mat[rows, rows]
        at(j, 1, lambda: gather_step(7, chains))

        def last_of_w():
            gather_end()
            use(0)
            w_pair.start()

        at(j, 2, w_send_off)

        def halfway():
            at(j, 1, last_of_w)

        invert_factor(work, halfway)

        row = lax.broadcasted_iota(jnp.int32, (NB, NB), 0)
        lane = lax.broadcasted_iota(jnp.int32, (NB, NB), 1)
        inverse = jnp.where(lane <= row, work[...], 0.0)
        inverses[j] = inverse
        upper = jnp.dot(inverse, mat[rows, :], precision=HIGHEST, preferred_element_type=F32)
        mat[rows, :] = upper
        solved[rows, :] = upper[:, RANK:]
        for i in range(1, RANK // NB):
            @pl.when(i > j)
            def _():
                mat[below(i), :] -= lax.dot_general(
                    upper[:, i * NB : (i + 1) * NB], upper, TDOT, precision=HIGHEST, preferred_element_type=F32)

    basis_out[...] = (solved[...].T[:BLK] * math.sqrt(ROWS)).astype(BF16)
    left_late()
    w_solve()

    packed_p = jnp.zeros((N_DP, NB), F32)
    lane = lax.broadcasted_iota(jnp.int32, (N_DP, NB), 1)
    for r in range(PER_DP):
        part = solved_w[pl.ds(r, N_DP, stride=PER_DP), :]
        slot = PER_DP - 1 - r
        packed_p = jnp.where(lane // WIDE == slot, pltpu.roll(part, (WIDE * slot - BLK) % NB, 1), packed_p)
    outbox[...] = packed_p.reshape(NZ, NX, 1, NB)

    def x_copy(k):
        peer = (x + k) % NX
        return pltpu.make_async_remote_copy(
            src_ref=outbox.at[:, peer], dst_ref=inbox_x.at[x], send_sem=x_send.at[k], recv_sem=x_recv.at[k],
            device_id=(z * NX + peer, t), device_id_type=MESH,
        )

    for k in range(1, NX):
        x_copy(k).start()
    inbox_x[x] = outbox[:, x]
    for k in range(1, NX):
        x_copy(k).wait()

    @pl.loop(1, NZ)
    def _(i):
        k = far_first(i)
        z_copy(k, inbox_x.at[:, (z + k) % NZ], inbox_z.at[z], z_send, z_recv).start()

    inbox_z[z] = inbox_x[:, z]

    await_bytes(inbox_z.at[pl.ds(0, NZ - 1)], z_send)
    await_bytes(inbox_z.at[pl.ds(0, NZ - 1)], z_recv)
    per_tile = NB // WIDE
    lane = lax.broadcasted_iota(jnp.int32, (PER_DP, NB), 1)
    for q in range(N_DP // per_tile):
        tile = jnp.zeros((PER_DP, NB), F32)
        for i in range(per_tile):
            src = q * per_tile + i
            line = jnp.broadcast_to(inbox_z[src // NX, src % NX], (PER_DP, NB))
            line = pltpu.roll(line, 0, 1, stride=WIDE, stride_axis=0)
            line = pltpu.roll(line, (WIDE * (i + 1)) % NB, 1)
            tile = jnp.where(lane // WIDE == i, line, tile)
        proj_out[:, q * NB : (q + 1) * NB] = tile.astype(BF16)


def project(grad_buckets, sketch):
    vmem = pl.BlockSpec(memory_space=pltpu.VMEM)
    dma = pltpu.SemaphoreType.DMA
    return pl.pallas_call(
        kernel,
        out_shape=(
            jax.ShapeDtypeStruct((BLK, RANK), BF16),
            jax.ShapeDtypeStruct((PER_DP, N_DP * WIDE), BF16),
        ),
        in_specs=[pl.BlockSpec(memory_space=pl.ANY)] * 2,
        out_specs=(vmem, vmem),
        scratch_shapes=[
            pltpu.VMEM((WIDE, ROWS), BF16),
            pltpu.VMEM((NM, WIDE, COLS), BF16),
            pltpu.VMEM((PW, COLS), BF16),
            pltpu.VMEM((NX, NT, WIDE, RANK), BF16),
            pltpu.VMEM((COLS, RANK), F32),
            pltpu.VMEM((COLS, RANK), F32),
            pltpu.VMEM((8, BLK, RANK), F32),
            pltpu.VMEM((8, BLK, RANK), F32),
            pltpu.VMEM((NCHIP, 2, WIDE, RANK), F32),
            pltpu.VMEM((NCHIP, WIDE, RANK), F32),
            pltpu.VMEM((NCHIP, WIDE, RANK), F32),
            pltpu.VMEM((BLK, RANK), F32),
            pltpu.VMEM((NCHIP, GR, GL), F32),
            pltpu.VMEM((NCHIP, GR, GL), F32),
            pltpu.VMEM((GR, 1, GL), F32),
            pltpu.VMEM((NZ, 1, GL), F32),
            pltpu.VMEM((GR, 1, GL), F32),
            pltpu.VMEM((2, NCHIP, GR, GL), F32),
            pltpu.VMEM((BLK + WIDE, RANK), F32),
            pltpu.VMEM((RANK, RANK + NB), F32),
            pltpu.VMEM((NB, NB), F32),
            pltpu.VMEM((RANK // NB, NB, NB), F32),
            pltpu.VMEM((RANK, NB), F32),
            pltpu.VMEM((RANK, NB), F32),
            pltpu.VMEM((NZ, NX, 1, NB), F32),
            pltpu.VMEM((NX, NZ, 1, NB), F32),
            pltpu.VMEM((NZ, NX, 1, NB), F32),
            dma((3,)),
            dma((len(STEPS),)), dma((len(STEPS),)),
            dma((2, NT)), dma((2, NT)),
            dma((4, 8)), dma((4, 8)),
            dma((4, 8)), dma((4, 8)),
            dma((2,)), dma((2,)),
            dma, dma, dma, dma, dma, dma, dma, dma,
            dma((NCHIP,)), dma((NCHIP,)),
            dma((NCHIP,)), dma((NCHIP,)),
            dma((NX,)), dma((NX,)),
            dma, dma,
        ],
        compiler_params=pltpu.CompilerParams(
            collective_id=0, has_side_effects=True, vmem_limit_bytes=56 * 1024 * 1024),
    )(grad_buckets, sketch)


def shards(grad_buckets, sketch):
    basis, projected = project(grad_buckets, sketch.reshape(NZ, NX, WIDE, RANK))
    return basis.T, projected


def solution(mesh):
    in_specs = (P(("tensor", "dp"), None), P("tensor", None))
    out_specs = (P(None, ("dp", "tensor")), P("dp", "tensor"))
    return jax.shard_map(shards, mesh=mesh, in_specs=in_specs, out_specs=out_specs, check_vma=False)
```
